512 devices in a mesh: row: 8 (over y), col: 2 (over z_hi), ctx: 32 (over x, z_lo, core).
Axes of the slice: x: 4, y: 8, z: 8 (z_hi: 2, z_lo: 4; z = z_hi * 4 + z_lo), core: 2. Of those that a mesh axis runs over, the one named last changes fastest.
Arguments:
- featured: bfloat16 [16384, 3, 4096], P('ctx', None, ('row', 'col')), may hold values from -6 to 6
- feat_taps: float32 [3, 7, 4096], P(None, None, ('row', 'col')), may hold values from -2.5 to 2.5
- inner_taps: float32 [7, 4096], P(None, ('row', 'col')), may hold values from -2.5 to 2.5
- out_weight: bfloat16 [4096, 4096], P('row', 'col'), may hold values from -0.09375 to 0.09375
- out_grad: bfloat16 [16384, 4096], P('ctx', ('col', 'row')), may hold values from -6 to 6
Outputs:
- grad_features: bfloat16 [16384, 3, 4096], P('ctx', None, ('row', 'col'))
- grad_weight: bfloat16 [4096, 4096], P(('row', 'ctx'), 'col')
- grad_feat_taps: float32 [3, 7, 4096], P(None, None, ('row', 'col'))
- grad_inner_taps: float32 [7, 4096], P(None, ('row', 'col'))
The draws below stay inside these ranges and needn't reach their ends.
All inputs are finite; a program needn't handle non-finite values.
Results may differ from the reference program's by a relative error of at most 0.0049.
Values may be sent and summed in bfloat16 or wider, within the bound.
No kernel may reach another device: no remote copies, remote signals or barrier semaphores. Data moves between devices by JAX's collectives and lax.ppermute only.
A program may use at most 64 MiB of HBM per device.

```python
import math
import jax
import jax.numpy as jnp
from jax import lax

C = 4096
DO = 4096
TAPS = 7
LENGTH = 16384


def levels(rng, extent, cuts, low, top_value):
    gain = 1.0
    for axis_at, parts in cuts:
        heights = jax.random.uniform(jax.random.fold_in(jax.random.fold_in(rng, 6), axis_at), (parts,), jnp.float32, low / len(cuts), top_value / len(cuts))
        gain = gain * jnp.repeat(jnp.exp(heights), extent[axis_at] // parts).reshape((-1,) + (1,) * (len(extent) - 1 - axis_at))
    return gain


def normal_values(stream_key, shape, scale, limit, cuts=(), dtype=jnp.bfloat16):
    drawn = jax.random.normal(stream_key, shape, jnp.float32) * scale
    if len(cuts) > 0:
        drawn = levels(stream_key, shape, cuts, -0.22, 0.18) * drawn
    return jnp.clip(drawn, min=-limit, max=limit).astype(dtype)


def setup_inputs(seed: int = 0) -> dict:
    streams_of = jax.random.split(jax.random.key(seed), 6)
    return {
        "featured": normal_values(streams_of[0], (LENGTH, 3, C), 1.0, 6.0, ((0, 32), (2, 16))),
        "feat_taps": normal_values(streams_of[1], (3, TAPS, C), 0.4, 2.5, ((2, 16),), jnp.float32),
        "inner_taps": normal_values(streams_of[2], (TAPS, C), 0.4, 2.5, ((1, 16),), jnp.float32),
        "out_weight": normal_values(streams_of[3], (C, DO), C ** -0.5, 0.09375, ((0, 8), (1, 2))),
        "out_grad": normal_values(streams_of[4], (LENGTH, DO), 1.0, 6.0, ((0, 32), (1, 16))),
    }


def causal_conv(source, taps):
    width = taps.shape[0]
    total_rows = source.shape[0]
    padded = jnp.pad(source, ((width - 1, 0), (0, 0)))
    result = jnp.zeros_like(source)
    for tap_index in range(width):
        result = result + taps[tap_index] * padded[width - 1 - tap_index:width - 1 - tap_index + total_rows]
    return result

def anticausal_conv(source, taps):
    width = taps.shape[0]
    total_rows = source.shape[0]
    padded = jnp.pad(source, ((0, width - 1), (0, 0)))
    result = jnp.zeros_like(source)
    for tap_index in range(width):
        result = result + taps[tap_index] * padded[tap_index:tap_index + total_rows]
    return result

def lagged_sums(grad_part, source, width):
    total_rows = source.shape[0]
    padded = jnp.pad(source, ((width - 1, 0), (0, 0)))
    pieces = []
    for tap_index in range(width):
        pieces.append(lax.optimization_barrier(jnp.sum(grad_part * padded[width - 1 - tap_index:width - 1 - tap_index + total_rows], axis=0)))
    return jnp.stack(pieces, axis=0)

def reference(featured, feat_taps, inner_taps, out_weight, out_grad):
    inv_root = 1.0 / math.sqrt(LENGTH)
    source_list = [featured[:, j, :].astype(jnp.float32) for j in range(3)]
    mixed = [causal_conv(source_list[j], feat_taps[j]) for j in range(3)]
    query, key_part, value = mixed
    product = key_part * value
    window = causal_conv(product, inner_taps)
    gated = (query * window).astype(jnp.bfloat16)
    grad_gated = lax.dot_general(out_grad, out_weight, (((1,), (1,)), ((), ())), preferred_element_type=jnp.float32)
    weight_sum = lax.dot_general(gated, out_grad, (((0,), (0,)), ((), ())), preferred_element_type=jnp.float32) * inv_root
    grad_weight = weight_sum.astype(jnp.bfloat16)
    grad_query = grad_gated * window
    grad_window = grad_gated * query
    grad_product = anticausal_conv(grad_window, inner_taps)
    grad_key = grad_product * value
    grad_value = grad_product * key_part
    grad_mixed = [grad_query, grad_key, grad_value]
    grad_features = jnp.stack([anticausal_conv(grad_mixed[j], feat_taps[j]) for j in range(3)], axis=1).astype(jnp.bfloat16)
    grad_inner_taps = lagged_sums(grad_window, product, TAPS) * inv_root
    grad_feat_taps = jnp.stack([lagged_sums(grad_mixed[j], source_list[j], TAPS) for j in range(3)], axis=0) * inv_root
    return (grad_features, grad_weight, grad_feat_taps, grad_inner_taps)
```

```python
import math

import jax
import jax.numpy as jnp
from jax import lax
from jax.experimental import pallas as pl
from jax.experimental.pallas import tpu as pltpu
from jax.sharding import Mesh
from jax.sharding import PartitionSpec as P

TAPS = 7
REACH = TAPS - 1
HALO = 16
LEAD = 8
CHUNK = 64
LANES = 128
CTX = ("x", "zl", "core")
F32 = jnp.float32
BF16 = jnp.bfloat16


def chunks(total):
    return [(start, min(CHUNK, total - start)) for start in range(0, total, CHUNK)]


def load_features(before, own, scratch, after=None):
    rows = own.shape[1]
    for j in range(3):
        scratch[j, 0:HALO, :] = before[j].astype(F32)
        for start, count in chunks(rows):
            scratch[j, HALO + start : HALO + start + count, :] = own[
                j, start : start + count, :
            ].astype(F32)
        if after is not None:
            scratch[j, HALO + rows : 2 * HALO + rows, :] = after[j].astype(F32)


def forward_kernel(
    before, own, after, feat_taps, inner_taps, gated, query, window, key, value, product, feats
):
    rows = own.shape[1]
    load_features(before, own, feats, after)
    for start, count in chunks(rows + HALO + LEAD):
        parts = []
        for j in range(3):
            base = HALO - LEAD + start
            total = feat_taps[j, 0:1, :] * feats[j, base : base + count, :]
            for s in range(1, TAPS):
                total = total + feat_taps[j, s : s + 1, :] * feats[j, base - s : base - s + count, :]
            parts.append(total)
        query[start : start + count, :] = parts[0]
        key[start : start + count, :] = parts[1]
        value[start : start + count, :] = parts[2]
        product[start : start + count, :] = parts[1] * parts[2]
    for start, count in chunks(rows + HALO):
        base = LEAD + start
        total = inner_taps[0:1, :] * product[base : base + count, :]
        for s in range(1, TAPS):
            total = total + inner_taps[s : s + 1, :] * product[base - s : base - s + count, :]
        window[start : start + count, :] = total
        if start < rows:
            kept = min(count, rows - start)
            gated[start : start + kept, :] = (
                query[base : base + kept, :] * total[:kept]
            ).astype(BF16)


def backward_kernel(
    near, far, query, window, key, value, product, before, own, feat_taps, inner_taps,
    grads, tap_sums, feats, grad_window, grad_mixed,
):
    rows = own.shape[1]
    load_features(before, own, feats)
    for start, count in chunks(rows + HALO):
        total = near[start : start + count, :] + far[start : start + count, :].astype(F32)
        grad_window[start : start + count, :] = (
            total * query[LEAD + start : LEAD + start + count, :]
        )
        grad_mixed[0, start : start + count, :] = total * window[start : start + count, :]
    for start, count in chunks(rows + LEAD):
        total = inner_taps[0:1, :] * grad_window[start : start + count, :]
        for s in range(1, TAPS):
            total = total + inner_taps[s : s + 1, :] * grad_window[start + s : start + s + count, :]
        grad_mixed[1, start : start + count, :] = (
            total * value[LEAD + start : LEAD + start + count, :]
        )
        grad_mixed[2, start : start + count, :] = total * key[LEAD + start : LEAD + start + count, :]

    def folded(value):
        return jnp.sum(value.reshape(value.shape[0] // 8, 8, value.shape[1]), axis=0)

    def put(at, sums):
        for s in range(TAPS):
            tap_sums[at, s : s + 1, :] = jnp.sum(sums[s], axis=0, keepdims=True)
        tap_sums[at, TAPS : TAPS + 1, :] = jnp.zeros((1, LANES), F32)

    for j in range(3):
        sums = [jnp.zeros((8, LANES), F32) for _ in range(TAPS)]
        for start, count in chunks(rows):
            here = grad_mixed[j, start : start + count, :]
            total = feat_taps[j, 0:1, :] * here
            for s in range(1, TAPS):
                total = (
                    total
                    + feat_taps[j, s : s + 1, :] * grad_mixed[j, start + s : start + s + count, :]
                )
            grads[j, start : start + count, :] = total.astype(BF16)
            for s in range(TAPS):
                base = HALO + start - s
                sums[s] = sums[s] + folded(here * feats[j, base : base + count, :])
        put(j, sums)
    sums = [jnp.zeros((8, LANES), F32) for _ in range(TAPS)]
    for start, count in chunks(rows):
        here = grad_window[start : start + count, :]
        for s in range(TAPS):
            base = LEAD + start - s
            sums[s] = sums[s] + folded(here * product[base : base + count, :])
    put(3, sums)


def lane_spec(*lead):
    return pl.BlockSpec((*lead, LANES), lambda i: (0,) * len(lead) + (i,))


def forward(before, own, after, feat_taps, inner_taps):
    _, rows, channels = own.shape
    saved = jax.ShapeDtypeStruct((rows + HALO + LEAD, channels), F32)
    saved_spec = lane_spec(rows + HALO + LEAD)
    return pl.pallas_call(
        forward_kernel,
        grid=(channels // LANES,),
        in_specs=[
            lane_spec(3, HALO), lane_spec(3, rows), lane_spec(3, HALO),
            lane_spec(3, TAPS), lane_spec(TAPS),
        ],
        out_specs=[
            lane_spec(rows), saved_spec, lane_spec(rows + HALO),
            saved_spec, saved_spec, saved_spec,
        ],
        out_shape=[
            jax.ShapeDtypeStruct((rows, channels), BF16),
            saved,
            jax.ShapeDtypeStruct((rows + HALO, channels), F32),
            saved, saved, saved,
        ],
        scratch_shapes=[pltpu.VMEM((3, rows + 2 * HALO, LANES), F32)],
        compiler_params=pltpu.CompilerParams(vmem_limit_bytes=32 << 20),
        cost_estimate=pl.CostEstimate(
            flops=60 * rows * channels, bytes_accessed=30 * rows * channels, transcendentals=0
        ),
        name="forward",
    )(before, own, after, feat_taps, inner_taps)


def backward(near, far, saved, before, own, feat_taps, inner_taps):
    _, rows, channels = own.shape
    saved_spec = lane_spec(rows + HALO + LEAD)
    long_spec = lane_spec(rows + HALO)
    return pl.pallas_call(
        backward_kernel,
        grid=(channels // LANES,),
        in_specs=[
            long_spec, long_spec, saved_spec, long_spec, saved_spec, saved_spec, saved_spec,
            lane_spec(3, HALO), lane_spec(3, rows), lane_spec(3, TAPS), lane_spec(TAPS),
        ],
        out_specs=[lane_spec(3, rows), lane_spec(4, 8)],
        out_shape=[
            jax.ShapeDtypeStruct((3, rows, channels), BF16),
            jax.ShapeDtypeStruct((4, 8, channels), F32),
        ],
        scratch_shapes=[
            pltpu.VMEM((3, rows + HALO, LANES), F32),
            pltpu.VMEM((rows + HALO, LANES), F32),
            pltpu.VMEM((3, rows + HALO, LANES), F32),
        ],
        compiler_params=pltpu.CompilerParams(vmem_limit_bytes=32 << 20),
        cost_estimate=pl.CostEstimate(
            flops=120 * rows * channels, bytes_accessed=40 * rows * channels, transcendentals=0
        ),
        name="backward",
    )(near, far, *saved, before, own, feat_taps, inner_taps)


def gated_grad_kernel(grad, weight, far, near, total):
    at = pl.program_id(0)
    term = lax.dot_general(
        grad[0], weight[...], (((1,), (1,)), ((), ())), preferred_element_type=F32
    )

    @pl.when(at == 0)
    def _():
        total[...] = term

    @pl.when(at > 0)
    def _():
        total[...] += term

    @pl.when(at == pl.num_programs(0) - 1)
    def _():
        half = far.shape[1]
        far[...] = total[:, :half].astype(BF16)
        near[...] = total[:, half:]


def gated_grad(grads, weight):
    blocks, rows, width = grads.shape
    channels = weight.shape[0]
    half = channels // 2
    return pl.pallas_call(
        gated_grad_kernel,
        grid=(blocks,),
        in_specs=[
            pl.BlockSpec((1, rows, width), lambda i: (i, 0, 0)),
            pl.BlockSpec((channels, width), lambda i: (0, i)),
        ],
        out_specs=[
            pl.BlockSpec((rows, half), lambda i: (0, 0)),
            pl.BlockSpec((rows, half), lambda i: (0, 0)),
        ],
        out_shape=[
            jax.ShapeDtypeStruct((rows, half), BF16),
            jax.ShapeDtypeStruct((rows, half), F32),
        ],
        scratch_shapes=[pltpu.VMEM((rows, channels), F32)],
        compiler_params=pltpu.CompilerParams(vmem_limit_bytes=32 << 20),
        cost_estimate=pl.CostEstimate(
            flops=2 * rows * channels * blocks * width,
            bytes_accessed=2 * blocks * width * (rows + channels) + 6 * rows * half,
            transcendentals=0,
        ),
        name="gated_grad",
    )(grads, weight)


def weight_grad_kernel(gated, grad, out):
    rows = gated.shape[1]
    out[0] = jnp.dot(gated[...], grad[0, :rows, :], preferred_element_type=F32).astype(out.dtype)


def weight_grad(gated, grads, dtype):
    channels, rows = gated.shape
    blocks, _, width = grads.shape
    return pl.pallas_call(
        weight_grad_kernel,
        grid=(blocks,),
        in_specs=[
            pl.BlockSpec((channels, rows), lambda i: (0, 0)),
            pl.BlockSpec((1, grads.shape[1], width), lambda i: (i, 0, 0)),
        ],
        out_specs=pl.BlockSpec((1, channels, width), lambda i: (i, 0, 0)),
        out_shape=jax.ShapeDtypeStruct((blocks, channels, width), dtype),
        compiler_params=pltpu.CompilerParams(vmem_limit_bytes=32 << 20),
        cost_estimate=pl.CostEstimate(
            flops=2 * rows * channels * blocks * width,
            bytes_accessed=2 * blocks * width * (rows + 2 * channels) + 2 * rows * channels,
            transcendentals=0,
        ),
        name="weight_grad",
    )(gated, grads)


def ctx_permute(value, target):
    nx, nz, nc = (lax.axis_size(a) for a in CTX)
    pairs = []
    for x in range(nx):
        for z in range(nz):
            for c in range(nc):
                to = target(x, z, c)
                if to is not None:
                    pairs.append(((x * nz + z) * nc + c, (to[0] * nz + to[1]) * nc + to[2]))
    return lax.ppermute(value, CTX, pairs)


def ctx_shift(value, steps):
    nx, nz, nc = (lax.axis_size(a) for a in CTX)
    count = nx * nz * nc
    return lax.ppermute(
        value, CTX, [(i, i + steps) for i in range(count) if 0 <= i + steps < count]
    )


def scatter_sum(kept, axis, dim, wire):
    count = lax.axis_size(axis)
    me = lax.axis_index(axis)
    size = kept.shape[dim] // count
    total = None
    arrived = []
    for step in range(1, count):
        to = lax.rem(me + step, count)
        piece = lax.dynamic_slice_in_dim(wire, to * size, size, dim)
        arrived.append(
            lax.ppermute(piece, axis, [(i, (i + step) % count) for i in range(count)])
        )
    total = lax.dynamic_slice_in_dim(kept, me * size, size, dim)
    for piece in arrived:
        total = total + piece.astype(F32)
    return total


def body(featured, feat_taps, inner_taps, out_weight, out_grad):
    rows = featured.shape[0]
    nx, nz, nc = (lax.axis_size(a) for a in CTX)
    inv_root = 1.0 / math.sqrt(rows * nx * nz * nc)
    col = lax.axis_index("col")
    core = lax.axis_index("core")

    grad_after = ctx_shift(out_grad[:HALO], -1)
    own = jnp.transpose(featured, (1, 0, 2))
    before = ctx_shift(own[:, rows - HALO :], 1)
    after = ctx_shift(own[:, :HALO], -1)
    grads = lax.all_gather(jnp.concatenate([out_grad, grad_after], axis=0), "row", axis=0)

    gated, *saved = forward(before, own, after, feat_taps, inner_taps)
    both = lax.all_gather(gated, "col", axis=1, tiled=True)
    channels = both.shape[1]
    slots = channels // (nx * nz * nc)
    split = both.T.reshape(nx * nz, nc, slots, rows)
    keep_gated = lax.dynamic_index_in_dim(split, core, 1, keepdims=False)
    send_gated = lax.dynamic_index_in_dim(split, 1 - core, 1, keepdims=False)
    keep_gated = keep_gated.reshape(channels // nc, rows)
    send_gated = send_gated.reshape(channels // nc, rows)
    half = channels // 2
    weight = jnp.concatenate(
        [
            lax.dynamic_slice_in_dim(out_weight, (1 - col) * half, half, 0),
            lax.dynamic_slice_in_dim(out_weight, col * half, half, 0),
        ],
        axis=0,
    )

    far, near = gated_grad(grads, weight)
    far = lax.ppermute(far, "col", [(0, 1), (1, 0)])

    sent = ctx_permute(
        weight_grad(send_gated, grads, BF16), lambda x, z, c: (x, z, 1 - c)
    )
    pair = weight_grad(keep_gated, grads, F32) + sent.astype(F32)
    along_x = scatter_sum(pair, "x", 1, pair.astype(BF16))
    along_z = scatter_sum(along_x, "zl", 1, along_x.astype(BF16))
    grad_weight = (along_z * inv_root).astype(BF16)
    grad_weight = jnp.transpose(grad_weight, (1, 0, 2)).reshape(slots, -1)

    grad_own, taps = backward(near, far, saved, before, own, feat_taps, inner_taps)
    for target in (
        lambda x, z, c: (x, z, c ^ 1),
        lambda x, z, c: (x ^ 1, z, c),
        lambda x, z, c: (nx - 1 - x, z, c),
        lambda x, z, c: (x, z ^ 1, c),
        lambda x, z, c: (x, z ^ 2, c),
    ):
        taps = taps + ctx_permute(taps, target)
    taps = taps * inv_root
    return (
        jnp.transpose(grad_own, (1, 0, 2)),
        grad_weight,
        taps[:3, :TAPS],
        taps[3, :TAPS],
    )


def fine_mesh(mesh):
    row, col, ctx = mesh.devices.shape
    depth = ctx // 8
    return Mesh(
        mesh.devices.reshape(row, col, ctx // (2 * depth), depth, 2), ("row", "col", *CTX)
    )


def solution(mesh):
    return jax.shard_map(
        body,
        mesh=fine_mesh(mesh),
        in_specs=(
            P(CTX, None, ("row", "col")),
            P(None, None, ("row", "col")),
            P(None, ("row", "col")),
            P("row", "col"),
            P(CTX, ("col", "row")),
        ),
        out_specs=(
            P(CTX, None, ("row", "col")),
            P(("row", *CTX), "col"),
            P(None, None, ("row", "col")),
            P(None, ("row", "col")),
        ),
        check_vma=False,
    )
```

```python
import math

import jax
import jax.numpy as jnp
from jax import lax
from jax.experimental import pallas as pl
from jax.experimental.pallas import tpu as pltpu
from jax.sharding import Mesh
from jax.sharding import PartitionSpec as P

TAPS = 7
HALO = 16
LEAD = 8
CHUNK = 64
LANES = 128
CTX = ("x", "zl", "core")
F32 = jnp.float32
BF16 = jnp.bfloat16
VMEM_BYTES = 56 << 20


def spread(total):
    return [(start, min(CHUNK, total - start)) for start in range(0, total, CHUNK)]


def lane_spec(*lead):
    return pl.BlockSpec((*lead, LANES), lambda i: (0,) * len(lead) + (i,))


def whole(shape):
    return pl.BlockSpec(shape, lambda *_: (0,) * len(shape))


SCALAR = pl.BlockSpec(memory_space=pltpu.SMEM)
UNREAD = pl.BlockSpec(memory_space=pl.ANY)


def call(kernel, name, flops, moved, **kwargs):
    return pl.pallas_call(
        kernel,
        name=name,
        compiler_params=pltpu.CompilerParams(vmem_limit_bytes=VMEM_BYTES),
        cost_estimate=pl.CostEstimate(flops=flops, bytes_accessed=moved, transcendentals=0),
        **kwargs,
    )


def load_features(before, own, feats):
    rows = own.shape[1]
    for j in range(3):
        feats[j, 0:HALO, :] = before[j].astype(F32)
        for start, count in spread(rows):
            feats[j, HALO + start : HALO + start + count, :] = own[
                j, start : start + count, :
            ].astype(F32)


def forward_kernel(
    before, own, feat_taps, inner_taps, gated, query, window, key, value, product, feats
):
    rows = own.shape[1]
    load_features(before, own, feats)
    for start, count in spread(rows + LEAD):
        base = HALO - LEAD + start
        parts = []
        for j in range(3):
            total = feat_taps[j, 0:1, :] * feats[j, base : base + count, :]
            for s in range(1, TAPS):
                total = total + feat_taps[j, s : s + 1, :] * feats[j, base - s : base - s + count, :]
            parts.append(total)
        query[start : start + count, :] = parts[0]
        key[start : start + count, :] = parts[1]
        value[start : start + count, :] = parts[2]
        product[start : start + count, :] = parts[1] * parts[2]
    for start, count in spread(rows):
        base = LEAD + start
        total = inner_taps[0:1, :] * product[base : base + count, :]
        for s in range(1, TAPS):
            total = total + inner_taps[s : s + 1, :] * product[base - s : base - s + count, :]
        window[start : start + count, :] = total
        gated[start : start + count, :] = (query[base : base + count, :] * total).astype(BF16)


def forward(before, own, feat_taps, inner_taps):
    _, rows, channels = own.shape
    saved = jax.ShapeDtypeStruct((rows + LEAD, channels), F32)
    saved_spec = lane_spec(rows + LEAD)
    return call(
        forward_kernel,
        "forward",
        60 * rows * channels,
        30 * rows * channels,
        grid=(channels // LANES,),
        in_specs=[lane_spec(3, HALO), lane_spec(3, rows), lane_spec(3, TAPS), lane_spec(TAPS)],
        out_specs=[lane_spec(rows), saved_spec, lane_spec(rows), saved_spec, saved_spec, saved_spec],
        out_shape=[
            jax.ShapeDtypeStruct((rows, channels), BF16),
            saved,
            jax.ShapeDtypeStruct((rows, channels), F32),
            saved,
            saved,
            saved,
        ],
        scratch_shapes=[pltpu.VMEM((3, rows + HALO, LANES), F32)],
    )(before, own, feat_taps, inner_taps)


def backward_kernel(
    near, far, query, window, key, value, product, before, own, feat_taps, inner_taps, _,
    grads, head, tail, tap_sums, feats, grad_window, grad_mixed,
):
    rows = own.shape[1]
    load_features(before, own, feats)
    zeros = jnp.zeros((HALO, LANES), F32)
    grad_window[0:HALO, :] = zeros
    grad_window[HALO + rows :, :] = zeros[:LEAD]
    for j in range(3):
        grad_mixed[j, 0:HALO, :] = zeros
        grad_mixed[j, HALO + rows :, :] = zeros[:LEAD]
    for start, count in spread(rows):
        at = HALO + start
        total = near[start : start + count, :] + far[start : start + count, :].astype(F32)
        grad_window[at : at + count, :] = total * query[LEAD + start : LEAD + start + count, :]
        grad_mixed[0, at : at + count, :] = total * window[start : start + count, :]
    for start, count in spread(rows + LEAD):
        at = HALO - LEAD + start
        total = inner_taps[0:1, :] * grad_window[at : at + count, :]
        for s in range(1, TAPS):
            total = total + inner_taps[s : s + 1, :] * grad_window[at + s : at + s + count, :]
        grad_mixed[1, at : at + count, :] = total * value[start : start + count, :]
        grad_mixed[2, at : at + count, :] = total * key[start : start + count, :]

    def folded(terms):
        return jnp.sum(terms.reshape(terms.shape[0] // 8, 8, LANES), axis=0)

    def put(place, sums):
        for s in range(TAPS):
            tap_sums[place, s : s + 1, :] = jnp.sum(sums[s], axis=0, keepdims=True)
        tap_sums[place, TAPS : TAPS + 1, :] = jnp.zeros((1, LANES), F32)

    def transposed(j, at, count):
        total = feat_taps[j, 0:1, :] * grad_mixed[j, at : at + count, :]
        for s in range(1, TAPS):
            total = total + feat_taps[j, s : s + 1, :] * grad_mixed[j, at + s : at + s + count, :]
        return total

    for j in range(3):
        head[j] = transposed(j, 0, HALO)
        sums = [jnp.zeros((8, LANES), F32) for _ in range(TAPS)]
        spans = [(HALO + start, count) for start, count in spread(rows)]
        for at, count in ([(HALO - LEAD, LEAD)] if j > 0 else []) + spans:
            here = grad_mixed[j, at : at + count, :]
            for s in range(TAPS):
                sums[s] = sums[s] + folded(here * feats[j, at - s : at - s + count, :])
            if at >= HALO:
                total = transposed(j, at, count)
                grads[j, at - HALO : at - HALO + count, :] = total.astype(BF16)
                if at + count == HALO + rows:
                    tail[j] = total[count - HALO :]
        put(j, sums)
    sums = [jnp.zeros((8, LANES), F32) for _ in range(TAPS)]
    for start, count in spread(rows):
        here = grad_window[HALO + start : HALO + start + count, :]
        for s in range(TAPS):
            base = LEAD + start - s
            sums[s] = sums[s] + folded(here * product[base : base + count, :])
    put(3, sums)


def backward(near, far, saved, before, own, feat_taps, inner_taps, after):
    _, rows, channels = own.shape
    saved_spec = lane_spec(rows + LEAD)
    edge = jax.ShapeDtypeStruct((3, HALO, channels), F32)
    return call(
        backward_kernel,
        "backward",
        120 * rows * channels,
        40 * rows * channels,
        grid=(channels // LANES,),
        in_specs=[
            lane_spec(rows), lane_spec(rows), saved_spec, lane_spec(rows), saved_spec, saved_spec,
            saved_spec, lane_spec(3, HALO), lane_spec(3, rows), lane_spec(3, TAPS),
            lane_spec(TAPS), UNREAD,
        ],
        out_specs=[lane_spec(3, rows), lane_spec(3, HALO), lane_spec(3, HALO), lane_spec(4, 8)],
        out_shape=[
            jax.ShapeDtypeStruct((3, rows, channels), BF16),
            edge,
            edge,
            jax.ShapeDtypeStruct((4, 8, channels), F32),
        ],
        scratch_shapes=[
            pltpu.VMEM((3, rows + HALO, LANES), F32),
            pltpu.VMEM((rows + HALO + LEAD, LANES), F32),
            pltpu.VMEM((3, rows + HALO + LEAD, LANES), F32),
        ],
    )(near, far, *saved, before, own, feat_taps, inner_taps, after)


def gated_grad_kernel(col, grads, weight, far, near):
    wide = jnp.concatenate([grads[b] for b in range(grads.shape[0])], axis=1)
    total = lax.dot_general(
        wide, weight[...], (((1,), (1,)), ((), ())), preferred_element_type=F32
    )
    half = near.shape[1]

    @pl.when(col[0] == 0)
    def _():
        near[...] = total[:, :half]
        far[...] = total[:, half:].astype(BF16)

    @pl.when(col[0] != 0)
    def _():
        near[...] = total[:, half:]
        far[...] = total[:, :half].astype(BF16)


def gated_grad(col, grads, weight):
    blocks, rows, width = grads.shape
    channels = weight.shape[0]
    half = channels // 2
    step = min(rows, 128)
    return call(
        gated_grad_kernel,
        "gated_grad",
        2 * rows * channels * blocks * width,
        2 * blocks * width * (rows + channels) + 6 * rows * half,
        grid=(rows // step,),
        in_specs=[
            SCALAR,
            pl.BlockSpec((blocks, step, width), lambda i: (0, i, 0)),
            whole(weight.shape),
        ],
        out_specs=[pl.BlockSpec((step, half), lambda i: (i, 0))] * 2,
        out_shape=[
            jax.ShapeDtypeStruct((rows, half), BF16),
            jax.ShapeDtypeStruct((rows, half), F32),
        ],
    )(col, grads, weight)


def sent_weight_kernel(gated, grad, _, out):
    out[0] = jnp.dot(gated[...], grad[0], preferred_element_type=F32).astype(BF16)


def sent_weight(gated, grads, after):
    channels, rows = gated.shape
    blocks, _, width = grads.shape
    return call(
        sent_weight_kernel,
        "sent_weight",
        2 * rows * channels * blocks * width,
        2 * blocks * width * (rows + channels) + 2 * rows * channels,
        grid=(blocks,),
        in_specs=[
            whole(gated.shape),
            pl.BlockSpec((1, rows, width), lambda i: (i, 0, 0)),
            UNREAD,
        ],
        out_specs=pl.BlockSpec((1, channels, width), lambda i: (i, 0, 0)),
        out_shape=jax.ShapeDtypeStruct((blocks, channels, width), BF16),
    )(gated, grads, after)


def slices(place, held, parts, out_own, out_far):
    size = held.shape[-2] // parts
    out_own[...] = held[..., pl.ds(pl.multiple_of(place * size, size), size), :]
    for step, out in enumerate(out_far, 1):
        to = lax.rem(place + step, parts)
        out[...] = held[..., pl.ds(pl.multiple_of(to * size, size), size), :].astype(BF16)


def kept_weight_kernel(x, gated, grad, arrived, own, *rest):
    *far, held = rest
    held[0] = jnp.dot(gated[...], grad[0], preferred_element_type=F32) + arrived[0].astype(F32)
    slices(x[0], held, len(far) + 1, own, far)


def kept_weight(x, parts, gated, grads, arrived):
    channels, rows = gated.shape
    blocks, _, width = grads.shape
    shape = (blocks, channels // parts, width)
    spec = pl.BlockSpec((1, *shape[1:]), lambda i: (i, 0, 0))
    return call(
        kept_weight_kernel,
        "kept_weight",
        2 * rows * channels * blocks * width,
        2 * blocks * width * (rows + 3 * channels) + 2 * rows * channels,
        grid=(blocks,),
        in_specs=[
            SCALAR,
            whole(gated.shape),
            pl.BlockSpec((1, rows, width), lambda i: (i, 0, 0)),
            pl.BlockSpec((1, channels, width), lambda i: (i, 0, 0)),
        ],
        out_specs=[spec] * parts,
        out_shape=[jax.ShapeDtypeStruct(shape, F32)]
        + [jax.ShapeDtypeStruct(shape, BF16)] * (parts - 1),
        scratch_shapes=[pltpu.VMEM((1, channels, width), F32)],
    )(x, gated, grads, arrived)


def middle_kernel(parts, z, own, *rest):
    arrived, rest = rest[: parts - 1], rest[parts - 1 :]
    taps, taps_arrived, tail, head, _, out_own, out_taps, *far, out_grads, held = rest
    total = own[...]
    for piece in arrived:
        total = total + piece[...].astype(F32)
    held[...] = total
    blocks = held.shape[0]
    slices(z[0], held, len(far) + 1, out_own, [out.at[0:blocks] for out in far])
    sums = taps[...] + taps_arrived[...]
    out_taps[...] = sums
    high = sums.astype(BF16).astype(F32)
    both = jnp.concatenate([high, sums - high], axis=1).astype(BF16)
    for out in far:
        out[blocks:, :, :] = both
    out_grads[...] = (tail[...] + head[...]).astype(BF16)


def middle(z, parts, own, arrived, taps, taps_arrived, tail, head, grads):
    blocks, channels, width = own.shape
    shape = (blocks, channels // parts, width)
    wire = (blocks + taps.shape[0], *shape[1:])
    last = grads.shape[1] // HALO - 1
    return call(
        lambda *refs: middle_kernel(len(arrived) + 1, *refs),
        "middle",
        4 * own.size,
        10 * own.size,
        grid=(1,),
        in_specs=[SCALAR]
        + [whole(v.shape) for v in (own, *arrived, taps, taps_arrived, tail, head)]
        + [UNREAD],
        out_specs=[whole(shape), whole(taps.shape)]
        + [whole(wire)] * (parts - 1)
        + [pl.BlockSpec(tail.shape, lambda i: (0, last, 0))],
        out_shape=[jax.ShapeDtypeStruct(shape, F32), jax.ShapeDtypeStruct(taps.shape, F32)]
        + [jax.ShapeDtypeStruct(wire, BF16)] * (parts - 1)
        + [jax.ShapeDtypeStruct(grads.shape, grads.dtype)],
        scratch_shapes=[pltpu.VMEM(own.shape, F32)],
        input_output_aliases={len(arrived) + 6: parts + 1},
    )(z, own, *arrived, taps, taps_arrived, tail, head, grads)


def last_kernel(scale, own, taps, *rest):
    *arrived, out, out_feat, out_inner = rest
    blocks, _, width = own.shape
    for b in range(blocks):
        total = own[b]
        for piece in arrived:
            total = total + piece[b].astype(F32)
        out[:, b * width : (b + 1) * width] = (total * scale).astype(BF16)
    for j in range(4):
        total = taps[j]
        for piece in arrived:
            both = piece[blocks + j].astype(F32)
            total = total + (both[:8] + both[8:])
        total = (total * scale)[:TAPS]
        if j < 3:
            out_feat[j] = total
        else:
            out_inner[...] = total


def last(scale, own, taps, arrived):
    blocks, channels, width = own.shape
    shapes = [
        jax.ShapeDtypeStruct((channels, blocks * width), BF16),
        jax.ShapeDtypeStruct((3, TAPS, width), F32),
        jax.ShapeDtypeStruct((TAPS, width), F32),
    ]
    return call(
        lambda *refs: last_kernel(scale, *refs),
        "last",
        4 * own.size,
        12 * own.size,
        grid=(1,),
        in_specs=[whole(v.shape) for v in (own, taps, *arrived)],
        out_specs=[whole(s.shape) for s in shapes],
        out_shape=shapes,
    )(own, taps, *arrived)


def ctx_permute(value, target):
    nx, nz, nc = (lax.axis_size(a) for a in CTX)
    pairs = []
    for x in range(nx):
        for z in range(nz):
            for c in range(nc):
                to = target(x, z, c)
                pairs.append(((x * nz + z) * nc + c, (to[0] * nz + to[1]) * nc + to[2]))
    return lax.ppermute(value, CTX, pairs)


def ctx_shift(value, steps):
    count = math.prod(lax.axis_size(a) for a in CTX)
    return lax.ppermute(
        value, CTX, [(i, i + steps) for i in range(count) if 0 <= i + steps < count]
    )


def rotated(pieces, axis):
    count = lax.axis_size(axis)
    return [
        lax.ppermute(piece, axis, [(i, (i + step) % count) for i in range(count)])
        for step, piece in enumerate(pieces, 1)
    ]


def body(featured, feat_taps, inner_taps, out_weight, out_grad):
    rows = featured.shape[0]
    nx, nz, nc = (lax.axis_size(a) for a in CTX)
    inv_root = 1.0 / math.sqrt(rows * nx * nz * nc)
    col, x, z, core = (lax.axis_index(a) for a in ("col", "x", "zl", "core"))

    grads = lax.all_gather(out_grad, "row", axis=0)

    own = jnp.transpose(featured, (1, 0, 2))
    before = ctx_shift(own[:, rows - HALO :], 1)
    gated, *saved = forward(before, own, feat_taps, inner_taps)
    other = lax.ppermute(gated, "col", [(0, 1), (1, 0)])
    both = jnp.concatenate(
        [jnp.where(col == 0, gated, other), jnp.where(col == 0, other, gated)], axis=1
    )
    channels = both.shape[1]
    split = both.T.reshape(nx * nz, nc, channels // (nx * nz * nc), rows)
    kept, sent = (
        lax.dynamic_index_in_dim(split, c, 1, keepdims=False).reshape(channels // nc, rows)
        for c in (core, 1 - core)
    )

    far, near = gated_grad(jnp.full((1,), col, jnp.int32), grads, out_weight)
    arrived_far = lax.ppermute(far, "col", [(0, 1), (1, 0)])

    arrived = ctx_permute(sent_weight(sent, grads, far), lambda x, z, c: (x, z, 1 - c))
    own_x, *pieces = kept_weight(jnp.full((1,), x, jnp.int32), nx, kept, grads, arrived)
    arrived = rotated(pieces, "x")

    grad_own, head, tail, taps = backward(
        near, arrived_far, saved, before, own, feat_taps, inner_taps, own_x
    )
    head = ctx_shift(head, -1)
    taps = taps + ctx_permute(taps, lambda x, z, c: (x, z, c ^ 1))
    taps = taps + ctx_permute(taps, lambda x, z, c: (x ^ 1, z, c))
    taps_arrived = ctx_permute(taps, lambda x, z, c: (nx - 1 - x, z, c))
    own_z, taps, *rest = middle(
        jnp.full((1,), z, jnp.int32), nz, own_x, arrived, taps, taps_arrived, tail, head, grad_own
    )
    *pieces, grad_own = rest
    grad_weight, grad_feat_taps, grad_inner_taps = last(
        inv_root, own_z, taps, rotated(pieces, "zl")
    )
    return jnp.transpose(grad_own, (1, 0, 2)), grad_weight, grad_feat_taps, grad_inner_taps


def fine_mesh(mesh):
    row, col, ctx = mesh.devices.shape
    return Mesh(mesh.devices.reshape(row, col, ctx // 8, 4, 2), ("row", "col", *CTX))


def solution(mesh):
    return jax.shard_map(
        body,
        mesh=fine_mesh(mesh),
        in_specs=(
            P(CTX, None, ("row", "col")),
            P(None, None, ("row", "col")),
            P(None, ("row", "col")),
            P("row", "col"),
            P(CTX, ("col", "row")),
        ),
        out_specs=(
            P(CTX, None, ("row", "col")),
            P(("row", *CTX), "col"),
            P(None, None, ("row", "col")),
            P(None, ("row", "col")),
        ),
        check_vma=False,
    )
```

```python
import math

import jax
import jax.numpy as jnp
from jax import lax
from jax.experimental import pallas as pl
from jax.experimental.pallas import tpu as pltpu
from jax.sharding import Mesh
from jax.sharding import PartitionSpec as P

TAPS = 7
HALO = 16
LEAD = 8
CHUNK = 64
LANES = 128
CTX = ("x", "zl", "core")
F32 = jnp.float32
BF16 = jnp.bfloat16
VMEM_BYTES = 24 << 20


def spread(total):
    return [(start, min(CHUNK, total - start)) for start in range(0, total, CHUNK)]


def lane_spec(*lead):
    return pl.BlockSpec((*lead, LANES), lambda i: (0,) * len(lead) + (i,))


def whole(shape):
    return pl.BlockSpec(shape, lambda *_: (0,) * len(shape))


SCALAR = pl.BlockSpec(memory_space=pltpu.SMEM)
UNREAD = pl.BlockSpec(memory_space=pl.ANY)


def call(kernel, name, flops, moved, **kwargs):
    return pl.pallas_call(
        kernel,
        name=name,
        compiler_params=pltpu.CompilerParams(vmem_limit_bytes=VMEM_BYTES),
        cost_estimate=pl.CostEstimate(flops=flops, bytes_accessed=moved, transcendentals=0),
        **kwargs,
    )


def load_features(before, own, feats):
    rows = own.shape[1]
    for j in range(3):
        feats[j, 0:HALO, :] = before[j].astype(F32)
        for start, count in spread(rows):
            feats[j, HALO + start : HALO + start + count, :] = own[
                j, start : start + count, :
            ].astype(F32)


def forward_kernel(
    before, own, feat_taps, inner_taps, gated, query, window, key, value, product, feats
):
    rows = own.shape[1]
    load_features(before, own, feats)
    for start, count in spread(rows + LEAD):
        base = HALO - LEAD + start
        parts = []
        for j in range(3):
            total = feat_taps[j, 0:1, :] * feats[j, base : base + count, :]
            for s in range(1, TAPS):
                total = total + feat_taps[j, s : s + 1, :] * feats[j, base - s : base - s + count, :]
            parts.append(total)
        query[start : start + count, :] = parts[0]
        key[start : start + count, :] = parts[1]
        value[start : start + count, :] = parts[2]
        product[start : start + count, :] = parts[1] * parts[2]
    for start, count in spread(rows):
        base = LEAD + start
        total = inner_taps[0:1, :] * product[base : base + count, :]
        for s in range(1, TAPS):
            total = total + inner_taps[s : s + 1, :] * product[base - s : base - s + count, :]
        window[start : start + count, :] = total
        gated[start : start + count, :] = (query[base : base + count, :] * total).astype(BF16)


def forward(before, own, feat_taps, inner_taps):
    _, rows, channels = own.shape
    saved = jax.ShapeDtypeStruct((rows + LEAD, channels), F32)
    saved_spec = lane_spec(rows + LEAD)
    return call(
        forward_kernel,
        "forward",
        60 * rows * channels,
        30 * rows * channels,
        grid=(channels // LANES,),
        in_specs=[lane_spec(3, HALO), lane_spec(3, rows), lane_spec(3, TAPS), lane_spec(TAPS)],
        out_specs=[lane_spec(rows), saved_spec, lane_spec(rows), saved_spec, saved_spec, saved_spec],
        out_shape=[
            jax.ShapeDtypeStruct((rows, channels), BF16),
            saved,
            jax.ShapeDtypeStruct((rows, channels), F32),
            saved,
            saved,
            saved,
        ],
        scratch_shapes=[pltpu.VMEM((3, rows + HALO, LANES), F32)],
    )(before, own, feat_taps, inner_taps)


def backward_kernel(
    col, near, far, query, window, key, value, product, before, own, feat_taps, inner_taps, _,
    grads, head, tail, tap_sums, feats, grad_window, grad_mixed,
):
    rows = own.shape[1]
    load_features(before, own, feats)
    zeros = jnp.zeros((HALO, LANES), F32)
    grad_window[0:HALO, :] = zeros
    grad_window[HALO + rows :, :] = zeros[:LEAD]
    for j in range(3):
        grad_mixed[j, 0:HALO, :] = zeros
        grad_mixed[j, HALO + rows :, :] = zeros[:LEAD]
    for start, count in spread(rows):
        at = HALO + start
        total = near[start : start + count, :] + far[1 - col[0], start : start + count, :].astype(F32)
        grad_window[at : at + count, :] = total * query[LEAD + start : LEAD + start + count, :]
        grad_mixed[0, at : at + count, :] = total * window[start : start + count, :]
    for start, count in spread(rows + LEAD):
        at = HALO - LEAD + start
        total = inner_taps[0:1, :] * grad_window[at : at + count, :]
        for s in range(1, TAPS):
            total = total + inner_taps[s : s + 1, :] * grad_window[at + s : at + s + count, :]
        grad_mixed[1, at : at + count, :] = total * value[start : start + count, :]
        grad_mixed[2, at : at + count, :] = total * key[start : start + count, :]

    def folded(terms):
        return jnp.sum(terms.reshape(terms.shape[0] // 8, 8, LANES), axis=0)

    def put(place, sums):
        for s in range(TAPS):
            tap_sums[place, s : s + 1, :] = jnp.sum(sums[s], axis=0, keepdims=True)
        tap_sums[place, TAPS : TAPS + 1, :] = jnp.zeros((1, LANES), F32)

    def transposed(j, at, count):
        total = feat_taps[j, 0:1, :] * grad_mixed[j, at : at + count, :]
        for s in range(1, TAPS):
            total = total + feat_taps[j, s : s + 1, :] * grad_mixed[j, at + s : at + s + count, :]
        return total

    for j in range(3):
        head[j] = transposed(j, 0, HALO)
        sums = [jnp.zeros((8, LANES), F32) for _ in range(TAPS)]
        spans = [(HALO + start, count) for start, count in spread(rows)]
        for at, count in ([(HALO - LEAD, LEAD)] if j > 0 else []) + spans:
            here = grad_mixed[j, at : at + count, :]
            for s in range(TAPS):
                sums[s] = sums[s] + folded(here * feats[j, at - s : at - s + count, :])
            if at >= HALO:
                total = transposed(j, at, count)
                grads[j, at - HALO : at - HALO + count, :] = total.astype(BF16)
                if at + count == HALO + rows:
                    tail[j] = total[count - HALO :]
        put(j, sums)
    sums = [jnp.zeros((8, LANES), F32) for _ in range(TAPS)]
    for start, count in spread(rows):
        here = grad_window[HALO + start : HALO + start + count, :]
        for s in range(TAPS):
            base = LEAD + start - s
            sums[s] = sums[s] + folded(here * product[base : base + count, :])
    put(3, sums)


def backward(col, near, far, saved, before, own, feat_taps, inner_taps, after):
    _, rows, channels = own.shape
    saved_spec = lane_spec(rows + LEAD)
    edge = jax.ShapeDtypeStruct((3, HALO, channels), F32)
    return call(
        backward_kernel,
        "backward",
        120 * rows * channels,
        40 * rows * channels,
        grid=(channels // LANES,),
        in_specs=[
            SCALAR, lane_spec(rows), lane_spec(2, rows), saved_spec, lane_spec(rows), saved_spec,
            saved_spec, saved_spec, lane_spec(3, HALO), lane_spec(3, rows), lane_spec(3, TAPS),
            lane_spec(TAPS), UNREAD,
        ],
        out_specs=[lane_spec(3, rows), lane_spec(3, HALO), lane_spec(3, HALO), lane_spec(4, 8)],
        out_shape=[
            jax.ShapeDtypeStruct((3, rows, channels), BF16),
            edge,
            edge,
            jax.ShapeDtypeStruct((4, 8, channels), F32),
        ],
        scratch_shapes=[
            pltpu.VMEM((3, rows + HALO, LANES), F32),
            pltpu.VMEM((rows + HALO + LEAD, LANES), F32),
            pltpu.VMEM((3, rows + HALO + LEAD, LANES), F32),
        ],
    )(col, near, far, *saved, before, own, feat_taps, inner_taps, after)


def gated_grad_kernel(col, grads, weight, _, far, near):
    wide = jnp.concatenate([grads[b] for b in range(grads.shape[0])], axis=1)
    total = lax.dot_general(
        wide, weight[...], (((1,), (1,)), ((), ())), preferred_element_type=F32
    )
    half = near.shape[1]

    @pl.when(col[0] == 0)
    def _():
        near[...] = total[:, :half]
        far[...] = total[:, half:].astype(BF16)

    @pl.when(col[0] != 0)
    def _():
        near[...] = total[:, half:]
        far[...] = total[:, :half].astype(BF16)


def gated_grad(col, grads, weight, after):
    blocks, rows, width = grads.shape
    channels = weight.shape[0]
    half = channels // 2
    step = min(rows, 128)
    return call(
        gated_grad_kernel,
        "gated_grad",
        2 * rows * channels * blocks * width,
        2 * blocks * width * (rows + channels) + 6 * rows * half,
        grid=(rows // step,),
        in_specs=[
            SCALAR,
            pl.BlockSpec((blocks, step, width), lambda i: (0, i, 0)),
            whole(weight.shape),
            UNREAD,
        ],
        out_specs=[pl.BlockSpec((step, half), lambda i: (i, 0))] * 2,
        out_shape=[
            jax.ShapeDtypeStruct((rows, half), BF16),
            jax.ShapeDtypeStruct((rows, half), F32),
        ],
    )(col, grads, weight, after)


def sent_weight_kernel(gated, grad, out):
    out[0] = jnp.dot(gated[...], grad[0], preferred_element_type=F32).astype(BF16)


def sent_weight(gated, grads):
    channels, rows = gated.shape
    blocks, _, width = grads.shape
    return call(
        sent_weight_kernel,
        "sent_weight",
        2 * rows * channels * blocks * width,
        2 * blocks * width * (rows + channels) + 2 * rows * channels,
        grid=(blocks,),
        in_specs=[
            whole(gated.shape),
            pl.BlockSpec((1, rows, width), lambda i: (i, 0, 0)),
        ],
        out_specs=pl.BlockSpec((1, channels, width), lambda i: (i, 0, 0)),
        out_shape=jax.ShapeDtypeStruct((blocks, channels, width), BF16),
    )(gated, grads)


def kept_weight_kernel(gated, grad, arrived, _, out):
    total = jnp.dot(gated[...], grad[0], preferred_element_type=F32) + arrived[0].astype(F32)
    out[...] = total.astype(BF16).reshape(out.shape)


def kept_weight(parts, gated, grads, arrived, after):
    channels, rows = gated.shape
    blocks, _, width = grads.shape
    size = channels // parts
    return call(
        kept_weight_kernel,
        "kept_weight",
        2 * rows * channels * blocks * width,
        2 * blocks * width * (rows + 2 * channels) + 2 * rows * channels,
        grid=(blocks,),
        in_specs=[
            whole(gated.shape),
            pl.BlockSpec((1, rows, width), lambda i: (i, 0, 0)),
            pl.BlockSpec((1, channels, width), lambda i: (i, 0, 0)),
            UNREAD,
        ],
        out_specs=pl.BlockSpec((parts, 1, size, width), lambda i: (0, i, 0, 0)),
        out_shape=jax.ShapeDtypeStruct((parts, blocks, size, width), BF16),
    )(gated, grads, arrived, after)


def middle_kernel(pair, taps, taps_arrived, tail, head, _, out, out_taps, out_grads):
    parts, _, size, _ = out.shape
    blocks = pair.shape[0]
    sums = taps[...] + taps_arrived[...]
    out_taps[...] = sums
    high = sums.astype(BF16).astype(F32)
    both = jnp.concatenate([high, sums - high], axis=1).astype(BF16)
    for part in range(parts):
        out[part, 0:blocks] = pair[:, part * size : (part + 1) * size, :]
        out[part, blocks:] = both
    out_grads[...] = (tail[...] + head[...]).astype(BF16)


def middle(parts, pair, taps, taps_arrived, tail, head, grads):
    blocks, channels, width = pair.shape
    shape = (parts, blocks + taps.shape[0], channels // parts, width)
    final = grads.shape[1] // HALO - 1
    return call(
        middle_kernel,
        "middle",
        4 * pair.size,
        4 * pair.size,
        grid=(1,),
        in_specs=[whole(v.shape) for v in (pair, taps, taps_arrived, tail, head)] + [UNREAD],
        out_specs=[
            whole(shape),
            whole(taps.shape),
            pl.BlockSpec(tail.shape, lambda i: (0, final, 0)),
        ],
        out_shape=[
            jax.ShapeDtypeStruct(shape, BF16),
            jax.ShapeDtypeStruct(taps.shape, F32),
            jax.ShapeDtypeStruct(grads.shape, grads.dtype),
        ],
        input_output_aliases={5: 2},
    )(pair, taps, taps_arrived, tail, head, grads)


def last_kernel(scale, z, taps, arrived, out, out_feat, out_inner):
    parts, _, _, width = arrived.shape
    blocks = out.shape[1] // width
    for b in range(blocks):
        total = arrived[0, b].astype(F32)
        for part in range(1, parts):
            total = total + arrived[part, b].astype(F32)
        out[:, b * width : (b + 1) * width] = (total * scale).astype(BF16)
    for j in range(4):
        total = taps[j]
        for part in range(parts):
            both = arrived[part, blocks + j].astype(F32)
            total = total + jnp.where(z[0] == part, 0.0, both[:8] + both[8:])
        total = (total * scale)[:TAPS]
        if j < 3:
            out_feat[j] = total
        else:
            out_inner[...] = total


def last(scale, z, taps, arrived):
    parts, count, channels, width = arrived.shape
    blocks = count - taps.shape[0]
    shapes = [
        jax.ShapeDtypeStruct((channels, blocks * width), BF16),
        jax.ShapeDtypeStruct((3, TAPS, width), F32),
        jax.ShapeDtypeStruct((TAPS, width), F32),
    ]
    return call(
        lambda *refs: last_kernel(scale, *refs),
        "last",
        2 * arrived.size,
        2 * arrived.size,
        grid=(1,),
        in_specs=[SCALAR, whole(taps.shape), whole(arrived.shape)],
        out_specs=[whole(s.shape) for s in shapes],
        out_shape=shapes,
    )(z, taps, arrived)


def ctx_permute(value, target):
    nx, nz, nc = (lax.axis_size(a) for a in CTX)
    pairs = []
    for x in range(nx):
        for z in range(nz):
            for c in range(nc):
                to = target(x, z, c)
                pairs.append(((x * nz + z) * nc + c, (to[0] * nz + to[1]) * nc + to[2]))
    return lax.ppermute(value, CTX, pairs)


def ctx_shift(value, steps):
    count = math.prod(lax.axis_size(a) for a in CTX)
    return lax.ppermute(
        value, CTX, [(i, i + steps) for i in range(count) if 0 <= i + steps < count]
    )


def body(featured, feat_taps, inner_taps, out_weight, out_grad):
    rows = featured.shape[0]
    nx, nz, nc = (lax.axis_size(a) for a in CTX)
    inv_root = 1.0 / math.sqrt(rows * nx * nz * nc)
    core = lax.axis_index("core")
    col, z = (jnp.full((1,), lax.axis_index(a), jnp.int32) for a in ("col", "zl"))

    grads = lax.all_gather(out_grad, "row", axis=0)

    own = jnp.transpose(featured, (1, 0, 2))
    before = ctx_shift(own[:, rows - HALO :], 1)
    gated, *saved = forward(before, own, feat_taps, inner_taps)
    both = lax.all_gather(gated, "col", axis=1, tiled=True)
    channels = both.shape[1]
    split = both.T.reshape(nx * nz, nc, channels // (nx * nz * nc), rows)
    kept, sent = (
        lax.dynamic_index_in_dim(split, c, 1, keepdims=False).reshape(channels // nc, rows)
        for c in (core, 1 - core)
    )

    sent = sent_weight(sent, grads)
    arrived = ctx_permute(sent, lambda x, z, c: (x, z, 1 - c))
    far, near = gated_grad(col, grads, out_weight, sent)
    pair = kept_weight(nx, kept, grads, arrived, far)
    pair = lax.psum_scatter(pair, "x", scatter_dimension=0)

    far = lax.all_gather(far, "col", axis=0)
    grad_own, head, tail, taps = backward(
        col, near, far, saved, before, own, feat_taps, inner_taps, far
    )
    head = ctx_shift(head, -1)
    taps = lax.psum(taps, "core")
    taps = taps + ctx_permute(taps, lambda x, z, c: (x ^ 1, z, c))
    taps_arrived = ctx_permute(taps, lambda x, z, c: (nx - 1 - x, z, c))

    pieces, taps, grad_own = middle(nz, pair, taps, taps_arrived, tail, head, grad_own)
    pieces = lax.all_to_all(pieces, "zl", split_axis=0, concat_axis=0)
    grad_weight, grad_feat_taps, grad_inner_taps = last(inv_root, z, taps, pieces)
    return jnp.transpose(grad_own, (1, 0, 2)), grad_weight, grad_feat_taps, grad_inner_taps


def fine_mesh(mesh):
    row, col, ctx = mesh.devices.shape
    return Mesh(mesh.devices.reshape(row, col, ctx // 8, 4, 2), ("row", "col", *CTX))


def solution(mesh):
    return jax.shard_map(
        body,
        mesh=fine_mesh(mesh),
        in_specs=(
            P(CTX, None, ("row", "col")),
            P(None, None, ("row", "col")),
            P(None, ("row", "col")),
            P("row", "col"),
            P(CTX, ("col", "row")),
        ),
        out_specs=(
            P(CTX, None, ("row", "col")),
            P(("row", *CTX), "col"),
            P(None, None, ("row", "col")),
            P(None, ("row", "col")),
        ),
        check_vma=False,
    )
```

```python
import math

import jax
import jax.numpy as jnp
from jax import lax
from jax.experimental import pallas as pl
from jax.experimental.pallas import tpu as pltpu
from jax.sharding import Mesh
from jax.sharding import PartitionSpec as P

TAPS = 7
HALO = 16
LEAD = 8
CHUNK = 64
LANES = 128
CTX = ("x", "zl", "core")
F32 = jnp.float32
BF16 = jnp.bfloat16
VMEM_BYTES = 24 << 20
STREAM_BYTES = 56 << 20


def spread(total):
    return [(start, min(CHUNK, total - start)) for start in range(0, total, CHUNK)]


def lane_spec(*lead):
    return pl.BlockSpec((*lead, LANES), lambda i: (0,) * len(lead) + (i,))


def whole(shape):
    return pl.BlockSpec(shape, lambda *_: (0,) * len(shape))


SCALAR = pl.BlockSpec(memory_space=pltpu.SMEM)
UNREAD = pl.BlockSpec(memory_space=pl.ANY)
IN_HBM = pl.BlockSpec(memory_space=pltpu.HBM)


def call(kernel, name, flops, moved, vmem=VMEM_BYTES, **kwargs):
    return pl.pallas_call(
        kernel,
        name=name,
        compiler_params=pltpu.CompilerParams(vmem_limit_bytes=vmem),
        cost_estimate=pl.CostEstimate(flops=flops, bytes_accessed=moved, transcendentals=0),
        **kwargs,
    )


def load_features(before, own, feats):
    rows = own.shape[1]
    for j in range(3):
        feats[j, 0:HALO, :] = before[j].astype(F32)
        for start, count in spread(rows):
            feats[j, HALO + start : HALO + start + count, :] = own[
                j, start : start + count, :
            ].astype(F32)


def mixed_parts(feats, feat_taps, start, count):
    base = HALO - LEAD + start
    parts = []
    for j in range(3):
        total = feat_taps[j, 0:1, :] * feats[j, base : base + count, :]
        for s in range(1, TAPS):
            total = total + feat_taps[j, s : s + 1, :] * feats[j, base - s : base - s + count, :]
        parts.append(total)
    return parts


def window_rows(product, inner_taps, start, count):
    base = LEAD + start
    total = inner_taps[0:1, :] * product[base : base + count, :]
    for s in range(1, TAPS):
        total = total + inner_taps[s : s + 1, :] * product[base - s : base - s + count, :]
    return total


def forward_kernel(before, own, feat_taps, inner_taps, gated, feats, query, product):
    rows = own.shape[1]
    load_features(before, own, feats)
    for start, count in spread(rows + LEAD):
        parts = mixed_parts(feats, feat_taps, start, count)
        query[start : start + count, :] = parts[0]
        product[start : start + count, :] = parts[1] * parts[2]
    for start, count in spread(rows):
        base = LEAD + start
        gated[start : start + count, :] = (
            query[base : base + count, :] * window_rows(product, inner_taps, start, count)
        ).astype(BF16)


def forward(before, own, feat_taps, inner_taps):
    _, rows, channels = own.shape
    return call(
        forward_kernel,
        "forward",
        60 * rows * channels,
        8 * rows * channels,
        grid=(channels // LANES,),
        in_specs=[lane_spec(3, HALO), lane_spec(3, rows), lane_spec(3, TAPS), lane_spec(TAPS)],
        out_specs=lane_spec(rows),
        out_shape=jax.ShapeDtypeStruct((rows, channels), BF16),
        scratch_shapes=[
            pltpu.VMEM((3, rows + HALO, LANES), F32),
            pltpu.VMEM((rows + LEAD, LANES), F32),
            pltpu.VMEM((rows + LEAD, LANES), F32),
        ],
    )(before, own, feat_taps, inner_taps)


def backward_kernel(
    col, near, far, before, own, feat_taps, inner_taps, _,
    grads, head, tail, tap_sums, feats, query, key, value, product, grad_window, grad_mixed,
):
    rows = own.shape[1]
    load_features(before, own, feats)
    for start, count in spread(rows + LEAD):
        parts = mixed_parts(feats, feat_taps, start, count)
        query[start : start + count, :] = parts[0]
        key[start : start + count, :] = parts[1]
        value[start : start + count, :] = parts[2]
        product[start : start + count, :] = parts[1] * parts[2]
    zeros = jnp.zeros((HALO, LANES), F32)
    grad_window[0:HALO, :] = zeros
    grad_window[HALO + rows :, :] = zeros[:LEAD]
    for j in range(3):
        grad_mixed[j, 0:HALO, :] = zeros
        grad_mixed[j, HALO + rows :, :] = zeros[:LEAD]
    for start, count in spread(rows):
        at = HALO + start
        total = near[start : start + count, :] + far[
            1 - col[0], start : start + count, :
        ].astype(F32)
        grad_window[at : at + count, :] = total * query[LEAD + start : LEAD + start + count, :]
        grad_mixed[0, at : at + count, :] = total * window_rows(product, inner_taps, start, count)
    for start, count in spread(rows + LEAD):
        at = HALO - LEAD + start
        total = inner_taps[0:1, :] * grad_window[at : at + count, :]
        for s in range(1, TAPS):
            total = total + inner_taps[s : s + 1, :] * grad_window[at + s : at + s + count, :]
        grad_mixed[1, at : at + count, :] = total * value[start : start + count, :]
        grad_mixed[2, at : at + count, :] = total * key[start : start + count, :]

    def folded(terms):
        return jnp.sum(terms.reshape(terms.shape[0] // 8, 8, LANES), axis=0)

    def put(place, sums):
        for s in range(TAPS):
            tap_sums[place, s : s + 1, :] = jnp.sum(sums[s], axis=0, keepdims=True)
        tap_sums[place, TAPS : TAPS + 1, :] = jnp.zeros((1, LANES), F32)

    def transposed(j, at, count):
        total = feat_taps[j, 0:1, :] * grad_mixed[j, at : at + count, :]
        for s in range(1, TAPS):
            total = total + feat_taps[j, s : s + 1, :] * grad_mixed[j, at + s : at + s + count, :]
        return total

    for j in range(3):
        head[j] = transposed(j, 0, HALO)
        sums = [jnp.zeros((8, LANES), F32) for _ in range(TAPS)]
        spans = [(HALO + start, count) for start, count in spread(rows)]
        for at, count in ([(HALO - LEAD, LEAD)] if j > 0 else []) + spans:
            here = grad_mixed[j, at : at + count, :]
            for s in range(TAPS):
                sums[s] = sums[s] + folded(here * feats[j, at - s : at - s + count, :])
            if at >= HALO:
                total = transposed(j, at, count)
                grads[j, at - HALO : at - HALO + count, :] = total.astype(BF16)
                if at + count == HALO + rows:
                    tail[j] = total[count - HALO :]
        put(j, sums)
    sums = [jnp.zeros((8, LANES), F32) for _ in range(TAPS)]
    for start, count in spread(rows):
        here = grad_window[HALO + start : HALO + start + count, :]
        for s in range(TAPS):
            base = LEAD + start - s
            sums[s] = sums[s] + folded(here * product[base : base + count, :])
    put(3, sums)


def backward(col, near, far, before, own, feat_taps, inner_taps, after):
    _, rows, channels = own.shape
    edge = jax.ShapeDtypeStruct((3, HALO, channels), F32)
    return call(
        backward_kernel,
        "backward",
        160 * rows * channels,
        20 * rows * channels,
        grid=(channels // LANES,),
        in_specs=[
            SCALAR, lane_spec(rows), lane_spec(2, rows), lane_spec(3, HALO), lane_spec(3, rows),
            lane_spec(3, TAPS), lane_spec(TAPS), UNREAD,
        ],
        out_specs=[lane_spec(3, rows), lane_spec(3, HALO), lane_spec(3, HALO), lane_spec(4, 8)],
        out_shape=[
            jax.ShapeDtypeStruct((3, rows, channels), BF16),
            edge,
            edge,
            jax.ShapeDtypeStruct((4, 8, channels), F32),
        ],
        scratch_shapes=[pltpu.VMEM((3, rows + HALO, LANES), F32)]
        + [pltpu.VMEM((rows + LEAD, LANES), F32)] * 4
        + [
            pltpu.VMEM((rows + HALO + LEAD, LANES), F32),
            pltpu.VMEM((3, rows + HALO + LEAD, LANES), F32),
        ],
    )(col, near, far, before, own, feat_taps, inner_taps, after)


def fetch(source, target, sems):
    copies = [
        pltpu.make_async_copy(source.at[i], target.at[i], sems.at[i])
        for i in range(source.shape[0])
    ]
    for copy in copies:
        copy.start()
    return copies


def products_kernel(
    col, gated, grads, weight, sent, far, near, held_grads, held_weight, grad_sems, weight_sem
):
    copies = fetch(grads, held_grads, grad_sems)
    weights = pltpu.make_async_copy(weight, held_weight, weight_sem)
    weights.start()
    blocks, rows, _ = held_grads.shape
    half = near.shape[1]
    for b in range(blocks):
        copies[b].wait()
        sent[b] = jnp.dot(gated[...], held_grads[b], preferred_element_type=F32).astype(BF16)
    weights.wait()
    step = min(rows, 128)
    for start in range(0, rows, step):
        span = slice(start, start + step)
        wide = jnp.concatenate([held_grads[b, span, :] for b in range(blocks)], axis=1)
        total = lax.dot_general(
            wide, held_weight[...], (((1,), (1,)), ((), ())), preferred_element_type=F32
        )
        first = col[0] == 0
        near[span, :] = jnp.where(first, total[:, :half], total[:, half:])
        far[span, :] = jnp.where(first, total[:, half:], total[:, :half]).astype(BF16)


def products(col, gated, grads, weight):
    channels, rows = gated.shape
    blocks, _, width = grads.shape
    half = weight.shape[0] // 2
    return call(
        products_kernel,
        "products",
        2 * rows * (channels + 2 * half) * blocks * width,
        2 * blocks * width * (rows + channels + 2 * half) + 6 * rows * half,
        vmem=STREAM_BYTES,
        in_specs=[SCALAR, pl.BlockSpec(memory_space=pltpu.VMEM), IN_HBM, IN_HBM],
        out_specs=[pl.BlockSpec(memory_space=pltpu.VMEM)] * 3,
        out_shape=[
            jax.ShapeDtypeStruct((blocks, channels, width), BF16),
            jax.ShapeDtypeStruct((rows, half), BF16),
            jax.ShapeDtypeStruct((rows, half), F32),
        ],
        scratch_shapes=[
            pltpu.VMEM(grads.shape, BF16),
            pltpu.VMEM(weight.shape, BF16),
            pltpu.SemaphoreType.DMA((blocks,)),
            pltpu.SemaphoreType.DMA,
        ],
    )(col, gated, grads, weight)


def kept_weight_kernel(gated, grads, arrived, out, done, held_grads, held, grad_sems, sems):
    copies = fetch(grads, held_grads, grad_sems)
    others = fetch(arrived, held, sems)
    done[...] = jnp.zeros_like(done)
    parts, _, size, _ = out.shape
    for b in range(held.shape[0]):
        copies[b].wait()
        total = jnp.dot(gated[...], held_grads[b], preferred_element_type=F32)
        others[b].wait()
        total = (total + held[b].astype(F32)).astype(BF16)
        for part in range(parts):
            out[part, b] = total[part * size : (part + 1) * size]


def kept_weight(parts, gated, grads, arrived):
    channels, rows = gated.shape
    blocks, _, width = grads.shape
    size = channels // parts
    return call(
        kept_weight_kernel,
        "kept_weight",
        2 * rows * channels * blocks * width,
        2 * blocks * width * (rows + 2 * channels) + 2 * rows * channels,
        in_specs=[pl.BlockSpec(memory_space=pltpu.VMEM), IN_HBM, IN_HBM],
        out_specs=[pl.BlockSpec(memory_space=pltpu.VMEM)] * 2,
        out_shape=[
            jax.ShapeDtypeStruct((parts, blocks, size, width), BF16),
            jax.ShapeDtypeStruct((8, LANES), F32),
        ],
        scratch_shapes=[
            pltpu.VMEM(grads.shape, BF16),
            pltpu.VMEM(arrived.shape, BF16),
            pltpu.SemaphoreType.DMA((blocks,)),
            pltpu.SemaphoreType.DMA((blocks,)),
        ],
    )(gated, grads, arrived)


def middle_kernel(pair, taps, taps_arrived, head, out, out_taps, out_head):
    parts, _, size, _ = out.shape
    blocks = pair.shape[0]
    sums = taps[...] + taps_arrived[...]
    out_taps[...] = sums
    high = sums.astype(BF16).astype(F32)
    both = jnp.concatenate([high, sums - high], axis=1).astype(BF16)
    for part in range(parts):
        out[part, 0:blocks] = pair[:, part * size : (part + 1) * size, :]
        out[part, blocks:] = both
    out_head[...] = head[...]


def middle(parts, pair, taps, taps_arrived, head):
    blocks, channels, width = pair.shape
    shape = (parts, blocks + taps.shape[0], channels // parts, width)
    args = (pair, taps, taps_arrived, head)
    outs = [
        jax.ShapeDtypeStruct(shape, BF16),
        jax.ShapeDtypeStruct(taps.shape, F32),
        jax.ShapeDtypeStruct(head.shape, F32),
    ]
    return call(
        middle_kernel,
        "middle",
        4 * pair.size,
        4 * pair.size,
        grid=(1,),
        in_specs=[whole(v.shape) for v in args],
        out_specs=[whole(v.shape) for v in outs],
        out_shape=outs,
    )(*args)


def last_kernel(
    scale, z, taps, arrived, tail, head, _, out, out_feat, out_inner, out_grads
):
    parts, _, _, width = arrived.shape
    blocks = out.shape[1] // width
    out_grads[...] = (tail[...] + head[...]).astype(BF16)
    for b in range(blocks):
        total = arrived[0, b].astype(F32)
        for part in range(1, parts):
            total = total + arrived[part, b].astype(F32)
        out[:, b * width : (b + 1) * width] = (total * scale).astype(BF16)
    for j in range(4):
        total = taps[j]
        for part in range(parts):
            both = arrived[part, blocks + j].astype(F32)
            total = total + jnp.where(z[0] == part, 0.0, both[:8] + both[8:])
        total = (total * scale)[:TAPS]
        if j < 3:
            out_feat[j] = total
        else:
            out_inner[...] = total


def last(scale, z, taps, arrived, tail, head, grads):
    parts, count, channels, width = arrived.shape
    blocks = count - taps.shape[0]
    final = grads.shape[1] // HALO - 1
    args = (taps, arrived, tail, head)
    shapes = [
        jax.ShapeDtypeStruct((channels, blocks * width), BF16),
        jax.ShapeDtypeStruct((3, TAPS, width), F32),
        jax.ShapeDtypeStruct((TAPS, width), F32),
    ]
    return call(
        lambda *refs: last_kernel(scale, *refs),
        "last",
        2 * arrived.size,
        2 * arrived.size,
        grid=(1,),
        in_specs=[SCALAR] + [whole(v.shape) for v in args] + [UNREAD],
        out_specs=[whole(v.shape) for v in shapes]
        + [pl.BlockSpec(tail.shape, lambda i: (0, final, 0))],
        out_shape=shapes + [jax.ShapeDtypeStruct(grads.shape, grads.dtype)],
        input_output_aliases={5: 3},
    )(z, *args, grads)


def ctx_permute(value, target):
    nx, nz, nc = (lax.axis_size(a) for a in CTX)
    pairs = []
    for x in range(nx):
        for z in range(nz):
            for c in range(nc):
                to = target(x, z, c)
                pairs.append(((x * nz + z) * nc + c, (to[0] * nz + to[1]) * nc + to[2]))
    return lax.ppermute(value, CTX, pairs)


def ctx_shift(value, steps):
    count = math.prod(lax.axis_size(a) for a in CTX)
    return lax.ppermute(
        value, CTX, [(i, i + steps) for i in range(count) if 0 <= i + steps < count]
    )


def body(featured, feat_taps, inner_taps, out_weight, out_grad):
    rows = featured.shape[0]
    nx, nz, nc = (lax.axis_size(a) for a in CTX)
    inv_root = 1.0 / math.sqrt(rows * nx * nz * nc)
    core = lax.axis_index("core")
    col, z = (jnp.full((1,), lax.axis_index(a), jnp.int32) for a in ("col", "zl"))

    grads = lax.all_gather(out_grad, "row", axis=0)

    own = jnp.transpose(featured, (1, 0, 2))
    before = ctx_shift(own[:, rows - HALO :], 1)
    gated = forward(before, own, feat_taps, inner_taps)
    both = lax.all_gather(gated, "col", axis=1, tiled=True)
    channels = both.shape[1]
    split = both.T.reshape(nx * nz, nc, channels // (nx * nz * nc), rows)
    kept, sent = (
        lax.dynamic_index_in_dim(split, c, 1, keepdims=False).reshape(channels // nc, rows)
        for c in (core, 1 - core)
    )

    sent, far, near = products(col, sent, grads, out_weight)
    arrived = ctx_permute(sent, lambda x, z, c: (x, z, 1 - c))
    pair, done = kept_weight(nx, kept, grads, arrived)
    far = lax.all_gather(far, "col", axis=0)
    summed = lax.psum_scatter(pair, "x", scatter_dimension=0)

    grad_own, head, tail, taps = backward(
        col, near, far, before, own, feat_taps, inner_taps, done
    )
    taps = lax.psum(taps, "core")
    taps = taps + ctx_permute(taps, lambda x, z, c: (x ^ 1, z, c))
    taps_arrived = ctx_permute(taps, lambda x, z, c: (nx - 1 - x, z, c))

    pieces, taps, head = middle(nz, summed, taps, taps_arrived, head)
    pieces = lax.all_to_all(pieces, "zl", split_axis=0, concat_axis=0)
    head = ctx_shift(head, -1)
    grad_weight, grad_feat_taps, grad_inner_taps, grad_own = last(
        inv_root, z, taps, pieces, tail, head, grad_own
    )
    return jnp.transpose(grad_own, (1, 0, 2)), grad_weight, grad_feat_taps, grad_inner_taps


def fine_mesh(mesh):
    row, col, ctx = mesh.devices.shape
    return Mesh(mesh.devices.reshape(row, col, ctx // 8, 4, 2), ("row", "col", *CTX))


def solution(mesh):
    return jax.shard_map(
        body,
        mesh=fine_mesh(mesh),
        in_specs=(
            P(CTX, None, ("row", "col")),
            P(None, None, ("row", "col")),
            P(None, ("row", "col")),
            P("row", "col"),
            P(CTX, ("col", "row")),
        ),
        out_specs=(
            P(CTX, None, ("row", "col")),
            P(("row", *CTX), "col"),
            P(None, None, ("row", "col")),
            P(None, ("row", "col")),
        ),
        check_vma=False,
    )
```

```python
import math

import jax
import jax.numpy as jnp
from jax import lax
from jax.experimental import pallas as pl
from jax.experimental.pallas import tpu as pltpu
from jax.sharding import Mesh
from jax.sharding import PartitionSpec as P

TAPS = 7
HALO = 16
LEAD = 8
CHUNK = 64
LANES = 128
CTX = ("x", "zl", "core")
F32 = jnp.float32
BF16 = jnp.bfloat16
VMEM_BYTES = 24 << 20
STREAM_BYTES = 56 << 20


def spread(total):
    return [(start, min(CHUNK, total - start)) for start in range(0, total, CHUNK)]


def lane_spec(*lead):
    return pl.BlockSpec((*lead, LANES), lambda i: (0,) * len(lead) + (i,))


def whole(shape):
    return pl.BlockSpec(shape, lambda *_: (0,) * len(shape))


SCALAR = pl.BlockSpec(memory_space=pltpu.SMEM)
UNREAD = pl.BlockSpec(memory_space=pl.ANY)
IN_HBM = pl.BlockSpec(memory_space=pltpu.HBM)
IN_VMEM = pl.BlockSpec(memory_space=pltpu.VMEM)


def call(kernel, name, flops, moved, vmem=VMEM_BYTES, **kwargs):
    return pl.pallas_call(
        kernel,
        name=name,
        compiler_params=pltpu.CompilerParams(vmem_limit_bytes=vmem),
        cost_estimate=pl.CostEstimate(flops=flops, bytes_accessed=moved, transcendentals=0),
        **kwargs,
    )


def load_features(before, own, feats):
    rows = own.shape[1]
    for j in range(3):
        feats[j, 0:HALO, :] = before[j].astype(F32)
        for start, count in spread(rows):
            feats[j, HALO + start : HALO + start + count, :] = own[
                j, start : start + count, :
            ].astype(F32)


def mixed_parts(feats, feat_taps, start, count):
    base = HALO - LEAD + start
    parts = []
    for j in range(3):
        total = feat_taps[j, 0:1, :] * feats[j, base : base + count, :]
        for s in range(1, TAPS):
            total = total + feat_taps[j, s : s + 1, :] * feats[j, base - s : base - s + count, :]
        parts.append(total)
    return parts


def window_rows(product, inner_taps, start, count):
    base = LEAD + start
    total = inner_taps[0:1, :] * product[base : base + count, :]
    for s in range(1, TAPS):
        total = total + inner_taps[s : s + 1, :] * product[base - s : base - s + count, :]
    return total


def forward_kernel(before, own, feat_taps, inner_taps, gated, feats, query, product):
    rows = own.shape[1]
    load_features(before, own, feats)
    for start, count in spread(rows + LEAD):
        parts = mixed_parts(feats, feat_taps, start, count)
        query[start : start + count, :] = parts[0]
        product[start : start + count, :] = parts[1] * parts[2]
    for start, count in spread(rows):
        base = LEAD + start
        gated[start : start + count, :] = (
            query[base : base + count, :] * window_rows(product, inner_taps, start, count)
        ).astype(BF16)


def forward(before, own, feat_taps, inner_taps):
    _, rows, channels = own.shape
    return call(
        forward_kernel,
        "forward",
        60 * rows * channels,
        8 * rows * channels,
        grid=(channels // LANES,),
        in_specs=[lane_spec(3, HALO), lane_spec(3, rows), lane_spec(3, TAPS), lane_spec(TAPS)],
        out_specs=lane_spec(rows),
        out_shape=jax.ShapeDtypeStruct((rows, channels), BF16),
        scratch_shapes=[
            pltpu.VMEM((3, rows + HALO, LANES), F32),
            pltpu.VMEM((rows + LEAD, LANES), F32),
            pltpu.VMEM((rows + LEAD, LANES), F32),
        ],
    )(before, own, feat_taps, inner_taps)


def backward_kernel(
    col, near, far, before, own, feat_taps, inner_taps, _,
    grads, head, tail, tap_sums, feats, query, key, value, product, grad_window, grad_mixed,
):
    rows = own.shape[1]
    load_features(before, own, feats)
    for start, count in spread(rows + LEAD):
        parts = mixed_parts(feats, feat_taps, start, count)
        query[start : start + count, :] = parts[0]
        key[start : start + count, :] = parts[1]
        value[start : start + count, :] = parts[2]
        product[start : start + count, :] = parts[1] * parts[2]
    zeros = jnp.zeros((HALO, LANES), F32)
    grad_window[0:HALO, :] = zeros
    grad_window[HALO + rows :, :] = zeros[:LEAD]
    for j in range(3):
        grad_mixed[j, 0:HALO, :] = zeros
        grad_mixed[j, HALO + rows :, :] = zeros[:LEAD]
    for start, count in spread(rows):
        at = HALO + start
        total = near[start : start + count, :] + far[
            1 - col[0], start : start + count, :
        ].astype(F32)
        grad_window[at : at + count, :] = total * query[LEAD + start : LEAD + start + count, :]
        grad_mixed[0, at : at + count, :] = total * window_rows(product, inner_taps, start, count)
    for start, count in spread(rows + LEAD):
        at = HALO - LEAD + start
        total = inner_taps[0:1, :] * grad_window[at : at + count, :]
        for s in range(1, TAPS):
            total = total + inner_taps[s : s + 1, :] * grad_window[at + s : at + s + count, :]
        grad_mixed[1, at : at + count, :] = total * value[start : start + count, :]
        grad_mixed[2, at : at + count, :] = total * key[start : start + count, :]

    def folded(terms):
        return jnp.sum(terms.reshape(terms.shape[0] // 8, 8, LANES), axis=0)

    def put(place, sums):
        rows = [jnp.sum(total, axis=0, keepdims=True) for total in sums]
        tile = jnp.concatenate([*rows, jnp.zeros((1, LANES), F32)], axis=0)
        for copy in range(tap_sums.shape[0]):
            tap_sums[copy, place] = tile

    def transposed(j, at, count):
        total = feat_taps[j, 0:1, :] * grad_mixed[j, at : at + count, :]
        for s in range(1, TAPS):
            total = total + feat_taps[j, s : s + 1, :] * grad_mixed[j, at + s : at + s + count, :]
        return total

    for j in range(3):
        head[j] = transposed(j, 0, HALO)
        sums = [jnp.zeros((8, LANES), F32) for _ in range(TAPS)]
        spans = [(HALO + start, count) for start, count in spread(rows)]
        for at, count in ([(HALO - LEAD, LEAD)] if j > 0 else []) + spans:
            here = grad_mixed[j, at : at + count, :]
            for s in range(TAPS):
                sums[s] = sums[s] + folded(here * feats[j, at - s : at - s + count, :])
            if at >= HALO:
                total = transposed(j, at, count)
                grads[j, at - HALO : at - HALO + count, :] = total.astype(BF16)
                if at + count == HALO + rows:
                    tail[j] = total[count - HALO :]
        put(j, sums)
    sums = [jnp.zeros((8, LANES), F32) for _ in range(TAPS)]
    for start, count in spread(rows):
        here = grad_window[HALO + start : HALO + start + count, :]
        for s in range(TAPS):
            base = LEAD + start - s
            sums[s] = sums[s] + folded(here * product[base : base + count, :])
    put(3, sums)


def backward(copies, col, near, far, before, own, feat_taps, inner_taps, after):
    _, rows, channels = own.shape
    edge = jax.ShapeDtypeStruct((3, HALO, channels), F32)
    return call(
        backward_kernel,
        "backward",
        160 * rows * channels,
        20 * rows * channels,
        grid=(channels // LANES,),
        in_specs=[
            SCALAR, lane_spec(rows), lane_spec(2, rows), lane_spec(3, HALO), lane_spec(3, rows),
            lane_spec(3, TAPS), lane_spec(TAPS), UNREAD,
        ],
        out_specs=[
            lane_spec(3, rows), lane_spec(3, HALO), lane_spec(3, HALO), lane_spec(copies, 4, 8)
        ],
        out_shape=[
            jax.ShapeDtypeStruct((3, rows, channels), BF16),
            edge,
            edge,
            jax.ShapeDtypeStruct((copies, 4, 8, channels), F32),
        ],
        scratch_shapes=[pltpu.VMEM((3, rows + HALO, LANES), F32)]
        + [pltpu.VMEM((rows + LEAD, LANES), F32)] * 4
        + [
            pltpu.VMEM((rows + HALO + LEAD, LANES), F32),
            pltpu.VMEM((3, rows + HALO + LEAD, LANES), F32),
        ],
    )(col, near, far, before, own, feat_taps, inner_taps, after)


def fetch(source, target, sems):
    copies = [
        pltpu.make_async_copy(source.at[i], target.at[i], sems.at[i])
        for i in range(source.shape[0])
    ]
    for copy in copies:
        copy.start()
    return copies


def sent_weight_kernel(gated, grads, sent, done, held, sems):
    copies = fetch(grads, held, sems)
    done[...] = jnp.zeros_like(done)
    for b in range(held.shape[0]):
        copies[b].wait()
        sent[b] = jnp.dot(gated[...], held[b], preferred_element_type=F32).astype(BF16)


TOKEN = jax.ShapeDtypeStruct((8, LANES), F32)


def sent_weight(gated, grads):
    channels, rows = gated.shape
    blocks, _, width = grads.shape
    return call(
        sent_weight_kernel,
        "sent_weight",
        2 * rows * channels * blocks * width,
        2 * blocks * width * (rows + channels) + 2 * rows * channels,
        vmem=STREAM_BYTES,
        in_specs=[IN_VMEM, IN_HBM],
        out_specs=[IN_VMEM] * 2,
        out_shape=[jax.ShapeDtypeStruct((blocks, channels, width), BF16), TOKEN],
        scratch_shapes=[pltpu.VMEM(grads.shape, BF16), pltpu.SemaphoreType.DMA((blocks,))],
    )(gated, grads)


def gated_grad_kernel(
    col, grads, weight, _, far, near, held_grads, held_weight, grad_sems, weight_sems
):
    blocks, rows, width = held_grads.shape
    halves = held_weight.shape[0]
    per = blocks // halves
    span = per * width
    weights = [
        pltpu.make_async_copy(
            weight.at[:, part * span : (part + 1) * span], held_weight.at[part], weight_sems.at[part]
        )
        for part in range(halves)
    ]
    copies = [
        pltpu.make_async_copy(grads.at[b], held_grads.at[b], grad_sems.at[b])
        for b in range(blocks)
    ]
    for part in range(halves):
        weights[part].start()
        for b in range(part * per, (part + 1) * per):
            copies[b].start()
    half = near.shape[1]
    own = col[0]
    sums = [None, None]
    for part in range(halves):
        weights[part].wait()
        for b in range(part * per, (part + 1) * per):
            copies[b].wait()
        wide = jnp.concatenate(
            [held_grads[b] for b in range(part * per, (part + 1) * per)], axis=1
        )
        for at, which in enumerate((1 - own, own)):
            rows_of = pl.ds(pl.multiple_of(which * half, half), half)
            term = lax.dot_general(
                wide,
                held_weight[part, rows_of, :],
                (((1,), (1,)), ((), ())),
                preferred_element_type=F32,
            )
            sums[at] = term if part == 0 else sums[at] + term
    far[...] = sums[0].astype(BF16)
    near[...] = sums[1]


def gated_grad(col, grads, weight, after):
    blocks, rows, width = grads.shape
    channels = weight.shape[0]
    half = channels // 2
    parts = min(2, blocks)
    return call(
        gated_grad_kernel,
        "gated_grad",
        2 * rows * channels * blocks * width,
        2 * blocks * width * (rows + channels) + 6 * rows * half,
        vmem=STREAM_BYTES,
        in_specs=[SCALAR, IN_HBM, IN_HBM, UNREAD],
        out_specs=[IN_VMEM] * 2,
        out_shape=[
            jax.ShapeDtypeStruct((rows, half), BF16),
            jax.ShapeDtypeStruct((rows, half), F32),
        ],
        scratch_shapes=[
            pltpu.VMEM(grads.shape, BF16),
            pltpu.VMEM((parts, channels, blocks // parts * width), BF16),
            pltpu.SemaphoreType.DMA((blocks,)),
            pltpu.SemaphoreType.DMA((parts,)),
        ],
    )(col, grads, weight, after)


def kept_weight_kernel(gated, grads, arrived, out, done, held, sems):
    done[...] = jnp.zeros_like(done)
    blocks, parts, size, _ = held.shape
    copies = []
    for b in range(blocks):
        total = jnp.dot(gated[...], grads[b], preferred_element_type=F32)
        total = (total + arrived[b].astype(F32)).astype(BF16)
        for part in range(parts):
            held[b, part] = total[part * size : (part + 1) * size]
        copies.append(pltpu.make_async_copy(held.at[b], out.at[:, b], sems.at[b]))
        copies[-1].start()
    for copy in copies:
        copy.wait()


def kept_weight(parts, gated, grads, arrived):
    channels, rows = gated.shape
    blocks, _, width = grads.shape
    size = channels // parts
    return call(
        kept_weight_kernel,
        "kept_weight",
        2 * rows * channels * blocks * width,
        2 * blocks * width * (rows + 2 * channels) + 2 * rows * channels,
        in_specs=[IN_VMEM] * 3,
        out_specs=[IN_HBM, IN_VMEM],
        out_shape=[jax.ShapeDtypeStruct((parts, blocks, size, width), BF16), TOKEN],
        scratch_shapes=[
            pltpu.VMEM((blocks, parts, size, width), BF16),
            pltpu.SemaphoreType.DMA((blocks,)),
        ],
    )(gated, grads, arrived)


def two_roundings(sums):
    high = sums.astype(BF16).astype(F32)
    return jnp.concatenate([high, sums - high], axis=1).astype(BF16)


def rejoined(both):
    both = both.astype(F32)
    return both[:, :8] + both[:, 8:]


def first_half_kernel(z, pair, taps, head, out, kept, out_taps, out_head):
    blocks, rows, _ = pair.shape
    size = rows // 4
    total = taps[0]
    for copy in range(1, taps.shape[0]):
        total = total + taps[copy]
    out_taps[...] = total
    out_head[...] = head[...]
    low = lax.rem(z[0], 2)
    for high in range(2):
        own, other = (
            pl.ds(pl.multiple_of((2 * high + bit) * size, size), size) for bit in (low, 1 - low)
        )
        out[high * blocks : (high + 1) * blocks] = pair[:, other, :]
        kept[high] = pair[:, own, :].astype(F32)
    out[2 * blocks :] = two_roundings(total)


def second_half_kernel(z, kept, taps, arrived, out, out_kept, out_taps):
    _, blocks, _, _ = kept.shape
    total = taps[...] + rejoined(arrived[2 * blocks :])
    out_taps[...] = total
    high = lax.div(z[0], 2)
    own, other = (
        kept[bit] + arrived[pl.ds(bit * blocks, blocks)].astype(F32) for bit in (high, 1 - high)
    )
    out_kept[...] = own
    out[0:blocks] = other.astype(BF16)
    out[blocks:] = two_roundings(total)


def last_kernel(
    scale, kept, taps, arrived, tail, head, _, out, out_feat, out_inner, out_grads
):
    blocks, _, width = kept.shape
    out_grads[...] = (tail[...] + head[...]).astype(BF16)
    for b in range(blocks):
        total = kept[b] + arrived[b].astype(F32)
        out[:, b * width : (b + 1) * width] = (total * scale).astype(BF16)
    total = (taps[...] + rejoined(arrived[blocks:])) * scale
    out_feat[...] = total[:3, :TAPS]
    out_inner[...] = total[3, :TAPS]


def small_call(kernel, name, args, outs, scalars=0, **kwargs):
    moved = sum(v.size * v.dtype.itemsize for v in (*args, *outs))
    return call(
        kernel,
        name,
        moved,
        moved,
        grid=(1,),
        in_specs=[SCALAR] * scalars + [whole(v.shape) for v in args[scalars:]],
        out_specs=[whole(v.shape) for v in outs],
        out_shape=outs,
        **kwargs,
    )(*args)


def first_half(z, pair, taps, head):
    blocks, rows, width = pair.shape
    tile = (rows // 4, width)
    outs = [
        jax.ShapeDtypeStruct((2 * blocks + taps.shape[1], *tile), BF16),
        jax.ShapeDtypeStruct((2, blocks, *tile), F32),
        jax.ShapeDtypeStruct(taps.shape[1:], F32),
        jax.ShapeDtypeStruct(head.shape, F32),
    ]
    return small_call(first_half_kernel, "first_half", (z, pair, taps, head), outs, scalars=1)


def second_half(z, kept, taps, arrived):
    _, blocks, *tile = kept.shape
    outs = [
        jax.ShapeDtypeStruct((blocks + taps.shape[0], *tile), BF16),
        jax.ShapeDtypeStruct((blocks, *tile), F32),
        jax.ShapeDtypeStruct(taps.shape, F32),
    ]
    return small_call(second_half_kernel, "second_half", (z, kept, taps, arrived), outs, scalars=1)


def last(scale, kept, taps, arrived, tail, head, grads):
    blocks, channels, width = kept.shape
    final = grads.shape[1] // HALO - 1
    args = (kept, taps, arrived, tail, head)
    shapes = [
        jax.ShapeDtypeStruct((channels, blocks * width), BF16),
        jax.ShapeDtypeStruct((3, TAPS, width), F32),
        jax.ShapeDtypeStruct((TAPS, width), F32),
    ]
    return call(
        lambda *refs: last_kernel(scale, *refs),
        "last",
        2 * arrived.size,
        2 * arrived.size,
        grid=(1,),
        in_specs=[whole(v.shape) for v in args] + [UNREAD],
        out_specs=[whole(v.shape) for v in shapes]
        + [pl.BlockSpec(tail.shape, lambda i: (0, final, 0))],
        out_shape=shapes + [jax.ShapeDtypeStruct(grads.shape, grads.dtype)],
        input_output_aliases={5: 3},
    )(*args, grads)


def ctx_permute(value, target):
    nx, nz, nc = (lax.axis_size(a) for a in CTX)
    pairs = []
    for x in range(nx):
        for z in range(nz):
            for c in range(nc):
                to = target(x, z, c)
                pairs.append(((x * nz + z) * nc + c, (to[0] * nz + to[1]) * nc + to[2]))
    return lax.ppermute(value, CTX, pairs)


def ctx_shift(value, steps):
    count = math.prod(lax.axis_size(a) for a in CTX)
    return lax.ppermute(
        value, CTX, [(i, i + steps) for i in range(count) if 0 <= i + steps < count]
    )


def body(featured, feat_taps, inner_taps, out_weight, out_grad):
    rows = featured.shape[0]
    nx, nz, nc = (lax.axis_size(a) for a in CTX)
    inv_root = 1.0 / math.sqrt(rows * nx * nz * nc)
    core = lax.axis_index("core")
    col, z = (jnp.full((1,), lax.axis_index(a), jnp.int32) for a in ("col", "zl"))

    grads = lax.all_gather(out_grad, "row", axis=0)

    own = jnp.transpose(featured, (1, 0, 2))
    before = ctx_shift(own[:, rows - HALO :], 1)
    gated = forward(before, own, feat_taps, inner_taps)
    both = lax.all_gather(gated, "col", axis=1, tiled=True)
    channels = both.shape[1]
    split = both.T.reshape(nx * nz, nc, channels // (nx * nz * nc), rows)
    kept, sent = (
        lax.dynamic_index_in_dim(split, c, 1, keepdims=False).reshape(channels // nc, rows)
        for c in (core, 1 - core)
    )

    sent, done = sent_weight(sent, grads)
    arrived = ctx_permute(sent, lambda x, z, c: (x, z, 1 - c))
    far, near = gated_grad(col, grads, out_weight, done)
    pair, done = kept_weight(nx, kept, grads, arrived)
    far = lax.all_gather(far, "col", axis=0)
    summed = lax.psum_scatter(pair, "x", scatter_dimension=0)

    grad_own, head, tail, taps = backward(
        nx * nc, col, near, far, before, own, feat_taps, inner_taps, done
    )
    taps = lax.all_to_all(taps, ("x", "core"), split_axis=0, concat_axis=0)

    piece, part, taps, head = first_half(z, summed, taps, head)
    arrived = ctx_permute(piece, lambda x, z, c: (x, z ^ 1, c))
    head = ctx_shift(head, -1)
    piece, part, taps = second_half(z, part, taps, arrived)
    arrived = ctx_permute(piece, lambda x, z, c: (x, z ^ 2, c))
    grad_weight, grad_feat_taps, grad_inner_taps, grad_own = last(
        inv_root, part, taps, arrived, tail, head, grad_own
    )
    return jnp.transpose(grad_own, (1, 0, 2)), grad_weight, grad_feat_taps, grad_inner_taps


def fine_mesh(mesh):
    row, col, ctx = mesh.devices.shape
    return Mesh(mesh.devices.reshape(row, col, ctx // 8, 4, 2), ("row", "col", *CTX))


def solution(mesh):
    return jax.shard_map(
        body,
        mesh=fine_mesh(mesh),
        in_specs=(
            P(CTX, None, ("row", "col")),
            P(None, None, ("row", "col")),
            P(None, ("row", "col")),
            P("row", "col"),
            P(CTX, ("col", "row")),
        ),
        out_specs=(
            P(CTX, None, ("row", "col")),
            P(("row", *CTX), "col"),
            P(None, None, ("row", "col")),
            P(None, ("row", "col")),
        ),
        check_vma=False,
    )
```

```python
import math

import jax
import jax.numpy as jnp
from jax import lax
from jax.experimental import pallas as pl
from jax.experimental.pallas import tpu as pltpu
from jax.sharding import Mesh
from jax.sharding import PartitionSpec as P

TAPS = 7
HALO = 16
LEAD = 8
CHUNK = 64
LANES = 128
CTX = ("x", "zl", "core")
F32 = jnp.float32
BF16 = jnp.bfloat16
VMEM_BYTES = 24 << 20
BLOCKS = 8


def spread(total):
    return [(start, min(CHUNK, total - start)) for start in range(0, total, CHUNK)]


def lane_spec(*lead):
    return pl.BlockSpec((*lead, LANES), lambda i: (0,) * len(lead) + (i,))


def whole(shape):
    return pl.BlockSpec(shape, lambda *_: (0,) * len(shape))


SCALAR = pl.BlockSpec(memory_space=pltpu.SMEM)
UNREAD = pl.BlockSpec(memory_space=pl.ANY)
IN_HBM = pl.BlockSpec(memory_space=pltpu.HBM)
IN_VMEM = pl.BlockSpec(memory_space=pltpu.VMEM)


def call(kernel, name, flops, moved, vmem=VMEM_BYTES, **kwargs):
    return pl.pallas_call(
        kernel,
        name=name,
        compiler_params=pltpu.CompilerParams(vmem_limit_bytes=vmem),
        cost_estimate=pl.CostEstimate(flops=flops, bytes_accessed=moved, transcendentals=0),
        **kwargs,
    )


def load_features(before, own, feats):
    rows = own.shape[1]
    for j in range(3):
        feats[j, 0:HALO, :] = before[j].astype(F32)
        for start, count in spread(rows):
            feats[j, HALO + start : HALO + start + count, :] = own[
                j, start : start + count, :
            ].astype(F32)


def mixed_parts(feats, feat_taps, start, count):
    base = HALO - LEAD + start
    parts = []
    for j in range(3):
        total = feat_taps[j, 0:1, :] * feats[j, base : base + count, :]
        for s in range(1, TAPS):
            total = total + feat_taps[j, s : s + 1, :] * feats[j, base - s : base - s + count, :]
        parts.append(total)
    return parts


def window_rows(product, inner_taps, start, count):
    base = LEAD + start
    total = inner_taps[0:1, :] * product[base : base + count, :]
    for s in range(1, TAPS):
        total = total + inner_taps[s : s + 1, :] * product[base - s : base - s + count, :]
    return total


def forward_kernel(before, own, feat_taps, inner_taps, gated, feats, query, product):
    rows = own.shape[1]
    load_features(before, own, feats)
    for start, count in spread(rows + LEAD):
        parts = mixed_parts(feats, feat_taps, start, count)
        query[start : start + count, :] = parts[0]
        product[start : start + count, :] = parts[1] * parts[2]
    for start, count in spread(rows):
        base = LEAD + start
        gated[start : start + count, :] = (
            query[base : base + count, :] * window_rows(product, inner_taps, start, count)
        ).astype(BF16)


def forward(before, own, feat_taps, inner_taps):
    _, rows, channels = own.shape
    return call(
        forward_kernel,
        "forward",
        60 * rows * channels,
        8 * rows * channels,
        grid=(channels // LANES,),
        in_specs=[lane_spec(3, HALO), lane_spec(3, rows), lane_spec(3, TAPS), lane_spec(TAPS)],
        out_specs=lane_spec(rows),
        out_shape=jax.ShapeDtypeStruct((rows, channels), BF16),
        scratch_shapes=[
            pltpu.VMEM((3, rows + HALO, LANES), F32),
            pltpu.VMEM((rows + LEAD, LANES), F32),
            pltpu.VMEM((rows + LEAD, LANES), F32),
        ],
    )(before, own, feat_taps, inner_taps)


def backward_kernel(
    col, near, far, before, own, feat_taps, inner_taps, _,
    grads, head, tail, tap_sums, feats, query, key, value, product, grad_window, grad_mixed,
):
    rows = own.shape[1]
    load_features(before, own, feats)
    for start, count in spread(rows + LEAD):
        parts = mixed_parts(feats, feat_taps, start, count)
        query[start : start + count, :] = parts[0]
        key[start : start + count, :] = parts[1]
        value[start : start + count, :] = parts[2]
        product[start : start + count, :] = parts[1] * parts[2]
    zeros = jnp.zeros((HALO, LANES), F32)
    grad_window[0:HALO, :] = zeros
    grad_window[HALO + rows :, :] = zeros[:LEAD]
    for j in range(3):
        grad_mixed[j, 0:HALO, :] = zeros
        grad_mixed[j, HALO + rows :, :] = zeros[:LEAD]
    for start, count in spread(rows):
        at = HALO + start
        total = near[start : start + count, :] + far[
            1 - col[0], start : start + count, :
        ].astype(F32)
        grad_window[at : at + count, :] = total * query[LEAD + start : LEAD + start + count, :]
        grad_mixed[0, at : at + count, :] = total * window_rows(product, inner_taps, start, count)
    for start, count in spread(rows + LEAD):
        at = HALO - LEAD + start
        total = inner_taps[0:1, :] * grad_window[at : at + count, :]
        for s in range(1, TAPS):
            total = total + inner_taps[s : s + 1, :] * grad_window[at + s : at + s + count, :]
        grad_mixed[1, at : at + count, :] = total * value[start : start + count, :]
        grad_mixed[2, at : at + count, :] = total * key[start : start + count, :]

    def folded(terms):
        return jnp.sum(terms.reshape(terms.shape[0] // 8, 8, LANES), axis=0)

    def put(place, sums):
        rows = [jnp.sum(total, axis=0, keepdims=True) for total in sums]
        tile = jnp.concatenate([*rows, jnp.zeros((1, LANES), F32)], axis=0)
        for copy in range(tap_sums.shape[0]):
            tap_sums[copy, place] = tile

    def transposed(j, at, count):
        total = feat_taps[j, 0:1, :] * grad_mixed[j, at : at + count, :]
        for s in range(1, TAPS):
            total = total + feat_taps[j, s : s + 1, :] * grad_mixed[j, at + s : at + s + count, :]
        return total

    for j in range(3):
        head[j] = transposed(j, 0, HALO)
        sums = [jnp.zeros((8, LANES), F32) for _ in range(TAPS)]
        spans = [(HALO + start, count) for start, count in spread(rows)]
        for at, count in ([(HALO - LEAD, LEAD)] if j > 0 else []) + spans:
            here = grad_mixed[j, at : at + count, :]
            for s in range(TAPS):
                sums[s] = sums[s] + folded(here * feats[j, at - s : at - s + count, :])
            if at >= HALO:
                total = transposed(j, at, count)
                grads[j, at - HALO : at - HALO + count, :] = total.astype(BF16)
                if at + count == HALO + rows:
                    tail[j] = total[count - HALO :]
        put(j, sums)
    sums = [jnp.zeros((8, LANES), F32) for _ in range(TAPS)]
    for start, count in spread(rows):
        here = grad_window[HALO + start : HALO + start + count, :]
        for s in range(TAPS):
            base = LEAD + start - s
            sums[s] = sums[s] + folded(here * product[base : base + count, :])
    put(3, sums)


def backward(copies, col, near, far, before, own, feat_taps, inner_taps, after):
    _, rows, channels = own.shape
    edge = jax.ShapeDtypeStruct((3, HALO, channels), F32)
    return call(
        backward_kernel,
        "backward",
        160 * rows * channels,
        20 * rows * channels,
        grid=(channels // LANES,),
        in_specs=[
            SCALAR, lane_spec(rows), lane_spec(2, rows), lane_spec(3, HALO), lane_spec(3, rows),
            lane_spec(3, TAPS), lane_spec(TAPS), UNREAD,
        ],
        out_specs=[
            lane_spec(3, rows), lane_spec(3, HALO), lane_spec(3, HALO), lane_spec(copies, 4, 8)
        ],
        out_shape=[
            jax.ShapeDtypeStruct((3, rows, channels), BF16),
            edge,
            edge,
            jax.ShapeDtypeStruct((copies, 4, 8, channels), F32),
        ],
        scratch_shapes=[pltpu.VMEM((3, rows + HALO, LANES), F32)]
        + [pltpu.VMEM((rows + LEAD, LANES), F32)] * 4
        + [
            pltpu.VMEM((rows + HALO + LEAD, LANES), F32),
            pltpu.VMEM((3, rows + HALO + LEAD, LANES), F32),
        ],
    )(col, near, far, before, own, feat_taps, inner_taps, after)


TOKEN = jax.ShapeDtypeStruct((8, LANES), F32)


def blocks_of(refs):
    own, right, left, rights, lefts, low, high = refs
    return [
        [own], [right], [rights.at[0]], [rights.at[1]], [low, high], [lefts.at[1]], [lefts.at[0]],
        [left],
    ]


def times_block(gated, block):
    total, at = None, 0
    for ref in block:
        rows = ref.shape[0]
        term = jnp.dot(gated[:, at : at + rows], ref[...], preferred_element_type=F32)
        total = term if total is None else total + term
        at += rows
    return total


def sent_weight_kernel(gated, *refs):
    *grads, sent, done = refs
    done[...] = jnp.zeros_like(done)
    for b, block in enumerate(blocks_of(grads)):
        sent[b] = times_block(gated, block).astype(BF16)


def sent_weight(gated, grads):
    channels, rows = gated.shape
    blocks, width = BLOCKS, grads[0].shape[1]
    return call(
        sent_weight_kernel,
        "sent_weight",
        2 * rows * channels * blocks * width,
        2 * blocks * width * (rows + channels) + 2 * rows * channels,
        in_specs=[IN_VMEM] * (1 + len(grads)),
        out_specs=[IN_VMEM] * 2,
        out_shape=[jax.ShapeDtypeStruct((blocks, channels, width), BF16), TOKEN],
    )(gated, *grads)


def gated_grad_kernel(place, weight, *refs):
    *grads, _, far, near = refs
    blocks = blocks_of(grads)
    width = grads[0].shape[1]
    wide = jnp.concatenate(
        [
            jnp.concatenate([ref[...] for ref in block], axis=0) if len(block) > 1 else block[0][...]
            for block in blocks
        ],
        axis=1,
    )
    half = near.shape[1]
    row, own = place[0], place[1]
    for out, which in ((far, 1 - own), (near, own)):
        rows_of = pl.ds(pl.multiple_of(which * half, half), half)
        taken = []
        for b in range(len(blocks)):
            at = lax.rem(row + b, len(blocks)) * width
            taken.append(weight[rows_of, pl.ds(pl.multiple_of(at, width), width)])
        total = lax.dot_general(
            wide,
            jnp.concatenate(taken, axis=1),
            (((1,), (1,)), ((), ())),
            preferred_element_type=F32,
        )
        out[...] = total.astype(out.dtype)


def gated_grad(place, weight, grads, after):
    rows, width = grads[0].shape
    channels = weight.shape[0]
    half = channels // 2
    return call(
        gated_grad_kernel,
        "gated_grad",
        2 * rows * channels * BLOCKS * width,
        2 * BLOCKS * width * (rows + channels) + 6 * rows * half,
        in_specs=[SCALAR] + [IN_VMEM] * (1 + len(grads)) + [UNREAD],
        out_specs=[IN_VMEM] * 2,
        out_shape=[
            jax.ShapeDtypeStruct((rows, half), BF16),
            jax.ShapeDtypeStruct((rows, half), F32),
        ],
    )(place, weight, *grads, after)


def kept_weight_kernel(x, gated, *refs):
    *grads, arrived, own, right, middle, left, done, held = refs
    done[...] = jnp.zeros_like(done)
    size = own.shape[1]
    parts = held.shape[0] // size
    for b, block in enumerate(blocks_of(grads)):
        held[...] = times_block(gated, block) + arrived[b].astype(F32)
        for step, out in enumerate((own, right, middle, left)):
            at = lax.rem(x[0] + step, parts) * size
            out[b] = held[pl.ds(pl.multiple_of(at, size), size), :].astype(out.dtype)


def kept_weight(x, parts, gated, grads, arrived):
    channels, rows = gated.shape
    blocks, width = BLOCKS, grads[0].shape[1]
    shape = (blocks, channels // parts, width)
    return call(
        kept_weight_kernel,
        "kept_weight",
        2 * rows * channels * blocks * width,
        2 * blocks * width * (rows + 2 * channels) + 2 * rows * channels,
        in_specs=[SCALAR] + [IN_VMEM] * (2 + len(grads)),
        out_specs=[IN_VMEM] * (parts + 1),
        out_shape=[jax.ShapeDtypeStruct(shape, F32)]
        + [jax.ShapeDtypeStruct(shape, BF16)] * (parts - 1)
        + [TOKEN],
        scratch_shapes=[pltpu.VMEM((channels, width), F32)],
    )(x, gated, *grads, arrived)


def two_roundings(sums):
    high = sums.astype(BF16).astype(F32)
    return jnp.concatenate([high, sums - high], axis=1).astype(BF16)


def rejoined(both):
    both = both.astype(F32)
    return both[:, :8] + both[:, 8:]


def middle_kernel(z, own, *refs):
    *arrived, taps, head, out, kept, out_taps, out_head = refs
    parts, _, size, _ = out.shape
    blocks = own.shape[0]
    total = own[...]
    for piece in arrived:
        total = total + piece[...].astype(F32)
    sums = taps[0]
    for copy in range(1, taps.shape[0]):
        sums = sums + taps[copy]
    out_taps[...] = sums
    out_head[...] = head[...]
    both = two_roundings(sums)
    for part in range(parts):
        piece = total[:, part * size : (part + 1) * size, :]
        out[part, 0:blocks] = piece.astype(BF16)
        out[part, blocks:] = both

        @pl.when(z[0] == part)
        def _(piece=piece):
            kept[...] = piece


def last_kernel(
    scale, place, kept, taps, arrived, tail, head, _, out, out_feat, out_inner, out_grads
):
    parts = arrived.shape[0]
    blocks, _, width = kept.shape
    row, z = place[0], place[1]
    out_grads[...] = (tail[...] + head[...]).astype(BF16)
    for b in range(blocks):
        total = kept[b]
        for part in range(parts):
            total = total + jnp.where(z == part, 0.0, arrived[part, b].astype(F32))
        at = pl.multiple_of(lax.rem(row + b, blocks) * width, width)
        out[:, pl.ds(at, width)] = (total * scale).astype(BF16)
    total = taps[...]
    for part in range(parts):
        total = total + jnp.where(z == part, 0.0, rejoined(arrived[part, blocks:]))
    total = total * scale
    out_feat[...] = total[:3, :TAPS]
    out_inner[...] = total[3, :TAPS]


def middle(z, parts, own, arrived, taps, head):
    blocks, rows, width = own.shape
    tile = (rows // parts, width)
    args = (z, own, *arrived, taps, head)
    outs = [
        jax.ShapeDtypeStruct((parts, blocks + taps.shape[1], *tile), BF16),
        jax.ShapeDtypeStruct((blocks, *tile), F32),
        jax.ShapeDtypeStruct(taps.shape[1:], F32),
        jax.ShapeDtypeStruct(head.shape, F32),
    ]
    moved = 10 * own.size
    return call(
        middle_kernel,
        "middle",
        moved,
        moved,
        in_specs=[SCALAR] + [IN_VMEM] * (len(args) - 1),
        out_specs=[IN_VMEM] * len(outs),
        out_shape=outs,
    )(*args)


def last(scale, place, kept, taps, arrived, tail, head, grads):
    blocks, channels, width = kept.shape
    final = grads.shape[1] // HALO - 1
    args = (kept, taps, arrived, tail, head)
    shapes = [
        jax.ShapeDtypeStruct((channels, blocks * width), BF16),
        jax.ShapeDtypeStruct((3, TAPS, width), F32),
        jax.ShapeDtypeStruct((TAPS, width), F32),
    ]
    return call(
        lambda *refs: last_kernel(scale, *refs),
        "last",
        2 * arrived.size,
        2 * arrived.size,
        grid=(1,),
        in_specs=[SCALAR] + [whole(v.shape) for v in args] + [UNREAD],
        out_specs=[whole(v.shape) for v in shapes]
        + [pl.BlockSpec(tail.shape, lambda i: (0, final, 0))],
        out_shape=shapes + [jax.ShapeDtypeStruct(grads.shape, grads.dtype)],
        input_output_aliases={6: 3},
    )(place, *args, grads)


def ctx_permute(value, target):
    nx, nz, nc = (lax.axis_size(a) for a in CTX)
    pairs = []
    for x in range(nx):
        for z in range(nz):
            for c in range(nc):
                to = target(x, z, c)
                pairs.append(((x * nz + z) * nc + c, (to[0] * nz + to[1]) * nc + to[2]))
    return lax.ppermute(value, CTX, pairs)


def ctx_shift(value, steps):
    count = math.prod(lax.axis_size(a) for a in CTX)
    return lax.ppermute(
        value, CTX, [(i, i + steps) for i in range(count) if 0 <= i + steps < count]
    )


def turned(value, axis, steps):
    count = lax.axis_size(axis)
    return lax.ppermute(value, axis, [(i, (i + steps) % count) for i in range(count)])


def halves_kernel(rights, lefts, _, low, high):
    rows = low.shape[0]
    low[...] = rights[1, :rows, :]
    high[...] = lefts[1, rows:, :]


def halves(rights, lefts, after):
    _, rows, width = rights.shape
    half = jax.ShapeDtypeStruct((rows // 2, width), rights.dtype)
    return call(
        halves_kernel,
        "halves",
        rows * width,
        4 * rows * width,
        in_specs=[IN_VMEM] * 2 + [UNREAD],
        out_specs=[IN_VMEM] * 2,
        out_shape=[half] * 2,
    )(rights, lefts, after)


def two_steps(own):
    right, left = turned(own, "row", -1), turned(own, "row", 1)
    rights = turned(jnp.stack([own, right]), "row", -2)
    lefts = turned(jnp.stack([own, left]), "row", 2)
    return own, right, left, rights, lefts


def third_step(blocks, after):
    low, high = halves(*blocks[3:], after)
    return *blocks, turned(low, "row", -1), turned(high, "row", 1)


def body(featured, feat_taps, inner_taps, out_weight, out_grad):
    rows = featured.shape[0]
    nx, nz, nc = (lax.axis_size(a) for a in CTX)
    inv_root = 1.0 / math.sqrt(rows * nx * nz * nc)
    core = lax.axis_index("core")
    row, col, x, z = (
        jnp.full((1,), lax.axis_index(a), jnp.int32) for a in ("row", "col", "x", "zl")
    )

    grads = two_steps(out_grad)

    own = jnp.transpose(featured, (1, 0, 2))
    before = ctx_shift(own[:, rows - HALO :], 1)
    gated = forward(before, own, feat_taps, inner_taps)
    both = lax.all_gather(gated, "col", axis=1, tiled=True)
    grads = third_step(grads, both)
    channels = both.shape[1]
    split = both.T.reshape(nx * nz, nc, channels // (nx * nz * nc), rows)
    kept, sent = (
        lax.dynamic_index_in_dim(split, c, 1, keepdims=False).reshape(channels // nc, rows)
        for c in (core, 1 - core)
    )

    sent, done = sent_weight(sent, grads)
    arrived = ctx_permute(sent, lambda x, z, c: (x, z, 1 - c))
    own_x, *pieces, done = kept_weight(x, nx, kept, grads, arrived)
    arrived = [turned(piece, "x", step) for step, piece in enumerate(pieces, 1)]
    far, near = gated_grad(jnp.concatenate([row, col]), out_weight, grads, done)
    far = lax.all_gather(far, "col", axis=0)

    grad_own, head, tail, taps = backward(
        nx * nc, col, near, far, before, own, feat_taps, inner_taps, done
    )
    taps = lax.all_to_all(taps, ("x", "core"), split_axis=0, concat_axis=0)

    pieces, kept, taps, head = middle(z, nz, own_x, arrived, taps, head)
    pieces = lax.all_to_all(pieces, "zl", split_axis=0, concat_axis=0)
    head = ctx_shift(head, -1)
    grad_weight, grad_feat_taps, grad_inner_taps, grad_own = last(
        inv_root, jnp.concatenate([row, z]), kept, taps, pieces, tail, head, grad_own
    )
    return jnp.transpose(grad_own, (1, 0, 2)), grad_weight, grad_feat_taps, grad_inner_taps


def fine_mesh(mesh):
    row, col, ctx = mesh.devices.shape
    return Mesh(mesh.devices.reshape(row, col, ctx // 8, 4, 2), ("row", "col", *CTX))


def solution(mesh):
    return jax.shard_map(
        body,
        mesh=fine_mesh(mesh),
        in_specs=(
            P(CTX, None, ("row", "col")),
            P(None, None, ("row", "col")),
            P(None, ("row", "col")),
            P("row", "col"),
            P(CTX, ("col", "row")),
        ),
        out_specs=(
            P(CTX, None, ("row", "col")),
            P(("row", *CTX), "col"),
            P(None, None, ("row", "col")),
            P(None, ("row", "col")),
        ),
        check_vma=False,
    )
```

```python
import math

import jax
import jax.numpy as jnp
from jax import lax
from jax.experimental import pallas as pl
from jax.experimental.pallas import tpu as pltpu
from jax.sharding import Mesh
from jax.sharding import PartitionSpec as P

TAPS = 7
HALO = 16
LEAD = 8
CHUNK = 64
LANES = 128
CTX = ("x", "zl", "core")
F32 = jnp.float32
BF16 = jnp.bfloat16
VMEM_BYTES = 24 << 20


def spread(total):
    return [(start, min(CHUNK, total - start)) for start in range(0, total, CHUNK)]


def lane_spec(*lead):
    return pl.BlockSpec((*lead, LANES), lambda i: (0,) * len(lead) + (i,))


def whole(shape):
    return pl.BlockSpec(shape, lambda *_: (0,) * len(shape))


SCALAR = pl.BlockSpec(memory_space=pltpu.SMEM)
UNREAD = pl.BlockSpec(memory_space=pl.ANY)
IN_HBM = pl.BlockSpec(memory_space=pltpu.HBM)
IN_VMEM = pl.BlockSpec(memory_space=pltpu.VMEM)


def call(kernel, name, flops, moved, **kwargs):
    return pl.pallas_call(
        kernel,
        name=name,
        compiler_params=pltpu.CompilerParams(vmem_limit_bytes=VMEM_BYTES),
        cost_estimate=pl.CostEstimate(flops=flops, bytes_accessed=moved, transcendentals=0),
        **kwargs,
    )


def load_features(before, own, feats):
    rows = own.shape[1]
    for j in range(3):
        feats[j, 0:HALO, :] = before[j].astype(F32)
        for start, count in spread(rows):
            feats[j, HALO + start : HALO + start + count, :] = own[
                j, start : start + count, :
            ].astype(F32)


def mixed_parts(feats, feat_taps, start, count):
    base = HALO - LEAD + start
    parts = []
    for j in range(3):
        total = feat_taps[j, 0:1, :] * feats[j, base : base + count, :]
        for s in range(1, TAPS):
            total = total + feat_taps[j, s : s + 1, :] * feats[j, base - s : base - s + count, :]
        parts.append(total)
    return parts


def window_rows(product, inner_taps, start, count):
    base = LEAD + start
    total = inner_taps[0:1, :] * product[base : base + count, :]
    for s in range(1, TAPS):
        total = total + inner_taps[s : s + 1, :] * product[base - s : base - s + count, :]
    return total


def forward_kernel(before, own, feat_taps, inner_taps, gated, feats, query, product):
    rows = own.shape[1]
    load_features(before, own, feats)
    for start, count in spread(rows + LEAD):
        parts = mixed_parts(feats, feat_taps, start, count)
        query[start : start + count, :] = parts[0]
        product[start : start + count, :] = parts[1] * parts[2]
    for start, count in spread(rows):
        base = LEAD + start
        gated[start : start + count, :] = (
            query[base : base + count, :] * window_rows(product, inner_taps, start, count)
        ).astype(BF16)


def forward(before, own, feat_taps, inner_taps):
    _, rows, channels = own.shape
    return call(
        forward_kernel,
        "forward",
        60 * rows * channels,
        8 * rows * channels,
        grid=(channels // LANES,),
        in_specs=[lane_spec(3, HALO), lane_spec(3, rows), lane_spec(3, TAPS), lane_spec(TAPS)],
        out_specs=lane_spec(rows),
        out_shape=jax.ShapeDtypeStruct((rows, channels), BF16),
        scratch_shapes=[
            pltpu.VMEM((3, rows + HALO, LANES), F32),
            pltpu.VMEM((rows + LEAD, LANES), F32),
            pltpu.VMEM((rows + LEAD, LANES), F32),
        ],
    )(before, own, feat_taps, inner_taps)


def backward_kernel(
    col, near, far, before, own, feat_taps, inner_taps, _,
    grads, head, tail, tap_sums, feats, query, key, value, product, grad_window, grad_mixed,
):
    rows = own.shape[1]
    load_features(before, own, feats)
    for start, count in spread(rows + LEAD):
        parts = mixed_parts(feats, feat_taps, start, count)
        query[start : start + count, :] = parts[0]
        key[start : start + count, :] = parts[1]
        value[start : start + count, :] = parts[2]
        product[start : start + count, :] = parts[1] * parts[2]
    zeros = jnp.zeros((HALO, LANES), F32)
    grad_window[0:HALO, :] = zeros
    grad_window[HALO + rows :, :] = zeros[:LEAD]
    for j in range(3):
        grad_mixed[j, 0:HALO, :] = zeros
        grad_mixed[j, HALO + rows :, :] = zeros[:LEAD]
    for start, count in spread(rows):
        at = HALO + start
        total = near[start : start + count, :] + far[
            1 - col[0], start : start + count, :
        ].astype(F32)
        grad_window[at : at + count, :] = total * query[LEAD + start : LEAD + start + count, :]
        grad_mixed[0, at : at + count, :] = total * window_rows(product, inner_taps, start, count)
    for start, count in spread(rows + LEAD):
        at = HALO - LEAD + start
        total = inner_taps[0:1, :] * grad_window[at : at + count, :]
        for s in range(1, TAPS):
            total = total + inner_taps[s : s + 1, :] * grad_window[at + s : at + s + count, :]
        grad_mixed[1, at : at + count, :] = total * value[start : start + count, :]
        grad_mixed[2, at : at + count, :] = total * key[start : start + count, :]

    def folded(terms):
        return jnp.sum(terms.reshape(terms.shape[0] // 8, 8, LANES), axis=0)

    def put(place, sums):
        rows = [jnp.sum(total, axis=0, keepdims=True) for total in sums]
        tile = jnp.concatenate([*rows, jnp.zeros((1, LANES), F32)], axis=0)
        for copy in range(tap_sums.shape[0]):
            tap_sums[copy, place] = tile

    def transposed(j, at, count):
        total = feat_taps[j, 0:1, :] * grad_mixed[j, at : at + count, :]
        for s in range(1, TAPS):
            total = total + feat_taps[j, s : s + 1, :] * grad_mixed[j, at + s : at + s + count, :]
        return total

    for j in range(3):
        head[j] = transposed(j, 0, HALO)
        sums = [jnp.zeros((8, LANES), F32) for _ in range(TAPS)]
        spans = [(HALO + start, count) for start, count in spread(rows)]
        for at, count in ([(HALO - LEAD, LEAD)] if j > 0 else []) + spans:
            here = grad_mixed[j, at : at + count, :]
            for s in range(TAPS):
                sums[s] = sums[s] + folded(here * feats[j, at - s : at - s + count, :])
            if at >= HALO:
                total = transposed(j, at, count)
                grads[j, at - HALO : at - HALO + count, :] = total.astype(BF16)
                if at + count == HALO + rows:
                    tail[j] = total[count - HALO :]
        put(j, sums)
    sums = [jnp.zeros((8, LANES), F32) for _ in range(TAPS)]
    for start, count in spread(rows):
        here = grad_window[HALO + start : HALO + start + count, :]
        for s in range(TAPS):
            base = LEAD + start - s
            sums[s] = sums[s] + folded(here * product[base : base + count, :])
    put(3, sums)


def backward(copies, col, near, far, before, own, feat_taps, inner_taps, after):
    _, rows, channels = own.shape
    edge = jax.ShapeDtypeStruct((3, HALO, channels), F32)
    return call(
        backward_kernel,
        "backward",
        160 * rows * channels,
        20 * rows * channels,
        grid=(channels // LANES,),
        in_specs=[
            SCALAR, lane_spec(rows), lane_spec(2, rows), lane_spec(3, HALO), lane_spec(3, rows),
            lane_spec(3, TAPS), lane_spec(TAPS), UNREAD,
        ],
        out_specs=[
            lane_spec(3, rows), lane_spec(3, HALO), lane_spec(3, HALO), lane_spec(copies, 4, 8)
        ],
        out_shape=[
            jax.ShapeDtypeStruct((3, rows, channels), BF16),
            edge,
            edge,
            jax.ShapeDtypeStruct((copies, 4, 8, channels), F32),
        ],
        scratch_shapes=[pltpu.VMEM((3, rows + HALO, LANES), F32)]
        + [pltpu.VMEM((rows + LEAD, LANES), F32)] * 4
        + [
            pltpu.VMEM((rows + HALO + LEAD, LANES), F32),
            pltpu.VMEM((3, rows + HALO + LEAD, LANES), F32),
        ],
    )(col, near, far, before, own, feat_taps, inner_taps, after)


TOKEN = jax.ShapeDtypeStruct((8, LANES), F32)


def sent_weight_kernel(gated, grads, sent, done):
    done[...] = jnp.zeros_like(done)
    for b in range(grads.shape[0]):
        sent[b] = jnp.dot(gated[...], grads[b], preferred_element_type=F32).astype(BF16)


def sent_weight(gated, grads):
    channels, rows = gated.shape
    blocks, _, width = grads.shape
    return call(
        sent_weight_kernel,
        "sent_weight",
        2 * rows * channels * blocks * width,
        2 * blocks * width * (rows + channels) + 2 * rows * channels,
        in_specs=[IN_VMEM] * 2,
        out_specs=[IN_VMEM] * 2,
        out_shape=[jax.ShapeDtypeStruct((blocks, channels, width), BF16), TOKEN],
    )(gated, grads)


def gated_grad_kernel(col, grads, weight, _, far, near):
    half = near.shape[1]
    wide = jnp.concatenate([grads[b] for b in range(grads.shape[0])], axis=1)
    for out, which in ((far, 1 - col[0]), (near, col[0])):
        total = lax.dot_general(
            wide,
            weight[pl.ds(pl.multiple_of(which * half, half), half), :],
            (((1,), (1,)), ((), ())),
            preferred_element_type=F32,
        )
        out[...] = total.astype(out.dtype)


def gated_grad(col, grads, weight, after):
    blocks, rows, width = grads.shape
    channels = weight.shape[0]
    half = channels // 2
    return call(
        gated_grad_kernel,
        "gated_grad",
        2 * rows * channels * blocks * width,
        2 * blocks * width * (rows + channels) + 6 * rows * half,
        in_specs=[SCALAR, IN_VMEM, IN_VMEM, UNREAD],
        out_specs=[IN_VMEM] * 2,
        out_shape=[
            jax.ShapeDtypeStruct((rows, half), BF16),
            jax.ShapeDtypeStruct((rows, half), F32),
        ],
    )(col, grads, weight, after)


def kept_weight_kernel(gated, grads, arrived, out, done, held, sems):
    done[...] = jnp.zeros_like(done)
    blocks, parts, size, _ = held.shape
    copies = []
    for b in range(blocks):
        total = jnp.dot(gated[...], grads[b], preferred_element_type=F32)
        total = (total + arrived[b].astype(F32)).astype(BF16)
        for part in range(parts):
            held[b, part] = total[part * size : (part + 1) * size]
        copies.append(pltpu.make_async_copy(held.at[b], out.at[:, b], sems.at[b]))
        copies[-1].start()
    for copy in copies:
        copy.wait()


def kept_weight(parts, gated, grads, arrived):
    channels, rows = gated.shape
    blocks, _, width = grads.shape
    size = channels // parts
    return call(
        kept_weight_kernel,
        "kept_weight",
        2 * rows * channels * blocks * width,
        2 * blocks * width * (rows + 2 * channels) + 2 * rows * channels,
        in_specs=[IN_VMEM] * 3,
        out_specs=[IN_HBM, IN_VMEM],
        out_shape=[jax.ShapeDtypeStruct((parts, blocks, size, width), BF16), TOKEN],
        scratch_shapes=[
            pltpu.VMEM((blocks, parts, size, width), BF16),
            pltpu.SemaphoreType.DMA((blocks,)),
        ],
    )(gated, grads, arrived)


def two_roundings(sums):
    high = sums.astype(BF16).astype(F32)
    return jnp.concatenate([high, sums - high], axis=1).astype(BF16)


def rejoined(both):
    both = both.astype(F32)
    return both[:, :8] + both[:, 8:]


def middle_kernel(pair, taps, head, out, out_taps, out_head):
    parts, _, size, _ = out.shape
    blocks = pair.shape[0]
    sums = taps[0]
    for copy in range(1, taps.shape[0]):
        sums = sums + taps[copy]
    out_taps[...] = sums
    out_head[...] = head[...]
    both = two_roundings(sums)
    for part in range(parts):
        out[part, 0:blocks] = pair[:, part * size : (part + 1) * size, :]
        out[part, blocks:] = both


def middle(parts, pair, taps, head):
    blocks, channels, width = pair.shape
    shape = (parts, blocks + taps.shape[1], channels // parts, width)
    outs = [
        jax.ShapeDtypeStruct(shape, BF16),
        jax.ShapeDtypeStruct(taps.shape[1:], F32),
        jax.ShapeDtypeStruct(head.shape, F32),
    ]
    return call(
        middle_kernel,
        "middle",
        4 * pair.size,
        4 * pair.size,
        in_specs=[IN_VMEM] * 3,
        out_specs=[IN_VMEM] * 3,
        out_shape=outs,
    )(pair, taps, head)


def last_kernel(
    scale, z, taps, arrived, tail, head, _, out, out_feat, out_inner, out_grads
):
    parts, _, _, width = arrived.shape
    blocks = out.shape[1] // width
    out_grads[...] = (tail[...] + head[...]).astype(BF16)
    for b in range(blocks):
        total = arrived[0, b].astype(F32)
        for part in range(1, parts):
            total = total + arrived[part, b].astype(F32)
        out[:, b * width : (b + 1) * width] = (total * scale).astype(BF16)
    total = taps[...]
    for part in range(parts):
        total = total + jnp.where(z[0] == part, 0.0, rejoined(arrived[part, blocks:]))
    total = total * scale
    out_feat[...] = total[:3, :TAPS]
    out_inner[...] = total[3, :TAPS]


def last(scale, z, taps, arrived, tail, head, grads):
    parts, count, channels, width = arrived.shape
    blocks = count - taps.shape[0]
    final = grads.shape[1] // HALO - 1
    args = (taps, arrived, tail, head)
    shapes = [
        jax.ShapeDtypeStruct((channels, blocks * width), BF16),
        jax.ShapeDtypeStruct((3, TAPS, width), F32),
        jax.ShapeDtypeStruct((TAPS, width), F32),
    ]
    return call(
        lambda *refs: last_kernel(scale, *refs),
        "last",
        2 * arrived.size,
        2 * arrived.size,
        grid=(1,),
        in_specs=[SCALAR] + [whole(v.shape) for v in args] + [UNREAD],
        out_specs=[whole(v.shape) for v in shapes]
        + [pl.BlockSpec(tail.shape, lambda i: (0, final, 0))],
        out_shape=shapes + [jax.ShapeDtypeStruct(grads.shape, grads.dtype)],
        input_output_aliases={5: 3},
    )(z, *args, grads)


def ctx_permute(value, target):
    nx, nz, nc = (lax.axis_size(a) for a in CTX)
    pairs = []
    for x in range(nx):
        for z in range(nz):
            for c in range(nc):
                to = target(x, z, c)
                pairs.append(((x * nz + z) * nc + c, (to[0] * nz + to[1]) * nc + to[2]))
    return lax.ppermute(value, CTX, pairs)


def ctx_shift(value, steps):
    count = math.prod(lax.axis_size(a) for a in CTX)
    return lax.ppermute(
        value, CTX, [(i, i + steps) for i in range(count) if 0 <= i + steps < count]
    )


def body(featured, feat_taps, inner_taps, out_weight, out_grad):
    rows = featured.shape[0]
    nx, nz, nc = (lax.axis_size(a) for a in CTX)
    inv_root = 1.0 / math.sqrt(rows * nx * nz * nc)
    core = lax.axis_index("core")
    col, z = (jnp.full((1,), lax.axis_index(a), jnp.int32) for a in ("col", "zl"))

    grads = lax.all_gather(out_grad, "row", axis=0)

    own = jnp.transpose(featured, (1, 0, 2))
    before = ctx_shift(own[:, rows - HALO :], 1)
    gated = forward(before, own, feat_taps, inner_taps)
    both = lax.all_gather(gated, "col", axis=1, tiled=True)
    channels = both.shape[1]
    split = both.T.reshape(nx * nz, nc, channels // (nx * nz * nc), rows)
    kept, sent = (
        lax.dynamic_index_in_dim(split, c, 1, keepdims=False).reshape(channels // nc, rows)
        for c in (core, 1 - core)
    )

    sent, done = sent_weight(sent, grads)
    arrived = ctx_permute(sent, lambda x, z, c: (x, z, 1 - c))
    far, near = gated_grad(col, grads, out_weight, done)
    pair, done = kept_weight(nx, kept, grads, arrived)
    far = lax.all_gather(far, "col", axis=0)
    summed = lax.psum_scatter(pair, "x", scatter_dimension=0)

    grad_own, head, tail, taps = backward(
        nx * nc, col, near, far, before, own, feat_taps, inner_taps, done
    )
    taps = lax.all_to_all(taps, ("x", "core"), split_axis=0, concat_axis=0)

    pieces, taps, head = middle(nz, summed, taps, head)
    pieces = lax.all_to_all(pieces, "zl", split_axis=0, concat_axis=0)
    head = ctx_shift(head, -1)
    grad_weight, grad_feat_taps, grad_inner_taps, grad_own = last(
        inv_root, z, taps, pieces, tail, head, grad_own
    )
    return jnp.transpose(grad_own, (1, 0, 2)), grad_weight, grad_feat_taps, grad_inner_taps


def fine_mesh(mesh):
    row, col, ctx = mesh.devices.shape
    return Mesh(mesh.devices.reshape(row, col, ctx // 8, 4, 2), ("row", "col", *CTX))


def solution(mesh):
    return jax.shard_map(
        body,
        mesh=fine_mesh(mesh),
        in_specs=(
            P(CTX, None, ("row", "col")),
            P(None, None, ("row", "col")),
            P(None, ("row", "col")),
            P("row", "col"),
            P(CTX, ("col", "row")),
        ),
        out_specs=(
            P(CTX, None, ("row", "col")),
            P(("row", *CTX), "col"),
            P(None, None, ("row", "col")),
            P(None, ("row", "col")),
        ),
        check_vma=False,
    )
```

```python
import math

import jax
import jax.numpy as jnp
from jax import lax
from jax.experimental import pallas as pl
from jax.experimental.pallas import tpu as pltpu
from jax.sharding import Mesh
from jax.sharding import PartitionSpec as P

TAPS = 7
HALO = 16
LEAD = 8
CHUNK = 64
LANES = 128
CTX = ("x", "zl", "core")
F32 = jnp.float32
BF16 = jnp.bfloat16
VMEM_BYTES = 24 << 20


def spread(total):
    return [(start, min(CHUNK, total - start)) for start in range(0, total, CHUNK)]


def lane_spec(*lead):
    return pl.BlockSpec((*lead, LANES), lambda i: (0,) * len(lead) + (i,))


def whole(shape):
    return pl.BlockSpec(shape, lambda *_: (0,) * len(shape))


SCALAR = pl.BlockSpec(memory_space=pltpu.SMEM)
UNREAD = pl.BlockSpec(memory_space=pl.ANY)
IN_HBM = pl.BlockSpec(memory_space=pltpu.HBM)
IN_VMEM = pl.BlockSpec(memory_space=pltpu.VMEM)


def call(kernel, name, flops, moved, **kwargs):
    return pl.pallas_call(
        kernel,
        name=name,
        compiler_params=pltpu.CompilerParams(vmem_limit_bytes=VMEM_BYTES),
        cost_estimate=pl.CostEstimate(flops=flops, bytes_accessed=moved, transcendentals=0),
        **kwargs,
    )


def load_features(before, own, feats, after=None):
    rows = own.shape[1]
    for j in range(3):
        feats[j, 0:HALO, :] = before[j].astype(F32)
        if after is not None:
            feats[j, HALO + rows :, :] = after[j].astype(F32)
        for start, count in spread(rows):
            feats[j, HALO + start : HALO + start + count, :] = own[
                j, start : start + count, :
            ].astype(F32)


def mixed_parts(feats, feat_taps, start, count):
    base = HALO - LEAD + start
    parts = []
    for j in range(3):
        total = feat_taps[j, 0:1, :] * feats[j, base : base + count, :]
        for s in range(1, TAPS):
            total = total + feat_taps[j, s : s + 1, :] * feats[j, base - s : base - s + count, :]
        parts.append(total)
    return parts


def window_rows(product, inner_taps, start, count):
    base = LEAD + start
    total = inner_taps[0:1, :] * product[base : base + count, :]
    for s in range(1, TAPS):
        total = total + inner_taps[s : s + 1, :] * product[base - s : base - s + count, :]
    return total


def forward_kernel(before, own, feat_taps, inner_taps, gated, feats, query, product):
    rows = own.shape[1]
    load_features(before, own, feats)
    for start, count in spread(rows + LEAD):
        parts = mixed_parts(feats, feat_taps, start, count)
        query[start : start + count, :] = parts[0]
        product[start : start + count, :] = parts[1] * parts[2]
    for start, count in spread(rows):
        base = LEAD + start
        gated[start : start + count, :] = (
            query[base : base + count, :] * window_rows(product, inner_taps, start, count)
        ).astype(BF16)


def forward(before, own, feat_taps, inner_taps):
    _, rows, channels = own.shape
    return call(
        forward_kernel,
        "forward",
        60 * rows * channels,
        8 * rows * channels,
        grid=(channels // LANES,),
        in_specs=[lane_spec(3, HALO), lane_spec(3, rows), lane_spec(3, TAPS), lane_spec(TAPS)],
        out_specs=lane_spec(rows),
        out_shape=jax.ShapeDtypeStruct((rows, channels), BF16),
        scratch_shapes=[
            pltpu.VMEM((3, rows + HALO, LANES), F32),
            pltpu.VMEM((rows + LEAD, LANES), F32),
            pltpu.VMEM((rows + LEAD, LANES), F32),
        ],
    )(before, own, feat_taps, inner_taps)


def backward_kernel(
    col, near, far, before, own, after, feat_taps, inner_taps, _,
    grads, tap_sums, feats, query, key, value, product, grad_window, grad_mixed,
):
    rows = own.shape[1]
    load_features(before, own, feats, after)
    for start, count in spread(rows + HALO + LEAD):
        parts = mixed_parts(feats, feat_taps, start, count)
        query[start : start + count, :] = parts[0]
        key[start : start + count, :] = parts[1]
        value[start : start + count, :] = parts[2]
        product[start : start + count, :] = parts[1] * parts[2]
    for start, count in spread(rows + HALO):
        total = near[start : start + count, :] + far[
            1 - col[0], start : start + count, :
        ].astype(F32)
        grad_window[start : start + count, :] = (
            total * query[LEAD + start : LEAD + start + count, :]
        )
        grad_mixed[0, start : start + count, :] = total * window_rows(
            product, inner_taps, start, count
        )
    for start, count in spread(rows + LEAD):
        total = inner_taps[0:1, :] * grad_window[start : start + count, :]
        for s in range(1, TAPS):
            total = total + inner_taps[s : s + 1, :] * grad_window[start + s : start + s + count, :]
        grad_mixed[1, start : start + count, :] = (
            total * value[LEAD + start : LEAD + start + count, :]
        )
        grad_mixed[2, start : start + count, :] = total * key[LEAD + start : LEAD + start + count, :]

    def folded(terms):
        return jnp.sum(terms.reshape(terms.shape[0] // 8, 8, LANES), axis=0)

    def put(place, sums):
        tile = [jnp.sum(total, axis=0, keepdims=True) for total in sums]
        tile = jnp.concatenate([*tile, jnp.zeros((1, LANES), F32)], axis=0)
        for copy in range(tap_sums.shape[0]):
            tap_sums[copy, place] = tile

    for j in range(3):
        sums = [jnp.zeros((8, LANES), F32) for _ in range(TAPS)]
        for start, count in spread(rows):
            here = grad_mixed[j, start : start + count, :]
            total = feat_taps[j, 0:1, :] * here
            for s in range(1, TAPS):
                total = (
                    total
                    + feat_taps[j, s : s + 1, :] * grad_mixed[j, start + s : start + s + count, :]
                )
            grads[j, start : start + count, :] = total.astype(BF16)
            for s in range(TAPS):
                base = HALO + start - s
                sums[s] = sums[s] + folded(here * feats[j, base : base + count, :])
        put(j, sums)
    sums = [jnp.zeros((8, LANES), F32) for _ in range(TAPS)]
    for start, count in spread(rows):
        here = grad_window[start : start + count, :]
        for s in range(TAPS):
            base = LEAD + start - s
            sums[s] = sums[s] + folded(here * product[base : base + count, :])
    put(3, sums)


def backward(copies, col, near, far, before, own, after, feat_taps, inner_taps, later):
    _, rows, channels = own.shape
    return call(
        backward_kernel,
        "backward",
        160 * rows * channels,
        20 * rows * channels,
        grid=(channels // LANES,),
        in_specs=[
            SCALAR, lane_spec(rows + HALO), lane_spec(2, rows + HALO), lane_spec(3, HALO),
            lane_spec(3, rows), lane_spec(3, HALO), lane_spec(3, TAPS), lane_spec(TAPS), UNREAD,
        ],
        out_specs=[lane_spec(3, rows), lane_spec(copies, 4, 8)],
        out_shape=[
            jax.ShapeDtypeStruct((3, rows, channels), BF16),
            jax.ShapeDtypeStruct((copies, 4, 8, channels), F32),
        ],
        scratch_shapes=[pltpu.VMEM((3, rows + 2 * HALO, LANES), F32)]
        + [pltpu.VMEM((rows + HALO + LEAD, LANES), F32)] * 4
        + [
            pltpu.VMEM((rows + HALO, LANES), F32),
            pltpu.VMEM((3, rows + HALO, LANES), F32),
        ],
    )(col, near, far, before, own, after, feat_taps, inner_taps, later)


TOKEN = jax.ShapeDtypeStruct((8, LANES), F32)


def sent_weight_kernel(gated, grads, _, sent, done):
    done[...] = jnp.zeros_like(done)
    for b in range(grads.shape[0]):
        sent[b] = jnp.dot(gated[...], grads[b], preferred_element_type=F32).astype(BF16)


def sent_weight(gated, grads, later):
    channels, rows = gated.shape
    blocks, _, width = grads.shape
    return call(
        sent_weight_kernel,
        "sent_weight",
        2 * rows * channels * blocks * width,
        2 * blocks * width * (rows + channels) + 2 * rows * channels,
        in_specs=[IN_VMEM] * 2 + [UNREAD],
        out_specs=[IN_VMEM] * 2,
        out_shape=[jax.ShapeDtypeStruct((blocks, channels, width), BF16), TOKEN],
    )(gated, grads, later)


def gated_grad_kernel(col, grads, halo, weight, _, far, near):
    half = near.shape[1]
    blocks = range(grads.shape[0])
    wide = jnp.concatenate(
        [
            jnp.concatenate([grads[b] for b in blocks], axis=1),
            jnp.concatenate([halo[b] for b in blocks], axis=1),
        ],
        axis=0,
    )
    for out, which in ((far, 1 - col[0]), (near, col[0])):
        total = lax.dot_general(
            wide,
            weight[pl.ds(pl.multiple_of(which * half, half), half), :],
            (((1,), (1,)), ((), ())),
            preferred_element_type=F32,
        )
        out[...] = total.astype(out.dtype)


def gated_grad(col, grads, halo, weight, later):
    blocks, rows, width = grads.shape
    rows = rows + halo.shape[1]
    channels = weight.shape[0]
    half = channels // 2
    return call(
        gated_grad_kernel,
        "gated_grad",
        2 * rows * channels * blocks * width,
        2 * blocks * width * (rows + channels) + 6 * rows * half,
        in_specs=[SCALAR, IN_VMEM, IN_VMEM, IN_VMEM, UNREAD],
        out_specs=[IN_VMEM] * 2,
        out_shape=[
            jax.ShapeDtypeStruct((rows, half), BF16),
            jax.ShapeDtypeStruct((rows, half), F32),
        ],
    )(col, grads, halo, weight, later)


def kept_weight_kernel(gated, grads, arrived, out, done, held, sems):
    done[...] = jnp.zeros_like(done)
    blocks, parts, size, _ = held.shape
    copies = []
    for b in range(blocks):
        total = jnp.dot(gated[...], grads[b], preferred_element_type=F32)
        total = (total + arrived[b].astype(F32)).astype(BF16)
        for part in range(parts):
            held[b, part] = total[part * size : (part + 1) * size]
        copies.append(pltpu.make_async_copy(held.at[b], out.at[:, b], sems.at[b]))
        copies[-1].start()
    for copy in copies:
        copy.wait()


def kept_weight(parts, gated, grads, arrived):
    channels, rows = gated.shape
    blocks, _, width = grads.shape
    size = channels // parts
    return call(
        kept_weight_kernel,
        "kept_weight",
        2 * rows * channels * blocks * width,
        2 * blocks * width * (rows + 2 * channels) + 2 * rows * channels,
        in_specs=[IN_VMEM] * 3,
        out_specs=[IN_HBM, IN_VMEM],
        out_shape=[jax.ShapeDtypeStruct((parts, blocks, size, width), BF16), TOKEN],
        scratch_shapes=[
            pltpu.VMEM((blocks, parts, size, width), BF16),
            pltpu.SemaphoreType.DMA((blocks,)),
        ],
    )(gated, grads, arrived)


def two_roundings(sums):
    high = sums.astype(BF16).astype(F32)
    return jnp.concatenate([high, sums - high], axis=1).astype(BF16)


def rejoined(both):
    both = both.astype(F32)
    return both[:, :8] + both[:, 8:]


def middle_kernel(pair, taps, out, out_taps):
    parts, _, size, _ = out.shape
    blocks = pair.shape[0]
    sums = taps[0]
    for copy in range(1, taps.shape[0]):
        sums = sums + taps[copy]
    out_taps[...] = sums
    both = two_roundings(sums)
    for part in range(parts):
        out[part, 0:blocks] = pair[:, part * size : (part + 1) * size, :]
        out[part, blocks:] = both


def middle(parts, pair, taps):
    blocks, channels, width = pair.shape
    shape = (parts, blocks + taps.shape[1], channels // parts, width)
    return call(
        middle_kernel,
        "middle",
        4 * pair.size,
        4 * pair.size,
        in_specs=[IN_VMEM] * 2,
        out_specs=[IN_VMEM] * 2,
        out_shape=[
            jax.ShapeDtypeStruct(shape, BF16),
            jax.ShapeDtypeStruct(taps.shape[1:], F32),
        ],
    )(pair, taps)


def last_kernel(scale, z, taps, arrived, out, out_feat, out_inner):
    parts, _, _, width = arrived.shape
    blocks = out.shape[1] // width
    for b in range(blocks):
        total = arrived[0, b].astype(F32)
        for part in range(1, parts):
            total = total + arrived[part, b].astype(F32)
        out[:, b * width : (b + 1) * width] = (total * scale).astype(BF16)
    total = taps[...]
    for part in range(parts):
        total = total + jnp.where(z[0] == part, 0.0, rejoined(arrived[part, blocks:]))
    total = total * scale
    out_feat[...] = total[:3, :TAPS]
    out_inner[...] = total[3, :TAPS]


def last(scale, z, taps, arrived):
    parts, count, channels, width = arrived.shape
    blocks = count - taps.shape[0]
    return call(
        lambda *refs: last_kernel(scale, *refs),
        "last",
        2 * arrived.size,
        2 * arrived.size,
        in_specs=[SCALAR] + [IN_VMEM] * 2,
        out_specs=[IN_VMEM] * 3,
        out_shape=[
            jax.ShapeDtypeStruct((channels, blocks * width), BF16),
            jax.ShapeDtypeStruct((3, TAPS, width), F32),
            jax.ShapeDtypeStruct((TAPS, width), F32),
        ],
    )(z, taps, arrived)


def ctx_permute(value, target):
    nx, nz, nc = (lax.axis_size(a) for a in CTX)
    pairs = []
    for x in range(nx):
        for z in range(nz):
            for c in range(nc):
                to = target(x, z, c)
                pairs.append(((x * nz + z) * nc + c, (to[0] * nz + to[1]) * nc + to[2]))
    return lax.ppermute(value, CTX, pairs)


def ctx_shift(value, steps):
    count = math.prod(lax.axis_size(a) for a in CTX)
    return lax.ppermute(
        value, CTX, [(i, i + steps) for i in range(count) if 0 <= i + steps < count]
    )


def body(featured, feat_taps, inner_taps, out_weight, out_grad):
    rows = featured.shape[0]
    nx, nz, nc = (lax.axis_size(a) for a in CTX)
    inv_root = 1.0 / math.sqrt(rows * nx * nz * nc)
    core = lax.axis_index("core")
    col, z = (jnp.full((1,), lax.axis_index(a), jnp.int32) for a in ("col", "zl"))

    grads = lax.all_gather(out_grad, "row", axis=0)

    own = jnp.transpose(featured, (1, 0, 2))
    before = ctx_shift(own[:, rows - HALO :], 1)
    gated = forward(before, own, feat_taps, inner_taps)
    both = lax.all_gather(gated, "col", axis=1, tiled=True)
    channels = both.shape[1]
    split = both.T.reshape(nx * nz, nc, channels // (nx * nz * nc), rows)
    kept, sent = (
        lax.dynamic_index_in_dim(split, c, 1, keepdims=False).reshape(channels // nc, rows)
        for c in (core, 1 - core)
    )
    after = ctx_shift(jnp.concatenate([own[:, :HALO], out_grad[None, :HALO]]), -1)
    halo = jnp.broadcast_to(after[3], (lax.axis_size("row"), *after.shape[1:]))
    halo = lax.all_to_all(halo, "row", split_axis=0, concat_axis=0)

    sent, done = sent_weight(sent, grads, halo)
    arrived = ctx_permute(sent, lambda x, z, c: (x, z, 1 - c))
    far, near = gated_grad(col, grads, halo, out_weight, done)
    pair, done = kept_weight(nx, kept, grads, arrived)
    far = lax.all_gather(far, "col", axis=0)
    summed = lax.psum_scatter(pair, "x", scatter_dimension=0)

    grad_own, taps = backward(
        nx * nc, col, near, far, before, own, after, feat_taps, inner_taps, done
    )
    taps = lax.all_to_all(taps, ("x", "core"), split_axis=0, concat_axis=0)

    pieces, taps = middle(nz, summed, taps)
    pieces = lax.all_to_all(pieces, "zl", split_axis=0, concat_axis=0)
    grad_weight, grad_feat_taps, grad_inner_taps = last(inv_root, z, taps, pieces)
    return jnp.transpose(grad_own, (1, 0, 2)), grad_weight, grad_feat_taps, grad_inner_taps


def fine_mesh(mesh):
    row, col, ctx = mesh.devices.shape
    return Mesh(mesh.devices.reshape(row, col, ctx // 8, 4, 2), ("row", "col", *CTX))


def solution(mesh):
    return jax.shard_map(
        body,
        mesh=fine_mesh(mesh),
        in_specs=(
            P(CTX, None, ("row", "col")),
            P(None, None, ("row", "col")),
            P(None, ("row", "col")),
            P("row", "col"),
            P(CTX, ("col", "row")),
        ),
        out_specs=(
            P(CTX, None, ("row", "col")),
            P(("row", *CTX), "col"),
            P(None, None, ("row", "col")),
            P(None, ("row", "col")),
        ),
        check_vma=False,
    )
```

```python
import math

import jax
import jax.numpy as jnp
from jax import lax
from jax.experimental import pallas as pl
from jax.experimental.pallas import tpu as pltpu
from jax.sharding import Mesh
from jax.sharding import PartitionSpec as P

TAPS = 7
HALO = 16
LEAD = 8
CHUNK = 64
LANES = 128
CTX = ("x", "zl", "core")
F32 = jnp.float32
BF16 = jnp.bfloat16
VMEM_BYTES = 24 << 20


def spread(total):
    return [(start, min(CHUNK, total - start)) for start in range(0, total, CHUNK)]


def lane_spec(*lead):
    return pl.BlockSpec((*lead, LANES), lambda i: (0,) * len(lead) + (i,))


def whole(shape):
    return pl.BlockSpec(shape, lambda *_: (0,) * len(shape))


SCALAR = pl.BlockSpec(memory_space=pltpu.SMEM)
UNREAD = pl.BlockSpec(memory_space=pl.ANY)
IN_HBM = pl.BlockSpec(memory_space=pltpu.HBM)
IN_VMEM = pl.BlockSpec(memory_space=pltpu.VMEM)


def call(kernel, name, flops, moved, **kwargs):
    return pl.pallas_call(
        kernel,
        name=name,
        compiler_params=pltpu.CompilerParams(vmem_limit_bytes=VMEM_BYTES),
        cost_estimate=pl.CostEstimate(flops=flops, bytes_accessed=moved, transcendentals=0),
        **kwargs,
    )


def load_features(before, own, feats, after=None):
    rows = own.shape[1]
    for j in range(3):
        feats[j, 0:HALO, :] = before[j].astype(F32)
        if after is not None:
            feats[j, HALO + rows :, :] = after[j].astype(F32)
        for start, count in spread(rows):
            feats[j, HALO + start : HALO + start + count, :] = own[
                j, start : start + count, :
            ].astype(F32)


def mixed_parts(feats, feat_taps, start, count):
    base = HALO - LEAD + start
    parts = []
    for j in range(3):
        total = feat_taps[j, 0:1, :] * feats[j, base : base + count, :]
        for s in range(1, TAPS):
            total = total + feat_taps[j, s : s + 1, :] * feats[j, base - s : base - s + count, :]
        parts.append(total)
    return parts


def window_rows(product, inner_taps, start, count):
    base = LEAD + start
    total = inner_taps[0:1, :] * product[base : base + count, :]
    for s in range(1, TAPS):
        total = total + inner_taps[s : s + 1, :] * product[base - s : base - s + count, :]
    return total


def forward_kernel(_, before, own, feat_taps, inner_taps, gated, feats, query, product):
    rows = own.shape[1]
    load_features(before, own, feats)
    for start, count in spread(rows + LEAD):
        parts = mixed_parts(feats, feat_taps, start, count)
        query[start : start + count, :] = parts[0]
        product[start : start + count, :] = parts[1] * parts[2]
    for start, count in spread(rows):
        base = LEAD + start
        gated[start : start + count, :] = (
            query[base : base + count, :] * window_rows(product, inner_taps, start, count)
        ).astype(BF16)


def forward(place, before, own, feat_taps, inner_taps):
    _, rows, channels = own.shape
    return call(
        forward_kernel,
        "forward",
        60 * rows * channels,
        8 * rows * channels,
        grid=(channels // LANES,),
        in_specs=[
            SCALAR, lane_spec(3, HALO), lane_spec(3, rows), lane_spec(3, TAPS), lane_spec(TAPS)
        ],
        out_specs=lane_spec(rows),
        out_shape=jax.ShapeDtypeStruct((rows, channels), BF16),
        scratch_shapes=[
            pltpu.VMEM((3, rows + HALO, LANES), F32),
            pltpu.VMEM((rows + LEAD, LANES), F32),
            pltpu.VMEM((rows + LEAD, LANES), F32),
        ],
    )(place, before, own, feat_taps, inner_taps)


def backward_kernel(
    place, near, far, before, own, after, feat_taps, inner_taps, _,
    grads, tap_sums, feats, query, key, value, product, grad_window, grad_mixed,
):
    rows = own.shape[1]
    load_features(before, own, feats, after)
    for start, count in spread(rows + HALO + LEAD):
        parts = mixed_parts(feats, feat_taps, start, count)
        query[start : start + count, :] = parts[0]
        key[start : start + count, :] = parts[1]
        value[start : start + count, :] = parts[2]
        product[start : start + count, :] = parts[1] * parts[2]
    for start, count in spread(rows + HALO):
        total = near[start : start + count, :] + far[
            1 - place[0], start : start + count, :
        ].astype(F32)
        grad_window[start : start + count, :] = (
            total * query[LEAD + start : LEAD + start + count, :]
        )
        grad_mixed[0, start : start + count, :] = total * window_rows(
            product, inner_taps, start, count
        )
    for start, count in spread(rows + LEAD):
        total = inner_taps[0:1, :] * grad_window[start : start + count, :]
        for s in range(1, TAPS):
            total = total + inner_taps[s : s + 1, :] * grad_window[start + s : start + s + count, :]
        grad_mixed[1, start : start + count, :] = (
            total * value[LEAD + start : LEAD + start + count, :]
        )
        grad_mixed[2, start : start + count, :] = total * key[LEAD + start : LEAD + start + count, :]

    def folded(terms):
        return jnp.sum(terms.reshape(terms.shape[0] // 8, 8, LANES), axis=0)

    def put(place, sums):
        tile = [jnp.sum(total, axis=0, keepdims=True) for total in sums]
        tile = jnp.concatenate([*tile, jnp.zeros((1, LANES), F32)], axis=0)
        for copy in range(tap_sums.shape[0]):
            tap_sums[copy, place] = tile

    for j in range(3):
        sums = [jnp.zeros((8, LANES), F32) for _ in range(TAPS)]
        for start, count in spread(rows):
            here = grad_mixed[j, start : start + count, :]
            total = feat_taps[j, 0:1, :] * here
            for s in range(1, TAPS):
                total = (
                    total
                    + feat_taps[j, s : s + 1, :] * grad_mixed[j, start + s : start + s + count, :]
                )
            grads[j, start : start + count, :] = total.astype(BF16)
            for s in range(TAPS):
                base = HALO + start - s
                sums[s] = sums[s] + folded(here * feats[j, base : base + count, :])
        put(j, sums)
    sums = [jnp.zeros((8, LANES), F32) for _ in range(TAPS)]
    for start, count in spread(rows):
        here = grad_window[start : start + count, :]
        for s in range(TAPS):
            base = LEAD + start - s
            sums[s] = sums[s] + folded(here * product[base : base + count, :])
    put(3, sums)


def backward(copies, place, near, far, before, own, after, feat_taps, inner_taps, later):
    _, rows, channels = own.shape
    return call(
        backward_kernel,
        "backward",
        160 * rows * channels,
        20 * rows * channels,
        grid=(channels // LANES,),
        in_specs=[
            SCALAR, lane_spec(rows + HALO), lane_spec(2, rows + HALO), lane_spec(3, HALO),
            lane_spec(3, rows), lane_spec(3, HALO), lane_spec(3, TAPS), lane_spec(TAPS), UNREAD,
        ],
        out_specs=[lane_spec(3, rows), lane_spec(copies, 4, 8)],
        out_shape=[
            jax.ShapeDtypeStruct((3, rows, channels), BF16),
            jax.ShapeDtypeStruct((copies, 4, 8, channels), F32),
        ],
        scratch_shapes=[pltpu.VMEM((3, rows + 2 * HALO, LANES), F32)]
        + [pltpu.VMEM((rows + HALO + LEAD, LANES), F32)] * 4
        + [
            pltpu.VMEM((rows + HALO, LANES), F32),
            pltpu.VMEM((3, rows + HALO, LANES), F32),
        ],
    )(place, near, far, before, own, after, feat_taps, inner_taps, later)


TOKEN = jax.ShapeDtypeStruct((8, LANES), F32)


def sent_weight_kernel(gated, grads, _, sent, done):
    done[...] = jnp.zeros_like(done)
    for b in range(grads.shape[0]):
        sent[b] = jnp.dot(gated[...], grads[b], preferred_element_type=F32).astype(BF16)


def sent_weight(gated, grads, later):
    channels, rows = gated.shape
    blocks, _, width = grads.shape
    return call(
        sent_weight_kernel,
        "sent_weight",
        2 * rows * channels * blocks * width,
        2 * blocks * width * (rows + channels) + 2 * rows * channels,
        in_specs=[IN_VMEM] * 2 + [UNREAD],
        out_specs=[IN_VMEM] * 2,
        out_shape=[jax.ShapeDtypeStruct((blocks, channels, width), BF16), TOKEN],
    )(gated, grads, later)


def gated_grad_kernel(place, grads, halo, weight, _, far, near):
    half = near.shape[1]
    blocks = range(grads.shape[0])
    wide = jnp.concatenate(
        [
            jnp.concatenate([grads[b] for b in blocks], axis=1),
            jnp.concatenate([halo[b] for b in blocks], axis=1),
        ],
        axis=0,
    )
    for out, which in ((far, 1 - place[0]), (near, place[0])):
        total = lax.dot_general(
            wide,
            weight[pl.ds(pl.multiple_of(which * half, half), half), :],
            (((1,), (1,)), ((), ())),
            preferred_element_type=F32,
        )
        out[...] = total.astype(out.dtype)


def gated_grad(place, grads, halo, weight, later):
    blocks, rows, width = grads.shape
    rows = rows + halo.shape[1]
    channels = weight.shape[0]
    half = channels // 2
    return call(
        gated_grad_kernel,
        "gated_grad",
        2 * rows * channels * blocks * width,
        2 * blocks * width * (rows + channels) + 6 * rows * half,
        in_specs=[SCALAR, IN_VMEM, IN_VMEM, IN_VMEM, UNREAD],
        out_specs=[IN_VMEM] * 2,
        out_shape=[
            jax.ShapeDtypeStruct((rows, half), BF16),
            jax.ShapeDtypeStruct((rows, half), F32),
        ],
    )(place, grads, halo, weight, later)


def kept_weight_kernel(gated, grads, arrived, out, done, held, sems):
    done[...] = jnp.zeros_like(done)
    blocks, parts, size, _ = held.shape
    copies = []
    for b in range(blocks):
        total = jnp.dot(gated[...], grads[b], preferred_element_type=F32)
        total = (total + arrived[b].astype(F32)).astype(BF16)
        for part in range(parts):
            held[b, part] = total[part * size : (part + 1) * size]
        copies.append(pltpu.make_async_copy(held.at[b], out.at[:, b], sems.at[b]))
        copies[-1].start()
    for copy in copies:
        copy.wait()


def kept_weight(parts, gated, grads, arrived):
    channels, rows = gated.shape
    blocks, _, width = grads.shape
    size = channels // parts
    return call(
        kept_weight_kernel,
        "kept_weight",
        2 * rows * channels * blocks * width,
        2 * blocks * width * (rows + 2 * channels) + 2 * rows * channels,
        in_specs=[IN_VMEM] * 3,
        out_specs=[IN_HBM, IN_VMEM],
        out_shape=[jax.ShapeDtypeStruct((parts, blocks, size, width), BF16), TOKEN],
        scratch_shapes=[
            pltpu.VMEM((blocks, parts, size, width), BF16),
            pltpu.SemaphoreType.DMA((blocks,)),
        ],
    )(gated, grads, arrived)


def two_roundings(sums):
    high = sums.astype(BF16).astype(F32)
    return jnp.concatenate([high, sums - high], axis=1).astype(BF16)


def rejoined(both):
    both = both.astype(F32)
    return both[:, :8] + both[:, 8:]


def middle_kernel(pair, taps, out, out_taps):
    parts, _, size, _ = out.shape
    blocks = pair.shape[0]
    sums = taps[0]
    for copy in range(1, taps.shape[0]):
        sums = sums + taps[copy]
    out_taps[...] = sums
    both = two_roundings(sums)
    for part in range(parts):
        out[part, 0:blocks] = pair[:, part * size : (part + 1) * size, :]
        out[part, blocks:] = both


def middle(parts, pair, taps):
    blocks, channels, width = pair.shape
    shape = (parts, blocks + taps.shape[1], channels // parts, width)
    return call(
        middle_kernel,
        "middle",
        4 * pair.size,
        4 * pair.size,
        in_specs=[IN_VMEM] * 2,
        out_specs=[IN_VMEM] * 2,
        out_shape=[
            jax.ShapeDtypeStruct(shape, BF16),
            jax.ShapeDtypeStruct(taps.shape[1:], F32),
        ],
    )(pair, taps)


def last_kernel(scale, place, taps, arrived, out, out_feat, out_inner):
    parts, _, _, width = arrived.shape
    blocks = out.shape[1] // width
    for b in range(blocks):
        total = arrived[0, b].astype(F32)
        for part in range(1, parts):
            total = total + arrived[part, b].astype(F32)
        out[:, b * width : (b + 1) * width] = (total * scale).astype(BF16)
    total = taps[...]
    for part in range(parts):
        total = total + jnp.where(place[1] == part, 0.0, rejoined(arrived[part, blocks:]))
    total = total * scale
    out_feat[...] = total[:3, :TAPS]
    out_inner[...] = total[3, :TAPS]


def last(scale, place, taps, arrived):
    parts, count, channels, width = arrived.shape
    blocks = count - taps.shape[0]
    return call(
        lambda *refs: last_kernel(scale, *refs),
        "last",
        2 * arrived.size,
        2 * arrived.size,
        in_specs=[SCALAR] + [IN_VMEM] * 2,
        out_specs=[IN_VMEM] * 3,
        out_shape=[
            jax.ShapeDtypeStruct((channels, blocks * width), BF16),
            jax.ShapeDtypeStruct((3, TAPS, width), F32),
            jax.ShapeDtypeStruct((TAPS, width), F32),
        ],
    )(place, taps, arrived)


def ctx_permute(value, target):
    nx, nz, nc = (lax.axis_size(a) for a in CTX)
    pairs = []
    for x in range(nx):
        for z in range(nz):
            for c in range(nc):
                to = target(x, z, c)
                pairs.append(((x * nz + z) * nc + c, (to[0] * nz + to[1]) * nc + to[2]))
    return lax.ppermute(value, CTX, pairs)


def ctx_shift(value, steps):
    count = math.prod(lax.axis_size(a) for a in CTX)
    return lax.ppermute(
        value, CTX, [(i, i + steps) for i in range(count) if 0 <= i + steps < count]
    )


def body(featured, feat_taps, inner_taps, out_weight, out_grad):
    rows = featured.shape[0]
    nx, nz, nc = (lax.axis_size(a) for a in CTX)
    inv_root = 1.0 / math.sqrt(rows * nx * nz * nc)
    core = lax.axis_index("core")
    place = jnp.stack([lax.axis_index("col"), lax.axis_index("zl")])

    grads = lax.all_gather(out_grad, "row", axis=0)

    own = jnp.transpose(featured, (1, 0, 2))
    before = ctx_shift(own[:, rows - HALO :], 1)
    gated = forward(place, before, own, feat_taps, inner_taps)
    both = lax.all_gather(gated, "col", axis=1, tiled=True)
    channels = both.shape[1]
    split = both.T.reshape(nx * nz, nc, channels // (nx * nz * nc), rows)
    kept, sent = (
        lax.dynamic_index_in_dim(split, c, 1, keepdims=False).reshape(channels // nc, rows)
        for c in (core, 1 - core)
    )
    after = ctx_shift(jnp.concatenate([own[:, :HALO], out_grad[None, :HALO]]), -1)
    halo = jnp.broadcast_to(after[3], (lax.axis_size("row"), *after.shape[1:]))
    halo = lax.all_to_all(halo, "row", split_axis=0, concat_axis=0)

    sent, done = sent_weight(sent, grads, halo)
    arrived = ctx_permute(sent, lambda x, z, c: (x, z, 1 - c))
    far, near = gated_grad(place, grads, halo, out_weight, done)
    pair, done = kept_weight(nx, kept, grads, arrived)
    far = lax.all_gather(far, "col", axis=0)
    summed = lax.psum_scatter(pair, "x", scatter_dimension=0)

    grad_own, taps = backward(
        nx * nc, place, near, far, before, own, after, feat_taps, inner_taps, done
    )
    taps = lax.all_to_all(taps, ("x", "core"), split_axis=0, concat_axis=0)

    pieces, taps = middle(nz, summed, taps)
    pieces = lax.all_to_all(pieces, "zl", split_axis=0, concat_axis=0)
    grad_weight, grad_feat_taps, grad_inner_taps = last(inv_root, place, taps, pieces)
    return jnp.transpose(grad_own, (1, 0, 2)), grad_weight, grad_feat_taps, grad_inner_taps


def fine_mesh(mesh):
    row, col, ctx = mesh.devices.shape
    return Mesh(mesh.devices.reshape(row, col, ctx // 8, 4, 2), ("row", "col", *CTX))


def solution(mesh):
    return jax.shard_map(
        body,
        mesh=fine_mesh(mesh),
        in_specs=(
            P(CTX, None, ("row", "col")),
            P(None, None, ("row", "col")),
            P(None, ("row", "col")),
            P("row", "col"),
            P(CTX, ("col", "row")),
        ),
        out_specs=(
            P(CTX, None, ("row", "col")),
            P(("row", *CTX), "col"),
            P(None, None, ("row", "col")),
            P(None, ("row", "col")),
        ),
        check_vma=False,
    )
```

```python
import math

import jax
import jax.numpy as jnp
from jax import lax
from jax.experimental import pallas as pl
from jax.experimental.pallas import tpu as pltpu
from jax.sharding import Mesh
from jax.sharding import PartitionSpec as P

TAPS = 7
HALO = 16
LEAD = 8
CHUNK = 64
LANES = 128
CTX = ("x", "zl", "core")
F32 = jnp.float32
BF16 = jnp.bfloat16
VMEM_BYTES = 24 << 20


def spread(total):
    return [(start, min(CHUNK, total - start)) for start in range(0, total, CHUNK)]


def lane_spec(*lead):
    return pl.BlockSpec((*lead, LANES), lambda i: (0,) * len(lead) + (i,))


def whole(shape):
    return pl.BlockSpec(shape, lambda *_: (0,) * len(shape))


SCALAR = pl.BlockSpec(memory_space=pltpu.SMEM)
UNREAD = pl.BlockSpec(memory_space=pl.ANY)
IN_HBM = pl.BlockSpec(memory_space=pltpu.HBM)
IN_VMEM = pl.BlockSpec(memory_space=pltpu.VMEM)


def in_hbm(value):
    return pltpu.with_memory_space_constraint(value, pltpu.HBM)


def call(kernel, name, flops, moved, **kwargs):
    return pl.pallas_call(
        kernel,
        name=name,
        compiler_params=pltpu.CompilerParams(vmem_limit_bytes=VMEM_BYTES),
        cost_estimate=pl.CostEstimate(flops=flops, bytes_accessed=moved, transcendentals=0),
        **kwargs,
    )


def load_features(before, own, feats):
    rows = own.shape[1]
    for j in range(3):
        feats[j, 0:HALO, :] = before[j].astype(F32)
        for start, count in spread(rows):
            feats[j, HALO + start : HALO + start + count, :] = own[
                j, start : start + count, :
            ].astype(F32)


def mixed_parts(feats, feat_taps, start, count):
    base = HALO - LEAD + start
    parts = []
    for j in range(3):
        total = feat_taps[j, 0:1, :] * feats[j, base : base + count, :]
        for s in range(1, TAPS):
            total = total + feat_taps[j, s : s + 1, :] * feats[j, base - s : base - s + count, :]
        parts.append(total)
    return parts


def window_rows(product, inner_taps, start, count):
    base = LEAD + start
    total = inner_taps[0:1, :] * product[base : base + count, :]
    for s in range(1, TAPS):
        total = total + inner_taps[s : s + 1, :] * product[base - s : base - s + count, :]
    return total


def forward_kernel(before, own, feat_taps, inner_taps, gated, feats, query, product):
    rows = own.shape[1]
    load_features(before, own, feats)
    for start, count in spread(rows + LEAD):
        parts = mixed_parts(feats, feat_taps, start, count)
        query[start : start + count, :] = parts[0]
        product[start : start + count, :] = parts[1] * parts[2]
    for start, count in spread(rows):
        base = LEAD + start
        gated[start : start + count, :] = (
            query[base : base + count, :] * window_rows(product, inner_taps, start, count)
        ).astype(BF16)


def forward(before, own, feat_taps, inner_taps):
    _, rows, channels = own.shape
    return call(
        forward_kernel,
        "forward",
        60 * rows * channels,
        8 * rows * channels,
        grid=(channels // LANES,),
        in_specs=[
            lane_spec(3, HALO), lane_spec(3, rows), lane_spec(3, TAPS), lane_spec(TAPS)
        ],
        out_specs=lane_spec(rows),
        out_shape=jax.ShapeDtypeStruct((rows, channels), BF16),
        scratch_shapes=[
            pltpu.VMEM((3, rows + HALO, LANES), F32),
            pltpu.VMEM((rows + LEAD, LANES), F32),
            pltpu.VMEM((rows + LEAD, LANES), F32),
        ],
    )(before, own, feat_taps, inner_taps)


def backward_kernel(
    col, near, far, before, own, feat_taps, inner_taps, _,
    grads, head, tail, tap_sums, feats, query, key, value, product, grad_window, grad_mixed,
):
    rows = own.shape[1]
    load_features(before, own, feats)
    for start, count in spread(rows + LEAD):
        parts = mixed_parts(feats, feat_taps, start, count)
        query[start : start + count, :] = parts[0]
        key[start : start + count, :] = parts[1]
        value[start : start + count, :] = parts[2]
        product[start : start + count, :] = parts[1] * parts[2]
    zeros = jnp.zeros((HALO, LANES), F32)
    grad_window[0:HALO, :] = zeros
    grad_window[HALO + rows :, :] = zeros[:LEAD]
    for j in range(3):
        grad_mixed[j, 0:HALO, :] = zeros
        grad_mixed[j, HALO + rows :, :] = zeros[:LEAD]
    for start, count in spread(rows):
        at = HALO + start
        total = near[start : start + count, :] + far[
            1 - col[0], start : start + count, :
        ].astype(F32)
        grad_window[at : at + count, :] = total * query[LEAD + start : LEAD + start + count, :]
        grad_mixed[0, at : at + count, :] = total * window_rows(product, inner_taps, start, count)
    for start, count in spread(rows + LEAD):
        at = HALO - LEAD + start
        total = inner_taps[0:1, :] * grad_window[at : at + count, :]
        for s in range(1, TAPS):
            total = total + inner_taps[s : s + 1, :] * grad_window[at + s : at + s + count, :]
        grad_mixed[1, at : at + count, :] = total * value[start : start + count, :]
        grad_mixed[2, at : at + count, :] = total * key[start : start + count, :]

    def folded(terms):
        return jnp.sum(terms.reshape(terms.shape[0] // 8, 8, LANES), axis=0)

    def put(place, sums):
        rows = [jnp.sum(total, axis=0, keepdims=True) for total in sums]
        tile = jnp.concatenate([*rows, jnp.zeros((1, LANES), F32)], axis=0)
        for copy in range(tap_sums.shape[0]):
            tap_sums[copy, place] = tile

    def transposed(j, at, count):
        total = feat_taps[j, 0:1, :] * grad_mixed[j, at : at + count, :]
        for s in range(1, TAPS):
            total = total + feat_taps[j, s : s + 1, :] * grad_mixed[j, at + s : at + s + count, :]
        return total

    for j in range(3):
        head[j] = transposed(j, 0, HALO)
        sums = [jnp.zeros((8, LANES), F32) for _ in range(TAPS)]
        spans = [(HALO + start, count) for start, count in spread(rows)]
        for at, count in ([(HALO - LEAD, LEAD)] if j > 0 else []) + spans:
            here = grad_mixed[j, at : at + count, :]
            for s in range(TAPS):
                sums[s] = sums[s] + folded(here * feats[j, at - s : at - s + count, :])
            if at >= HALO:
                total = transposed(j, at, count)
                grads[j, at - HALO : at - HALO + count, :] = total.astype(BF16)
                if at + count == HALO + rows:
                    tail[j] = total[count - HALO :]
        put(j, sums)
    sums = [jnp.zeros((8, LANES), F32) for _ in range(TAPS)]
    for start, count in spread(rows):
        here = grad_window[HALO + start : HALO + start + count, :]
        for s in range(TAPS):
            base = LEAD + start - s
            sums[s] = sums[s] + folded(here * product[base : base + count, :])
    put(3, sums)


def backward(copies, col, near, far, before, own, feat_taps, inner_taps, after):
    _, rows, channels = own.shape
    edge = jax.ShapeDtypeStruct((3, HALO, channels), F32)
    return call(
        backward_kernel,
        "backward",
        160 * rows * channels,
        20 * rows * channels,
        grid=(channels // LANES,),
        in_specs=[
            SCALAR, lane_spec(rows), lane_spec(2, rows), lane_spec(3, HALO), lane_spec(3, rows),
            lane_spec(3, TAPS), lane_spec(TAPS), UNREAD,
        ],
        out_specs=[
            lane_spec(3, rows), lane_spec(3, HALO), lane_spec(3, HALO), lane_spec(copies, 4, 8)
        ],
        out_shape=[
            jax.ShapeDtypeStruct((3, rows, channels), BF16),
            edge,
            edge,
            jax.ShapeDtypeStruct((copies, 4, 8, channels), F32),
        ],
        scratch_shapes=[pltpu.VMEM((3, rows + HALO, LANES), F32)]
        + [pltpu.VMEM((rows + LEAD, LANES), F32)] * 4
        + [
            pltpu.VMEM((rows + HALO + LEAD, LANES), F32),
            pltpu.VMEM((3, rows + HALO + LEAD, LANES), F32),
        ],
    )(col, near, far, before, own, feat_taps, inner_taps, after)


TOKEN = jax.ShapeDtypeStruct((8, LANES), F32)


def products_kernel(
    col, core, own, other, grads, weight, far, near, out, done, held, held_weight, sems, weight_sems
):
    half = near.shape[1]
    fetches = [
        pltpu.make_async_copy(
            weight.at[pl.ds(pl.multiple_of(which * half, half), half), :],
            held_weight.at[at],
            weight_sems.at[at],
        )
        for at, which in enumerate((1 - col[0], col[0]))
    ]
    for copy in fetches:
        copy.start()
    done[...] = jnp.zeros_like(done)
    blocks, parts, size, _ = held.shape
    mine = [2 * b + core[0] for b in range(blocks)]
    copies = []
    for b in range(blocks):
        total = jnp.dot(own[...], grads[mine[b]], preferred_element_type=F32)
        total = total + jnp.dot(
            other[...], grads[4 * b + 1 - mine[b]], preferred_element_type=F32
        )
        for part in range(parts):
            held[b, part] = total[part * size : (part + 1) * size].astype(BF16)
        copies.append(pltpu.make_async_copy(held.at[b], out.at[:, b], sems.at[b]))
        copies[-1].start()
    wide = jnp.concatenate([grads[at] for at in mine], axis=1)
    for at, result in enumerate((far, near)):
        fetches[at].wait()
        total = lax.dot_general(
            wide, held_weight[at], (((1,), (1,)), ((), ())), preferred_element_type=F32
        )
        result[...] = total.astype(result.dtype)
    for copy in copies:
        copy.wait()


def products(parts, col, core, own, other, grads, weight):
    channels, rows = own.shape
    blocks, _, width = grads.shape
    blocks = blocks // 2
    half = weight.shape[0] // 2
    size = channels // parts
    return call(
        products_kernel,
        "products",
        4 * rows * (channels + half) * blocks * width,
        4 * blocks * width * (rows + channels) + 4 * rows * channels,
        in_specs=[SCALAR] * 2 + [IN_VMEM] * 3 + [IN_HBM],
        out_specs=[IN_VMEM, IN_VMEM, IN_HBM, IN_VMEM],
        out_shape=[
            jax.ShapeDtypeStruct((rows, half), BF16),
            jax.ShapeDtypeStruct((rows, half), F32),
            pltpu.HBM((parts, blocks, size, width), BF16),
            TOKEN,
        ],
        scratch_shapes=[
            pltpu.VMEM((blocks, parts, size, width), BF16),
            pltpu.VMEM((2, half, blocks * width), BF16),
            pltpu.SemaphoreType.DMA((blocks,)),
            pltpu.SemaphoreType.DMA((2,)),
        ],
    )(col, core, own, other, grads, in_hbm(weight))


def two_roundings(sums):
    high = sums.astype(BF16).astype(F32)
    return jnp.concatenate([high, sums - high], axis=1).astype(BF16)


def rejoined(both):
    both = both.astype(F32)
    return both[:, :8] + both[:, 8:]


def middle_kernel(pair, taps, head, out, out_taps, out_head):
    parts, _, size, _ = out.shape
    blocks = pair.shape[0]
    sums = taps[0]
    for copy in range(1, taps.shape[0]):
        sums = sums + taps[copy]
    out_taps[...] = sums
    out_head[...] = head[...]
    both = two_roundings(sums)
    for part in range(parts):
        out[part, 0:blocks] = pair[:, part * size : (part + 1) * size, :]
        out[part, blocks:] = both


def middle(parts, pair, taps, head):
    blocks, channels, width = pair.shape
    shape = (parts, blocks + taps.shape[1], channels // parts, width)
    outs = [
        jax.ShapeDtypeStruct(shape, BF16),
        jax.ShapeDtypeStruct(taps.shape[1:], F32),
        jax.ShapeDtypeStruct(head.shape, F32),
    ]
    return call(
        middle_kernel,
        "middle",
        4 * pair.size,
        4 * pair.size,
        in_specs=[IN_VMEM] * 3,
        out_specs=[IN_VMEM] * 3,
        out_shape=outs,
    )(pair, taps, head)


def last_kernel(
    scale, z, taps, arrived, tail, head, _, out, out_feat, out_inner, out_grads
):
    parts, _, _, width = arrived.shape
    blocks = out.shape[1] // width
    out_grads[...] = (tail[...] + head[...]).astype(BF16)
    for b in range(blocks):
        total = arrived[0, b].astype(F32)
        for part in range(1, parts):
            total = total + arrived[part, b].astype(F32)
        out[:, b * width : (b + 1) * width] = (total * scale).astype(BF16)
    total = taps[...]
    for part in range(parts):
        total = total + jnp.where(z[0] == part, 0.0, rejoined(arrived[part, blocks:]))
    total = total * scale
    out_feat[...] = total[:3, :TAPS]
    out_inner[...] = total[3, :TAPS]


def last(scale, z, taps, arrived, tail, head, grads):
    parts, count, channels, width = arrived.shape
    blocks = count - taps.shape[0]
    final = grads.shape[1] // HALO - 1
    args = (taps, arrived, tail, head)
    shapes = [
        jax.ShapeDtypeStruct((channels, blocks * width), BF16),
        jax.ShapeDtypeStruct((3, TAPS, width), F32),
        jax.ShapeDtypeStruct((TAPS, width), F32),
    ]
    return call(
        lambda *refs: last_kernel(scale, *refs),
        "last",
        2 * arrived.size,
        2 * arrived.size,
        grid=(1,),
        in_specs=[SCALAR] + [whole(v.shape) for v in args] + [UNREAD],
        out_specs=[whole(v.shape) for v in shapes]
        + [pl.BlockSpec(tail.shape, lambda i: (0, final, 0))],
        out_shape=shapes + [jax.ShapeDtypeStruct(grads.shape, grads.dtype)],
        input_output_aliases={5: 3},
    )(z, *args, grads)


def ctx_permute(value, target):
    nx, nz, nc = (lax.axis_size(a) for a in CTX)
    pairs = []
    for x in range(nx):
        for z in range(nz):
            for c in range(nc):
                to = target(x, z, c)
                pairs.append(((x * nz + z) * nc + c, (to[0] * nz + to[1]) * nc + to[2]))
    return lax.ppermute(value, CTX, pairs)


def ctx_shift(value, steps):
    count = math.prod(lax.axis_size(a) for a in CTX)
    return lax.ppermute(
        value, CTX, [(i, i + steps) for i in range(count) if 0 <= i + steps < count]
    )


def body(featured, feat_taps, inner_taps, out_weight, out_grad):
    rows = featured.shape[0]
    nx, nz, nc = (lax.axis_size(a) for a in CTX)
    inv_root = 1.0 / math.sqrt(rows * nx * nz * nc)
    col, core, z = (
        jnp.full((1,), lax.axis_index(a), jnp.int32) for a in ("col", "core", "zl")
    )

    grads = lax.all_gather(out_grad, ("row", "core"), axis=0)

    own = jnp.transpose(featured, (1, 0, 2))
    before = ctx_shift(own[:, rows - HALO :], 1)
    gated = forward(before, own, feat_taps, inner_taps)
    both = lax.all_gather(gated, "col", axis=1, tiled=True)
    channels = both.shape[1]
    split = both.T.reshape(nx * nz, nc, channels // (nx * nz * nc), rows)
    kept, sent = (
        lax.dynamic_index_in_dim(split, c, 1, keepdims=False).reshape(channels // nc, rows)
        for c in (core[0], 1 - core[0])
    )
    arrived = ctx_permute(sent, lambda x, z, c: (x, z, 1 - c))

    far, near, pair, done = products(nx, col, core, kept, arrived, grads, out_weight)
    summed = lax.psum_scatter(pair, "x", scatter_dimension=0)
    far = lax.all_gather(far, "col", axis=0)

    grad_own, head, tail, taps = backward(
        nx * nc, col, near, far, before, own, feat_taps, inner_taps, done
    )
    taps = lax.all_to_all(taps, ("x", "core"), split_axis=0, concat_axis=0)

    pieces, taps, head = middle(nz, summed, taps, head)
    pieces = lax.all_to_all(pieces, "zl", split_axis=0, concat_axis=0)
    head = ctx_shift(head, -1)
    grad_weight, grad_feat_taps, grad_inner_taps, grad_own = last(
        inv_root, z, taps, pieces, tail, head, grad_own
    )
    return jnp.transpose(grad_own, (1, 0, 2)), grad_weight, grad_feat_taps, grad_inner_taps


def fine_mesh(mesh):
    row, col, ctx = mesh.devices.shape
    return Mesh(mesh.devices.reshape(row, col, ctx // 8, 4, 2), ("row", "col", *CTX))


def solution(mesh):
    return jax.shard_map(
        body,
        mesh=fine_mesh(mesh),
        in_specs=(
            P(CTX, None, ("row", "col")),
            P(None, None, ("row", "col")),
            P(None, ("row", "col")),
            P("row", "col"),
            P(CTX, ("col", "row")),
        ),
        out_specs=(
            P(CTX, None, ("row", "col")),
            P(("row", *CTX), "col"),
            P(None, None, ("row", "col")),
            P(None, ("row", "col")),
        ),
        check_vma=False,
    )
```

```python
import math

import jax
import jax.numpy as jnp
from jax import lax
from jax.experimental import pallas as pl
from jax.experimental.pallas import tpu as pltpu
from jax.sharding import Mesh
from jax.sharding import PartitionSpec as P

TAPS = 7
HALO = 16
LEAD = 8
CHUNK = 64
LANES = 128
CTX = ("x", "zl", "core")
F32 = jnp.float32
BF16 = jnp.bfloat16
VMEM_BYTES = 24 << 20


def spread(total):
    return [(start, min(CHUNK, total - start)) for start in range(0, total, CHUNK)]


def lane_spec(*lead):
    return pl.BlockSpec((*lead, LANES), lambda i: (0,) * len(lead) + (i,))


def whole(shape):
    return pl.BlockSpec(shape, lambda *_: (0,) * len(shape))


SCALAR = pl.BlockSpec(memory_space=pltpu.SMEM)
UNREAD = pl.BlockSpec(memory_space=pl.ANY)
IN_HBM = pl.BlockSpec(memory_space=pltpu.HBM)
IN_VMEM = pl.BlockSpec(memory_space=pltpu.VMEM)


def in_hbm(value):
    return pltpu.with_memory_space_constraint(value, pltpu.HBM)


def call(kernel, name, flops, moved, **kwargs):
    return pl.pallas_call(
        kernel,
        name=name,
        compiler_params=pltpu.CompilerParams(vmem_limit_bytes=VMEM_BYTES),
        cost_estimate=pl.CostEstimate(flops=flops, bytes_accessed=moved, transcendentals=0),
        **kwargs,
    )


def load_features(before, own, feats):
    rows = own.shape[1]
    for j in range(3):
        feats[j, 0:HALO, :] = before[j].astype(F32)
        for start, count in spread(rows):
            feats[j, HALO + start : HALO + start + count, :] = own[
                j, start : start + count, :
            ].astype(F32)


def mixed_parts(feats, feat_taps, start, count):
    base = HALO - LEAD + start
    parts = []
    for j in range(3):
        total = feat_taps[j, 0:1, :] * feats[j, base : base + count, :]
        for s in range(1, TAPS):
            total = total + feat_taps[j, s : s + 1, :] * feats[j, base - s : base - s + count, :]
        parts.append(total)
    return parts


def window_rows(product, inner_taps, start, count):
    base = LEAD + start
    total = inner_taps[0:1, :] * product[base : base + count, :]
    for s in range(1, TAPS):
        total = total + inner_taps[s : s + 1, :] * product[base - s : base - s + count, :]
    return total


def forward_kernel(before, own, feat_taps, inner_taps, gated, feats, query, product):
    rows = own.shape[1]
    load_features(before, own, feats)
    for start, count in spread(rows + LEAD):
        parts = mixed_parts(feats, feat_taps, start, count)
        query[start : start + count, :] = parts[0]
        product[start : start + count, :] = parts[1] * parts[2]
    for start, count in spread(rows):
        base = LEAD + start
        gated[start : start + count, :] = (
            query[base : base + count, :] * window_rows(product, inner_taps, start, count)
        ).astype(BF16)


def forward(before, own, feat_taps, inner_taps):
    _, rows, channels = own.shape
    return call(
        forward_kernel,
        "forward",
        60 * rows * channels,
        8 * rows * channels,
        grid=(channels // LANES,),
        in_specs=[
            lane_spec(3, HALO), lane_spec(3, rows), lane_spec(3, TAPS), lane_spec(TAPS)
        ],
        out_specs=lane_spec(rows),
        out_shape=jax.ShapeDtypeStruct((rows, channels), BF16),
        scratch_shapes=[
            pltpu.VMEM((3, rows + HALO, LANES), F32),
            pltpu.VMEM((rows + LEAD, LANES), F32),
            pltpu.VMEM((rows + LEAD, LANES), F32),
        ],
    )(before, own, feat_taps, inner_taps)


def backward_kernel(
    col, near, far, before, own, feat_taps, inner_taps, _,
    grads, head, tail, tap_sums, held, sems, *scratch,
):
    copies = []
    for at in range(near.shape[1] // LANES):
        lanes = slice(at * LANES, (at + 1) * LANES)
        backward_lanes(
            col, near.at[:, lanes], far.at[:, :, lanes], before.at[:, :, lanes],
            own.at[:, :, lanes], feat_taps.at[:, :, lanes], inner_taps.at[:, lanes],
            held.at[at], head.at[:, :, lanes], tail.at[:, :, lanes], tap_sums.at[:, :, :, lanes],
            *scratch,
        )
        copies.append(
            pltpu.make_async_copy(held.at[at], grads.at[:, :, lanes], sems.at[at])
        )
        copies[-1].start()
    for copy in copies:
        copy.wait()


def backward_lanes(
    col, near, far, before, own, feat_taps, inner_taps,
    grads, head, tail, tap_sums, feats, query, key, value, product, grad_window, grad_mixed,
):
    rows = own.shape[1]
    load_features(before, own, feats)
    for start, count in spread(rows + LEAD):
        parts = mixed_parts(feats, feat_taps, start, count)
        query[start : start + count, :] = parts[0]
        key[start : start + count, :] = parts[1]
        value[start : start + count, :] = parts[2]
        product[start : start + count, :] = parts[1] * parts[2]
    zeros = jnp.zeros((HALO, LANES), F32)
    grad_window[0:HALO, :] = zeros
    grad_window[HALO + rows :, :] = zeros[:LEAD]
    for j in range(3):
        grad_mixed[j, 0:HALO, :] = zeros
        grad_mixed[j, HALO + rows :, :] = zeros[:LEAD]
    for start, count in spread(rows):
        at = HALO + start
        total = near[start : start + count, :] + far[
            1 - col[0], start : start + count, :
        ].astype(F32)
        grad_window[at : at + count, :] = total * query[LEAD + start : LEAD + start + count, :]
        grad_mixed[0, at : at + count, :] = total * window_rows(product, inner_taps, start, count)
    for start, count in spread(rows + LEAD):
        at = HALO - LEAD + start
        total = inner_taps[0:1, :] * grad_window[at : at + count, :]
        for s in range(1, TAPS):
            total = total + inner_taps[s : s + 1, :] * grad_window[at + s : at + s + count, :]
        grad_mixed[1, at : at + count, :] = total * value[start : start + count, :]
        grad_mixed[2, at : at + count, :] = total * key[start : start + count, :]

    def folded(terms):
        return jnp.sum(terms.reshape(terms.shape[0] // 8, 8, LANES), axis=0)

    def put(place, sums):
        rows = [jnp.sum(total, axis=0, keepdims=True) for total in sums]
        tile = jnp.concatenate([*rows, jnp.zeros((1, LANES), F32)], axis=0)
        for copy in range(tap_sums.shape[0]):
            tap_sums[copy, place] = tile

    def transposed(j, at, count):
        total = feat_taps[j, 0:1, :] * grad_mixed[j, at : at + count, :]
        for s in range(1, TAPS):
            total = total + feat_taps[j, s : s + 1, :] * grad_mixed[j, at + s : at + s + count, :]
        return total

    for j in range(3):
        head[j] = transposed(j, 0, HALO)
        sums = [jnp.zeros((8, LANES), F32) for _ in range(TAPS)]
        spans = [(HALO + start, count) for start, count in spread(rows)]
        for at, count in ([(HALO - LEAD, LEAD)] if j > 0 else []) + spans:
            here = grad_mixed[j, at : at + count, :]
            for s in range(TAPS):
                sums[s] = sums[s] + folded(here * feats[j, at - s : at - s + count, :])
            if at >= HALO:
                total = transposed(j, at, count)
                grads[j, at - HALO : at - HALO + count, :] = total.astype(BF16)
                if at + count == HALO + rows:
                    tail[j] = total[count - HALO :]
        put(j, sums)
    sums = [jnp.zeros((8, LANES), F32) for _ in range(TAPS)]
    for start, count in spread(rows):
        here = grad_window[HALO + start : HALO + start + count, :]
        for s in range(TAPS):
            base = LEAD + start - s
            sums[s] = sums[s] + folded(here * product[base : base + count, :])
    put(3, sums)


def backward(copies, col, near, far, before, own, feat_taps, inner_taps, after):
    _, rows, channels = own.shape
    edge = jax.ShapeDtypeStruct((3, HALO, channels), F32)
    return call(
        backward_kernel,
        "backward",
        160 * rows * channels,
        20 * rows * channels,
        in_specs=[SCALAR] + [IN_VMEM] * 6 + [UNREAD],
        out_specs=[IN_HBM] + [IN_VMEM] * 3,
        out_shape=[
            pltpu.HBM((3, rows, channels), BF16),
            edge,
            edge,
            jax.ShapeDtypeStruct((copies, 4, 8, channels), F32),
        ],
        scratch_shapes=[
            pltpu.VMEM((channels // LANES, 3, rows, LANES), BF16),
            pltpu.SemaphoreType.DMA((channels // LANES,)),
            pltpu.VMEM((3, rows + HALO, LANES), F32),
        ]
        + [pltpu.VMEM((rows + LEAD, LANES), F32)] * 4
        + [
            pltpu.VMEM((rows + HALO + LEAD, LANES), F32),
            pltpu.VMEM((3, rows + HALO + LEAD, LANES), F32),
        ],
    )(col, near, far, before, own, feat_taps, inner_taps, after)


TOKEN = jax.ShapeDtypeStruct((8, LANES), F32)


def products_kernel(
    col, core, own, other, grads, weight, far, near, out, done, held, held_weight, sems, weight_sems
):
    half = near.shape[1]
    pieces = weight_sems.shape[1]
    size = half // pieces
    fetches = [
        [
            pltpu.make_async_copy(
                weight.at[pl.ds(pl.multiple_of(which * half + piece * size, size), size), :],
                held_weight.at[at, piece * size : (piece + 1) * size],
                weight_sems.at[at, piece],
            )
            for piece in range(pieces)
        ]
        for at, which in enumerate((1 - col[0], col[0]))
    ]
    for copy in fetches[0] + fetches[1]:
        copy.start()
    done[...] = jnp.zeros_like(done)
    blocks, parts, size, _ = held.shape
    mine = [2 * b + core[0] for b in range(blocks)]
    copies = []
    gated = jnp.concatenate([own[...], other[...]], axis=1)
    for b in range(blocks):
        pair = jnp.concatenate([grads[mine[b]], grads[4 * b + 1 - mine[b]]], axis=0)
        total = jnp.dot(gated, pair, preferred_element_type=F32)
        for part in range(parts):
            held[b, part] = total[part * size : (part + 1) * size].astype(BF16)
        copies.append(pltpu.make_async_copy(held.at[b], out.at[:, b], sems.at[b]))
        copies[-1].start()
    wide = jnp.concatenate([grads[at] for at in mine], axis=1)
    for at, result in enumerate((far, near)):
        for copy in fetches[at]:
            copy.wait()
        total = lax.dot_general(
            wide, held_weight[at], (((1,), (1,)), ((), ())), preferred_element_type=F32
        )
        result[...] = total.astype(result.dtype)
    for copy in copies:
        copy.wait()


def products(parts, col, core, own, other, grads, weight):
    channels, rows = own.shape
    blocks, _, width = grads.shape
    blocks = blocks // 2
    half = weight.shape[0] // 2
    size = channels // parts
    return call(
        products_kernel,
        "products",
        4 * rows * (channels + half) * blocks * width,
        4 * blocks * width * (rows + channels) + 4 * rows * channels,
        in_specs=[SCALAR] * 2 + [IN_VMEM] * 3 + [IN_HBM],
        out_specs=[IN_VMEM, IN_VMEM, IN_HBM, IN_VMEM],
        out_shape=[
            jax.ShapeDtypeStruct((rows, half), BF16),
            jax.ShapeDtypeStruct((rows, half), F32),
            pltpu.HBM((parts, blocks, size, width), BF16),
            TOKEN,
        ],
        scratch_shapes=[
            pltpu.VMEM((blocks, parts, size, width), BF16),
            pltpu.VMEM((2, half, blocks * width), BF16),
            pltpu.SemaphoreType.DMA((blocks,)),
            pltpu.SemaphoreType.DMA((2, 4)),
        ],
    )(col, core, own, other, grads, in_hbm(weight))


def two_roundings(sums):
    high = sums.astype(BF16).astype(F32)
    return jnp.concatenate([high, sums - high], axis=1).astype(BF16)


def rejoined(both):
    both = both.astype(F32)
    return both[:, :8] + both[:, 8:]


def middle_kernel(pair, taps, head, out, out_taps, out_head):
    parts, _, size, _ = out.shape
    blocks = pair.shape[0]
    sums = taps[0]
    for copy in range(1, taps.shape[0]):
        sums = sums + taps[copy]
    out_taps[...] = sums
    out_head[...] = head[...]
    both = two_roundings(sums)
    for part in range(parts):
        out[part, 0:blocks] = pair[:, part * size : (part + 1) * size, :]
        out[part, blocks:] = both


def middle(parts, pair, taps, head):
    blocks, channels, width = pair.shape
    shape = (parts, blocks + taps.shape[1], channels // parts, width)
    outs = [
        jax.ShapeDtypeStruct(shape, BF16),
        jax.ShapeDtypeStruct(taps.shape[1:], F32),
        jax.ShapeDtypeStruct(head.shape, F32),
    ]
    return call(
        middle_kernel,
        "middle",
        4 * pair.size,
        4 * pair.size,
        in_specs=[IN_VMEM] * 3,
        out_specs=[IN_VMEM] * 3,
        out_shape=outs,
    )(pair, taps, head)


def last_kernel(
    scale, z, taps, arrived, tail, head, _, out, out_feat, out_inner, out_grads
):
    parts, _, _, width = arrived.shape
    blocks = out.shape[1] // width
    out_grads[...] = (tail[...] + head[...]).astype(BF16)
    for b in range(blocks):
        total = arrived[0, b].astype(F32)
        for part in range(1, parts):
            total = total + arrived[part, b].astype(F32)
        out[:, b * width : (b + 1) * width] = (total * scale).astype(BF16)
    total = taps[...]
    for part in range(parts):
        total = total + jnp.where(z[0] == part, 0.0, rejoined(arrived[part, blocks:]))
    total = total * scale
    out_feat[...] = total[:3, :TAPS]
    out_inner[...] = total[3, :TAPS]


def last(scale, z, taps, arrived, tail, head, grads):
    parts, count, channels, width = arrived.shape
    blocks = count - taps.shape[0]
    final = grads.shape[1] // HALO - 1
    args = (taps, arrived, tail, head)
    shapes = [
        jax.ShapeDtypeStruct((channels, blocks * width), BF16),
        jax.ShapeDtypeStruct((3, TAPS, width), F32),
        jax.ShapeDtypeStruct((TAPS, width), F32),
    ]
    return call(
        lambda *refs: last_kernel(scale, *refs),
        "last",
        2 * arrived.size,
        2 * arrived.size,
        grid=(1,),
        in_specs=[SCALAR] + [whole(v.shape) for v in args] + [UNREAD],
        out_specs=[whole(v.shape) for v in shapes]
        + [pl.BlockSpec(tail.shape, lambda i: (0, final, 0))],
        out_shape=shapes + [jax.ShapeDtypeStruct(grads.shape, grads.dtype)],
        input_output_aliases={5: 3},
    )(z, *args, grads)


def ctx_permute(value, target):
    nx, nz, nc = (lax.axis_size(a) for a in CTX)
    pairs = []
    for x in range(nx):
        for z in range(nz):
            for c in range(nc):
                to = target(x, z, c)
                pairs.append(((x * nz + z) * nc + c, (to[0] * nz + to[1]) * nc + to[2]))
    return lax.ppermute(value, CTX, pairs)


def ctx_shift(value, steps):
    count = math.prod(lax.axis_size(a) for a in CTX)
    return lax.ppermute(
        value, CTX, [(i, i + steps) for i in range(count) if 0 <= i + steps < count]
    )


def body(featured, feat_taps, inner_taps, out_weight, out_grad):
    rows = featured.shape[0]
    nx, nz, nc = (lax.axis_size(a) for a in CTX)
    inv_root = 1.0 / math.sqrt(rows * nx * nz * nc)
    col, core, z = (
        jnp.full((1,), lax.axis_index(a), jnp.int32) for a in ("col", "core", "zl")
    )

    grads = lax.all_gather(out_grad, ("row", "core"), axis=0)

    own = jnp.transpose(featured, (1, 0, 2))
    before = ctx_shift(own[:, rows - HALO :], 1)
    gated = forward(before, own, feat_taps, inner_taps)
    both = lax.all_gather(gated, "col", axis=1, tiled=True)
    channels = both.shape[1]
    split = both.T.reshape(nx * nz, nc, channels // (nx * nz * nc), rows)
    kept, sent = (
        lax.dynamic_index_in_dim(split, c, 1, keepdims=False).reshape(channels // nc, rows)
        for c in (core[0], 1 - core[0])
    )
    arrived = ctx_permute(sent, lambda x, z, c: (x, z, 1 - c))

    far, near, pair, done = products(nx, col, core, kept, arrived, grads, out_weight)
    summed = lax.psum_scatter(pair, "x", scatter_dimension=0)
    far = lax.all_gather(far, "col", axis=0)

    grad_own, head, tail, taps = backward(
        nx * nc, col, near, far, before, own, feat_taps, inner_taps, done
    )
    taps = lax.all_to_all(taps, ("x", "core"), split_axis=0, concat_axis=0)

    pieces, taps, head = middle(nz, summed, taps, head)
    pieces = lax.all_to_all(pieces, "zl", split_axis=0, concat_axis=0)
    head = ctx_shift(head, -1)
    grad_weight, grad_feat_taps, grad_inner_taps, grad_own = last(
        inv_root, z, taps, pieces, tail, head, grad_own
    )
    return jnp.transpose(grad_own, (1, 0, 2)), grad_weight, grad_feat_taps, grad_inner_taps


def fine_mesh(mesh):
    row, col, ctx = mesh.devices.shape
    return Mesh(mesh.devices.reshape(row, col, ctx // 8, 4, 2), ("row", "col", *CTX))


def solution(mesh):
    return jax.shard_map(
        body,
        mesh=fine_mesh(mesh),
        in_specs=(
            P(CTX, None, ("row", "col")),
            P(None, None, ("row", "col")),
            P(None, ("row", "col")),
            P("row", "col"),
            P(CTX, ("col", "row")),
        ),
        out_specs=(
            P(CTX, None, ("row", "col")),
            P(("row", *CTX), "col"),
            P(None, None, ("row", "col")),
            P(None, ("row", "col")),
        ),
        check_vma=False,
    )
```

```python
import math

import jax
import jax.numpy as jnp
from jax import lax
from jax.experimental import pallas as pl
from jax.experimental.pallas import tpu as pltpu
from jax.sharding import Mesh
from jax.sharding import PartitionSpec as P

TAPS = 7
HALO = 16
LEAD = 8
CHUNK = 64
LANES = 128
CTX = ("x", "zl", "core")
F32 = jnp.float32
BF16 = jnp.bfloat16
VMEM_BYTES = 24 << 20


def spread(total):
    return [(start, min(CHUNK, total - start)) for start in range(0, total, CHUNK)]


def lane_spec(*lead):
    return pl.BlockSpec((*lead, LANES), lambda i: (0,) * len(lead) + (i,))


def whole(shape):
    return pl.BlockSpec(shape, lambda *_: (0,) * len(shape))


SCALAR = pl.BlockSpec(memory_space=pltpu.SMEM)
UNREAD = pl.BlockSpec(memory_space=pl.ANY)
IN_HBM = pl.BlockSpec(memory_space=pltpu.HBM)
IN_VMEM = pl.BlockSpec(memory_space=pltpu.VMEM)


def in_hbm(value):
    return pltpu.with_memory_space_constraint(value, pltpu.HBM)


def call(kernel, name, flops, moved, **kwargs):
    return pl.pallas_call(
        kernel,
        name=name,
        compiler_params=pltpu.CompilerParams(vmem_limit_bytes=VMEM_BYTES),
        cost_estimate=pl.CostEstimate(flops=flops, bytes_accessed=moved, transcendentals=0),
        **kwargs,
    )


def load_features(before, own, feats):
    rows = own.shape[1]
    for j in range(3):
        feats[j, 0:HALO, :] = before[j].astype(F32)
        for start, count in spread(rows):
            feats[j, HALO + start : HALO + start + count, :] = own[
                j, start : start + count, :
            ].astype(F32)


def mixed_parts(feats, feat_taps, start, count):
    base = HALO - LEAD + start
    parts = []
    for j in range(3):
        total = feat_taps[j, 0:1, :] * feats[j, base : base + count, :]
        for s in range(1, TAPS):
            total = total + feat_taps[j, s : s + 1, :] * feats[j, base - s : base - s + count, :]
        parts.append(total)
    return parts


def window_rows(product, inner_taps, start, count):
    base = LEAD + start
    total = inner_taps[0:1, :] * product[base : base + count, :]
    for s in range(1, TAPS):
        total = total + inner_taps[s : s + 1, :] * product[base - s : base - s + count, :]
    return total


def forward_kernel(before, own, feat_taps, inner_taps, gated, feats, query, product):
    rows = own.shape[1]
    load_features(before, own, feats)
    for start, count in spread(rows + LEAD):
        parts = mixed_parts(feats, feat_taps, start, count)
        query[start : start + count, :] = parts[0]
        product[start : start + count, :] = parts[1] * parts[2]
    for start, count in spread(rows):
        base = LEAD + start
        gated[start : start + count, :] = (
            query[base : base + count, :] * window_rows(product, inner_taps, start, count)
        ).astype(BF16)


def forward(before, own, feat_taps, inner_taps):
    _, rows, channels = own.shape
    return call(
        forward_kernel,
        "forward",
        60 * rows * channels,
        8 * rows * channels,
        grid=(channels // LANES,),
        in_specs=[
            lane_spec(3, HALO), lane_spec(3, rows), lane_spec(3, TAPS), lane_spec(TAPS)
        ],
        out_specs=lane_spec(rows),
        out_shape=jax.ShapeDtypeStruct((rows, channels), BF16),
        scratch_shapes=[
            pltpu.VMEM((3, rows + HALO, LANES), F32),
            pltpu.VMEM((rows + LEAD, LANES), F32),
            pltpu.VMEM((rows + LEAD, LANES), F32),
        ],
    )(before, own, feat_taps, inner_taps)


def backward_kernel(
    col, near, far, before, own, feat_taps, inner_taps, _,
    grads, head, tail, tap_sums, held, sems, *scratch,
):
    copies = []
    for at in range(near.shape[1] // LANES):
        lanes = slice(at * LANES, (at + 1) * LANES)
        backward_lanes(
            col, near.at[:, lanes], far.at[:, :, lanes], before.at[:, :, lanes],
            own.at[:, :, lanes], feat_taps.at[:, :, lanes], inner_taps.at[:, lanes],
            held.at[at], head.at[:, :, lanes], tail.at[:, :, lanes], tap_sums.at[:, :, :, lanes],
            *scratch,
        )
        copies.append(
            pltpu.make_async_copy(held.at[at], grads.at[:, :, lanes], sems.at[at])
        )
        copies[-1].start()
    for copy in copies:
        copy.wait()


def backward_lanes(
    col, near, far, before, own, feat_taps, inner_taps,
    grads, head, tail, tap_sums, feats, query, key, value, product, grad_window, grad_mixed,
):
    rows = own.shape[1]
    load_features(before, own, feats)
    for start, count in spread(rows + LEAD):
        parts = mixed_parts(feats, feat_taps, start, count)
        query[start : start + count, :] = parts[0]
        key[start : start + count, :] = parts[1]
        value[start : start + count, :] = parts[2]
        product[start : start + count, :] = parts[1] * parts[2]
    zeros = jnp.zeros((HALO, LANES), F32)
    grad_window[0:HALO, :] = zeros
    grad_window[HALO + rows :, :] = zeros[:LEAD]
    for j in range(3):
        grad_mixed[j, 0:HALO, :] = zeros
        grad_mixed[j, HALO + rows :, :] = zeros[:LEAD]
    for start, count in spread(rows):
        at = HALO + start
        total = near[start : start + count, :] + far[
            1 - col[0], start : start + count, :
        ].astype(F32)
        grad_window[at : at + count, :] = total * query[LEAD + start : LEAD + start + count, :]
        grad_mixed[0, at : at + count, :] = total * window_rows(product, inner_taps, start, count)
    for start, count in spread(rows + LEAD):
        at = HALO - LEAD + start
        total = inner_taps[0:1, :] * grad_window[at : at + count, :]
        for s in range(1, TAPS):
            total = total + inner_taps[s : s + 1, :] * grad_window[at + s : at + s + count, :]
        grad_mixed[1, at : at + count, :] = total * value[start : start + count, :]
        grad_mixed[2, at : at + count, :] = total * key[start : start + count, :]

    def folded(terms):
        return jnp.sum(terms.reshape(terms.shape[0] // 8, 8, LANES), axis=0)

    def put(place, sums):
        rows = [jnp.sum(total, axis=0, keepdims=True) for total in sums]
        tile = jnp.concatenate([*rows, jnp.zeros((1, LANES), F32)], axis=0)
        for copy in range(tap_sums.shape[0]):
            tap_sums[copy, place] = tile

    def transposed(j, at, count):
        total = feat_taps[j, 0:1, :] * grad_mixed[j, at : at + count, :]
        for s in range(1, TAPS):
            total = total + feat_taps[j, s : s + 1, :] * grad_mixed[j, at + s : at + s + count, :]
        return total

    for j in range(3):
        head[j] = transposed(j, 0, HALO)
        sums = [jnp.zeros((8, LANES), F32) for _ in range(TAPS)]
        spans = [(HALO + start, count) for start, count in spread(rows)]
        for at, count in ([(HALO - LEAD, LEAD)] if j > 0 else []) + spans:
            here = grad_mixed[j, at : at + count, :]
            for s in range(TAPS):
                sums[s] = sums[s] + folded(here * feats[j, at - s : at - s + count, :])
            if at >= HALO:
                total = transposed(j, at, count)
                grads[j, at - HALO : at - HALO + count, :] = total.astype(BF16)
                if at + count == HALO + rows:
                    tail[j] = total[count - HALO :]
        put(j, sums)
    sums = [jnp.zeros((8, LANES), F32) for _ in range(TAPS)]
    for start, count in spread(rows):
        here = grad_window[HALO + start : HALO + start + count, :]
        for s in range(TAPS):
            base = LEAD + start - s
            sums[s] = sums[s] + folded(here * product[base : base + count, :])
    put(3, sums)


def backward(copies, col, near, far, before, own, feat_taps, inner_taps, after):
    _, rows, channels = own.shape
    edge = jax.ShapeDtypeStruct((3, HALO, channels), F32)
    return call(
        backward_kernel,
        "backward",
        160 * rows * channels,
        20 * rows * channels,
        in_specs=[SCALAR] + [IN_VMEM] * 6 + [UNREAD],
        out_specs=[IN_HBM] + [IN_VMEM] * 3,
        out_shape=[
            pltpu.HBM((3, rows, channels), BF16),
            edge,
            edge,
            jax.ShapeDtypeStruct((copies, 4, 8, channels), F32),
        ],
        scratch_shapes=[
            pltpu.VMEM((channels // LANES, 3, rows, LANES), BF16),
            pltpu.SemaphoreType.DMA((channels // LANES,)),
            pltpu.VMEM((3, rows + HALO, LANES), F32),
        ]
        + [pltpu.VMEM((rows + LEAD, LANES), F32)] * 4
        + [
            pltpu.VMEM((rows + HALO + LEAD, LANES), F32),
            pltpu.VMEM((3, rows + HALO + LEAD, LANES), F32),
        ],
    )(col, near, far, before, own, feat_taps, inner_taps, after)


TOKEN = jax.ShapeDtypeStruct((8, LANES), F32)


def products_kernel(
    col, core, own, other, grads, weight, far, near, out, done, held, held_weight, sems, weight_sems
):
    half = near.shape[1]
    pieces = weight_sems.shape[1]
    size = half // pieces
    fetches = [
        [
            pltpu.make_async_copy(
                weight.at[pl.ds(pl.multiple_of(which * half + piece * size, size), size), :],
                held_weight.at[at, piece * size : (piece + 1) * size],
                weight_sems.at[at, piece],
            )
            for piece in range(pieces)
        ]
        for at, which in enumerate((1 - col[0], col[0]))
    ]
    for copy in fetches[0] + fetches[1]:
        copy.start()
    done[...] = jnp.zeros_like(done)
    blocks, parts, size, _ = held.shape
    mine = [2 * b + core[0] for b in range(blocks)]
    copies = []
    gated = jnp.concatenate([own[...], other[...]], axis=1)
    for b in range(blocks):
        pair = jnp.concatenate([grads[mine[b]], grads[4 * b + 1 - mine[b]]], axis=0)
        total = jnp.dot(gated, pair, preferred_element_type=F32)
        for part in range(parts):
            held[b, part] = total[part * size : (part + 1) * size].astype(BF16)
        copies.append(pltpu.make_async_copy(held.at[b], out.at[:, b], sems.at[b]))
        copies[-1].start()
    wide = jnp.concatenate([grads[at] for at in mine], axis=1)
    for at, result in enumerate((far, near)):
        for copy in fetches[at]:
            copy.wait()
        total = lax.dot_general(
            wide, held_weight[at], (((1,), (1,)), ((), ())), preferred_element_type=F32
        )
        result[...] = total.astype(result.dtype)
    for copy in copies:
        copy.wait()


def products(parts, col, core, own, other, grads, weight):
    channels, rows = own.shape
    blocks, _, width = grads.shape
    blocks = blocks // 2
    half = weight.shape[0] // 2
    size = channels // parts
    return call(
        products_kernel,
        "products",
        4 * rows * (channels + half) * blocks * width,
        4 * blocks * width * (rows + channels) + 4 * rows * channels,
        in_specs=[SCALAR] * 2 + [IN_VMEM] * 3 + [IN_HBM],
        out_specs=[IN_VMEM, IN_VMEM, IN_HBM, IN_VMEM],
        out_shape=[
            jax.ShapeDtypeStruct((rows, half), BF16),
            jax.ShapeDtypeStruct((rows, half), F32),
            pltpu.HBM((parts, blocks, size, width), BF16),
            TOKEN,
        ],
        scratch_shapes=[
            pltpu.VMEM((blocks, parts, size, width), BF16),
            pltpu.VMEM((2, half, blocks * width), BF16),
            pltpu.SemaphoreType.DMA((blocks,)),
            pltpu.SemaphoreType.DMA((2, 4)),
        ],
    )(col, core, own, other, grads, in_hbm(weight))


def paired(sums):
    return jnp.concatenate([sums[:2], sums[2:]], axis=1).astype(BF16)


def parted(tiles):
    tiles = tiles.astype(F32)
    return jnp.concatenate([tiles[:, :8], tiles[:, 8:]], axis=0)


def middle_kernel(pair, taps, head, out, out_taps, out_head):
    parts, _, size, _ = out.shape
    blocks = pair.shape[0]
    sums = taps[0]
    for copy in range(1, taps.shape[0]):
        sums = sums + taps[copy]
    out_taps[...] = sums
    out_head[...] = head[...].astype(BF16)
    both = paired(sums)
    for part in range(parts):
        out[part, 0:blocks] = pair[:, part * size : (part + 1) * size, :]
        out[part, blocks:] = both


def middle(parts, pair, taps, head):
    blocks, channels, width = pair.shape
    shape = (parts, blocks + taps.shape[1] // 2, channels // parts, width)
    outs = [
        jax.ShapeDtypeStruct(shape, BF16),
        jax.ShapeDtypeStruct(taps.shape[1:], F32),
        jax.ShapeDtypeStruct(head.shape, BF16),
    ]
    return call(
        middle_kernel,
        "middle",
        4 * pair.size,
        4 * pair.size,
        in_specs=[IN_VMEM] * 3,
        out_specs=[IN_VMEM] * 3,
        out_shape=outs,
    )(pair, taps, head)


def last_kernel(
    scale, z, taps, arrived, tail, head, _, out, out_feat, out_inner, out_grads
):
    parts, _, _, width = arrived.shape
    blocks = out.shape[1] // width
    out_grads[...] = (tail[...] + head[...].astype(F32)).astype(BF16)
    for b in range(blocks):
        total = arrived[0, b].astype(F32)
        for part in range(1, parts):
            total = total + arrived[part, b].astype(F32)
        out[:, b * width : (b + 1) * width] = (total * scale).astype(BF16)
    total = taps[...]
    for part in range(parts):
        total = total + jnp.where(z[0] == part, 0.0, parted(arrived[part, blocks:]))
    total = total * scale
    out_feat[...] = total[:3, :TAPS]
    out_inner[...] = total[3, :TAPS]


def last(scale, z, taps, arrived, tail, head, grads):
    parts, count, channels, width = arrived.shape
    blocks = count - taps.shape[0] // 2
    final = grads.shape[1] // HALO - 1
    args = (taps, arrived, tail, head)
    shapes = [
        jax.ShapeDtypeStruct((channels, blocks * width), BF16),
        jax.ShapeDtypeStruct((3, TAPS, width), F32),
        jax.ShapeDtypeStruct((TAPS, width), F32),
    ]
    return call(
        lambda *refs: last_kernel(scale, *refs),
        "last",
        2 * arrived.size,
        2 * arrived.size,
        grid=(1,),
        in_specs=[SCALAR] + [whole(v.shape) for v in args] + [UNREAD],
        out_specs=[whole(v.shape) for v in shapes]
        + [pl.BlockSpec(tail.shape, lambda i: (0, final, 0))],
        out_shape=shapes + [jax.ShapeDtypeStruct(grads.shape, grads.dtype)],
        input_output_aliases={5: 3},
    )(z, *args, grads)


def ctx_permute(value, target):
    nx, nz, nc = (lax.axis_size(a) for a in CTX)
    pairs = []
    for x in range(nx):
        for z in range(nz):
            for c in range(nc):
                to = target(x, z, c)
                pairs.append(((x * nz + z) * nc + c, (to[0] * nz + to[1]) * nc + to[2]))
    return lax.ppermute(value, CTX, pairs)


def ctx_shift(value, steps):
    count = math.prod(lax.axis_size(a) for a in CTX)
    return lax.ppermute(
        value, CTX, [(i, i + steps) for i in range(count) if 0 <= i + steps < count]
    )


def body(featured, feat_taps, inner_taps, out_weight, out_grad):
    rows = featured.shape[0]
    nx, nz, nc = (lax.axis_size(a) for a in CTX)
    inv_root = 1.0 / math.sqrt(rows * nx * nz * nc)
    col, core, z = (
        jnp.full((1,), lax.axis_index(a), jnp.int32) for a in ("col", "core", "zl")
    )

    grads = lax.all_gather(out_grad, ("row", "core"), axis=0)

    own = jnp.transpose(featured, (1, 0, 2))
    before = ctx_shift(own[:, rows - HALO :], 1)
    gated = forward(before, own, feat_taps, inner_taps)
    both = lax.all_gather(gated, "col", axis=1, tiled=True)
    channels = both.shape[1]
    split = both.T.reshape(nx * nz, nc, channels // (nx * nz * nc), rows)
    kept, sent = (
        lax.dynamic_index_in_dim(split, c, 1, keepdims=False).reshape(channels // nc, rows)
        for c in (core[0], 1 - core[0])
    )
    arrived = ctx_permute(sent, lambda x, z, c: (x, z, 1 - c))

    far, near, pair, done = products(nx, col, core, kept, arrived, grads, out_weight)
    summed = lax.psum_scatter(pair, "x", scatter_dimension=0)
    far = lax.all_gather(far, "col", axis=0)

    grad_own, head, tail, taps = backward(
        nx * nc, col, near, far, before, own, feat_taps, inner_taps, done
    )
    taps = lax.all_to_all(taps, ("x", "core"), split_axis=0, concat_axis=0)

    pieces, taps, head = middle(nz, summed, taps, head)
    pieces = lax.all_to_all(pieces, "zl", split_axis=0, concat_axis=0)
    head = ctx_shift(head, -1)
    grad_weight, grad_feat_taps, grad_inner_taps, grad_own = last(
        inv_root, z, taps, pieces, tail, head, grad_own
    )
    return jnp.transpose(grad_own, (1, 0, 2)), grad_weight, grad_feat_taps, grad_inner_taps


def fine_mesh(mesh):
    row, col, ctx = mesh.devices.shape
    return Mesh(mesh.devices.reshape(row, col, ctx // 8, 4, 2), ("row", "col", *CTX))


def solution(mesh):
    return jax.shard_map(
        body,
        mesh=fine_mesh(mesh),
        in_specs=(
            P(CTX, None, ("row", "col")),
            P(None, None, ("row", "col")),
            P(None, ("row", "col")),
            P("row", "col"),
            P(CTX, ("col", "row")),
        ),
        out_specs=(
            P(CTX, None, ("row", "col")),
            P(("row", *CTX), "col"),
            P(None, None, ("row", "col")),
            P(None, ("row", "col")),
        ),
        check_vma=False,
    )
```

```python
import math

import jax
import jax.numpy as jnp
from jax import lax
from jax.experimental import pallas as pl
from jax.experimental.pallas import tpu as pltpu
from jax.sharding import Mesh
from jax.sharding import PartitionSpec as P

TAPS = 7
HALO = 16
LEAD = 8
CHUNK = 64
LANES = 128
CTX = ("x", "zl", "core")
F32 = jnp.float32
BF16 = jnp.bfloat16
VMEM_BYTES = 24 << 20


def spread(total):
    return [(start, min(CHUNK, total - start)) for start in range(0, total, CHUNK)]


def lane_spec(*lead):
    return pl.BlockSpec((*lead, LANES), lambda i: (0,) * len(lead) + (i,))


def whole(shape):
    return pl.BlockSpec(shape, lambda *_: (0,) * len(shape))


SCALAR = pl.BlockSpec(memory_space=pltpu.SMEM)
UNREAD = pl.BlockSpec(memory_space=pl.ANY)
IN_HBM = pl.BlockSpec(memory_space=pltpu.HBM)
IN_VMEM = pl.BlockSpec(memory_space=pltpu.VMEM)


def in_hbm(value):
    return pltpu.with_memory_space_constraint(value, pltpu.HBM)


def call(kernel, name, flops, moved, **kwargs):
    return pl.pallas_call(
        kernel,
        name=name,
        compiler_params=pltpu.CompilerParams(vmem_limit_bytes=VMEM_BYTES),
        cost_estimate=pl.CostEstimate(flops=flops, bytes_accessed=moved, transcendentals=0),
        **kwargs,
    )


def load_features(before, own, feats):
    rows = own.shape[1]
    for j in range(3):
        feats[j, 0:HALO, :] = before[j].astype(F32)
        for start, count in spread(rows):
            feats[j, HALO + start : HALO + start + count, :] = own[
                j, start : start + count, :
            ].astype(F32)


def mixed_parts(feats, feat_taps, start, count):
    base = HALO - LEAD + start
    parts = []
    for j in range(3):
        total = feat_taps[j, 0:1, :] * feats[j, base : base + count, :]
        for s in range(1, TAPS):
            total = total + feat_taps[j, s : s + 1, :] * feats[j, base - s : base - s + count, :]
        parts.append(total)
    return parts


def window_rows(product, inner_taps, start, count):
    base = LEAD + start
    total = inner_taps[0:1, :] * product[base : base + count, :]
    for s in range(1, TAPS):
        total = total + inner_taps[s : s + 1, :] * product[base - s : base - s + count, :]
    return total


def forward_kernel(before, own, feat_taps, inner_taps, gated, feats, query, product):
    rows = own.shape[1]
    load_features(before, own, feats)
    for start, count in spread(rows + LEAD):
        parts = mixed_parts(feats, feat_taps, start, count)
        query[start : start + count, :] = parts[0]
        product[start : start + count, :] = parts[1] * parts[2]
    for start, count in spread(rows):
        base = LEAD + start
        gated[start : start + count, :] = (
            query[base : base + count, :] * window_rows(product, inner_taps, start, count)
        ).astype(BF16)


def forward(before, own, feat_taps, inner_taps):
    _, rows, channels = own.shape
    return call(
        forward_kernel,
        "forward",
        60 * rows * channels,
        8 * rows * channels,
        grid=(channels // LANES,),
        in_specs=[
            lane_spec(3, HALO), lane_spec(3, rows), lane_spec(3, TAPS), lane_spec(TAPS)
        ],
        out_specs=lane_spec(rows),
        out_shape=jax.ShapeDtypeStruct((rows, channels), BF16),
        scratch_shapes=[
            pltpu.VMEM((3, rows + HALO, LANES), F32),
            pltpu.VMEM((rows + LEAD, LANES), F32),
            pltpu.VMEM((rows + LEAD, LANES), F32),
        ],
    )(before, own, feat_taps, inner_taps)


def backward_kernel(
    col, near, far, before, own, feat_taps, inner_taps, _,
    grads, head, tail, tap_sums, held, sems, *scratch,
):
    copies = []
    for at in range(near.shape[1] // LANES):
        lanes = slice(at * LANES, (at + 1) * LANES)
        backward_lanes(
            col, near.at[:, lanes], far.at[:, :, lanes], before.at[:, :, lanes],
            own.at[:, :, lanes], feat_taps.at[:, :, lanes], inner_taps.at[:, lanes],
            held.at[at], head.at[:, :, lanes], tail.at[:, :, lanes], tap_sums.at[:, :, :, lanes],
            *scratch,
        )
        copies.append(
            pltpu.make_async_copy(held.at[at], grads.at[:, :, lanes], sems.at[at])
        )
        copies[-1].start()
    for copy in copies:
        copy.wait()


def backward_lanes(
    col, near, far, before, own, feat_taps, inner_taps,
    grads, head, tail, tap_sums, feats, query, key, value, product, grad_window, grad_mixed,
):
    rows = own.shape[1]
    load_features(before, own, feats)
    for start, count in spread(rows + LEAD):
        parts = mixed_parts(feats, feat_taps, start, count)
        query[start : start + count, :] = parts[0]
        key[start : start + count, :] = parts[1]
        value[start : start + count, :] = parts[2]
        product[start : start + count, :] = parts[1] * parts[2]
    zeros = jnp.zeros((HALO, LANES), F32)
    grad_window[0:HALO, :] = zeros
    grad_window[HALO + rows :, :] = zeros[:LEAD]
    for j in range(3):
        grad_mixed[j, 0:HALO, :] = zeros
        grad_mixed[j, HALO + rows :, :] = zeros[:LEAD]
    for start, count in spread(rows):
        at = HALO + start
        total = near[start : start + count, :] + far[
            1 - col[0], start : start + count, :
        ].astype(F32)
        grad_window[at : at + count, :] = total * query[LEAD + start : LEAD + start + count, :]
        grad_mixed[0, at : at + count, :] = total * window_rows(product, inner_taps, start, count)
    for start, count in spread(rows + LEAD):
        at = HALO - LEAD + start
        total = inner_taps[0:1, :] * grad_window[at : at + count, :]
        for s in range(1, TAPS):
            total = total + inner_taps[s : s + 1, :] * grad_window[at + s : at + s + count, :]
        grad_mixed[1, at : at + count, :] = total * value[start : start + count, :]
        grad_mixed[2, at : at + count, :] = total * key[start : start + count, :]

    def folded(terms):
        return jnp.sum(terms.reshape(terms.shape[0] // 8, 8, LANES), axis=0)

    tiles = [None] * 4

    def put(place, sums):
        rows = [jnp.sum(total, axis=0, keepdims=True) for total in sums]
        tiles[place] = jnp.concatenate([*rows, jnp.zeros((1, LANES), F32)], axis=0)

    def transposed(j, at, count):
        total = feat_taps[j, 0:1, :] * grad_mixed[j, at : at + count, :]
        for s in range(1, TAPS):
            total = total + feat_taps[j, s : s + 1, :] * grad_mixed[j, at + s : at + s + count, :]
        return total

    for j in range(3):
        head[j] = transposed(j, 0, HALO)
        sums = [jnp.zeros((8, LANES), F32) for _ in range(TAPS)]
        spans = [(HALO + start, count) for start, count in spread(rows)]
        for at, count in ([(HALO - LEAD, LEAD)] if j > 0 else []) + spans:
            here = grad_mixed[j, at : at + count, :]
            for s in range(TAPS):
                sums[s] = sums[s] + folded(here * feats[j, at - s : at - s + count, :])
            if at >= HALO:
                total = transposed(j, at, count)
                grads[j, at - HALO : at - HALO + count, :] = total.astype(BF16)
                if at + count == HALO + rows:
                    tail[j] = total[count - HALO :]
        put(j, sums)
    sums = [jnp.zeros((8, LANES), F32) for _ in range(TAPS)]
    for start, count in spread(rows):
        here = grad_window[HALO + start : HALO + start + count, :]
        for s in range(TAPS):
            base = LEAD + start - s
            sums[s] = sums[s] + folded(here * product[base : base + count, :])
    put(3, sums)
    for at in range(2):
        pair = jnp.concatenate([tiles[at], tiles[2 + at]], axis=0).astype(BF16)
        for copy in range(tap_sums.shape[0]):
            tap_sums[copy, at] = pair


def backward(copies, col, near, far, before, own, feat_taps, inner_taps, after):
    _, rows, channels = own.shape
    edge = jax.ShapeDtypeStruct((3, HALO, channels), F32)
    return call(
        backward_kernel,
        "backward",
        160 * rows * channels,
        20 * rows * channels,
        in_specs=[SCALAR] + [IN_VMEM] * 6 + [UNREAD],
        out_specs=[IN_HBM] + [IN_VMEM] * 3,
        out_shape=[
            pltpu.HBM((3, rows, channels), BF16),
            edge,
            edge,
            jax.ShapeDtypeStruct((copies, 2, 16, channels), BF16),
        ],
        scratch_shapes=[
            pltpu.VMEM((channels // LANES, 3, rows, LANES), BF16),
            pltpu.SemaphoreType.DMA((channels // LANES,)),
            pltpu.VMEM((3, rows + HALO, LANES), F32),
        ]
        + [pltpu.VMEM((rows + LEAD, LANES), F32)] * 4
        + [
            pltpu.VMEM((rows + HALO + LEAD, LANES), F32),
            pltpu.VMEM((3, rows + HALO + LEAD, LANES), F32),
        ],
    )(col, near, far, before, own, feat_taps, inner_taps, after)


TOKEN = jax.ShapeDtypeStruct((8, LANES), F32)


def products_kernel(
    col, core, own, other, grads, weight, far, near, out, done, held, held_weight, sems, weight_sems
):
    half = near.shape[1]
    pieces = weight_sems.shape[1]
    size = half // pieces
    fetches = [
        [
            pltpu.make_async_copy(
                weight.at[pl.ds(pl.multiple_of(which * half + piece * size, size), size), :],
                held_weight.at[at, piece * size : (piece + 1) * size],
                weight_sems.at[at, piece],
            )
            for piece in range(pieces)
        ]
        for at, which in enumerate((1 - col[0], col[0]))
    ]
    for copy in fetches[0] + fetches[1]:
        copy.start()
    done[...] = jnp.zeros_like(done)
    blocks, parts, size, _ = held.shape
    mine = [2 * b + core[0] for b in range(blocks)]
    copies = []
    gated = jnp.concatenate([own[...], other[...]], axis=1)
    for b in range(blocks):
        pair = jnp.concatenate([grads[mine[b]], grads[4 * b + 1 - mine[b]]], axis=0)
        total = jnp.dot(gated, pair, preferred_element_type=F32)
        for part in range(parts):
            held[b, part] = total[part * size : (part + 1) * size].astype(BF16)
        copies.append(pltpu.make_async_copy(held.at[b], out.at[:, b], sems.at[b]))
        copies[-1].start()
    wide = jnp.concatenate([grads[at] for at in mine], axis=1)
    for at, result in enumerate((far, near)):
        for copy in fetches[at]:
            copy.wait()
        total = lax.dot_general(
            wide, held_weight[at], (((1,), (1,)), ((), ())), preferred_element_type=F32
        )
        result[...] = total.astype(result.dtype)
    for copy in copies:
        copy.wait()


def products(parts, col, core, own, other, grads, weight):
    channels, rows = own.shape
    blocks, _, width = grads.shape
    blocks = blocks // 2
    half = weight.shape[0] // 2
    size = channels // parts
    return call(
        products_kernel,
        "products",
        4 * rows * (channels + half) * blocks * width,
        4 * blocks * width * (rows + channels) + 4 * rows * channels,
        in_specs=[SCALAR] * 2 + [IN_VMEM] * 3 + [IN_HBM],
        out_specs=[IN_VMEM, IN_VMEM, IN_HBM, IN_VMEM],
        out_shape=[
            jax.ShapeDtypeStruct((rows, half), BF16),
            jax.ShapeDtypeStruct((rows, half), F32),
            pltpu.HBM((parts, blocks, size, width), BF16),
            TOKEN,
        ],
        scratch_shapes=[
            pltpu.VMEM((blocks, parts, size, width), BF16),
            pltpu.VMEM((2, half, blocks * width), BF16),
            pltpu.SemaphoreType.DMA((blocks,)),
            pltpu.SemaphoreType.DMA((2, 4)),
        ],
    )(col, core, own, other, grads, in_hbm(weight))


def paired(sums):
    return jnp.concatenate([sums[:2], sums[2:]], axis=1).astype(BF16)


def parted(tiles):
    tiles = tiles.astype(F32)
    return jnp.concatenate([tiles[:, :8], tiles[:, 8:]], axis=0)


def middle_kernel(pair, taps, head, out, out_taps, out_head):
    parts, _, size, _ = out.shape
    blocks = pair.shape[0]
    sums = parted(taps[0])
    for copy in range(1, taps.shape[0]):
        sums = sums + parted(taps[copy])
    out_taps[...] = sums
    out_head[...] = head[...].astype(BF16)
    both = paired(sums)
    for part in range(parts):
        out[part, 0:blocks] = pair[:, part * size : (part + 1) * size, :]
        out[part, blocks:] = both


def middle(parts, pair, taps, head):
    blocks, channels, width = pair.shape
    shape = (parts, blocks + taps.shape[1], channels // parts, width)
    outs = [
        jax.ShapeDtypeStruct(shape, BF16),
        jax.ShapeDtypeStruct((2 * taps.shape[1], 8, width), F32),
        jax.ShapeDtypeStruct(head.shape, BF16),
    ]
    return call(
        middle_kernel,
        "middle",
        4 * pair.size,
        4 * pair.size,
        in_specs=[IN_VMEM] * 3,
        out_specs=[IN_VMEM] * 3,
        out_shape=outs,
    )(pair, taps, head)


def last_kernel(
    scale, z, taps, arrived, tail, head, _, out, out_feat, out_inner, out_grads
):
    parts, _, _, width = arrived.shape
    blocks = out.shape[1] // width
    out_grads[...] = (tail[...] + head[...].astype(F32)).astype(BF16)
    for b in range(blocks):
        total = arrived[0, b].astype(F32)
        for part in range(1, parts):
            total = total + arrived[part, b].astype(F32)
        out[:, b * width : (b + 1) * width] = (total * scale).astype(BF16)
    total = taps[...]
    for part in range(parts):
        total = total + jnp.where(z[0] == part, 0.0, parted(arrived[part, blocks:]))
    total = total * scale
    out_feat[...] = total[:3, :TAPS]
    out_inner[...] = total[3, :TAPS]


def last(scale, z, taps, arrived, tail, head, grads):
    parts, count, channels, width = arrived.shape
    blocks = count - taps.shape[0] // 2
    final = grads.shape[1] // HALO - 1
    args = (taps, arrived, tail, head)
    shapes = [
        jax.ShapeDtypeStruct((channels, blocks * width), BF16),
        jax.ShapeDtypeStruct((3, TAPS, width), F32),
        jax.ShapeDtypeStruct((TAPS, width), F32),
    ]
    return call(
        lambda *refs: last_kernel(scale, *refs),
        "last",
        2 * arrived.size,
        2 * arrived.size,
        grid=(1,),
        in_specs=[SCALAR] + [whole(v.shape) for v in args] + [UNREAD],
        out_specs=[whole(v.shape) for v in shapes]
        + [pl.BlockSpec(tail.shape, lambda i: (0, final, 0))],
        out_shape=shapes + [jax.ShapeDtypeStruct(grads.shape, grads.dtype)],
        input_output_aliases={5: 3},
    )(z, *args, grads)


def ctx_permute(value, target):
    nx, nz, nc = (lax.axis_size(a) for a in CTX)
    pairs = []
    for x in range(nx):
        for z in range(nz):
            for c in range(nc):
                to = target(x, z, c)
                pairs.append(((x * nz + z) * nc + c, (to[0] * nz + to[1]) * nc + to[2]))
    return lax.ppermute(value, CTX, pairs)


def ctx_shift(value, steps):
    count = math.prod(lax.axis_size(a) for a in CTX)
    return lax.ppermute(
        value, CTX, [(i, i + steps) for i in range(count) if 0 <= i + steps < count]
    )


def body(featured, feat_taps, inner_taps, out_weight, out_grad):
    rows = featured.shape[0]
    nx, nz, nc = (lax.axis_size(a) for a in CTX)
    inv_root = 1.0 / math.sqrt(rows * nx * nz * nc)
    col, core, z = (
        jnp.full((1,), lax.axis_index(a), jnp.int32) for a in ("col", "core", "zl")
    )

    grads = lax.all_gather(out_grad, ("row", "core"), axis=0)

    own = jnp.transpose(featured, (1, 0, 2))
    before = ctx_shift(own[:, rows - HALO :], 1)
    gated = forward(before, own, feat_taps, inner_taps)
    both = lax.all_gather(gated, "col", axis=1, tiled=True)
    channels = both.shape[1]
    split = both.T.reshape(nx * nz, nc, channels // (nx * nz * nc), rows)
    kept, sent = (
        lax.dynamic_index_in_dim(split, c, 1, keepdims=False).reshape(channels // nc, rows)
        for c in (core[0], 1 - core[0])
    )
    arrived = ctx_permute(sent, lambda x, z, c: (x, z, 1 - c))

    far, near, pair, done = products(nx, col, core, kept, arrived, grads, out_weight)
    summed = lax.psum_scatter(pair, "x", scatter_dimension=0)
    far = lax.all_gather(far, "col", axis=0)

    grad_own, head, tail, taps = backward(
        nx * nc, col, near, far, before, own, feat_taps, inner_taps, done
    )
    taps = lax.all_to_all(taps, ("x", "core"), split_axis=0, concat_axis=0)

    pieces, taps, head = middle(nz, summed, taps, head)
    pieces = lax.all_to_all(pieces, "zl", split_axis=0, concat_axis=0)
    head = ctx_shift(head, -1)
    grad_weight, grad_feat_taps, grad_inner_taps, grad_own = last(
        inv_root, z, taps, pieces, tail, head, grad_own
    )
    return jnp.transpose(grad_own, (1, 0, 2)), grad_weight, grad_feat_taps, grad_inner_taps


def fine_mesh(mesh):
    row, col, ctx = mesh.devices.shape
    return Mesh(mesh.devices.reshape(row, col, ctx // 8, 4, 2), ("row", "col", *CTX))


def solution(mesh):
    return jax.shard_map(
        body,
        mesh=fine_mesh(mesh),
        in_specs=(
            P(CTX, None, ("row", "col")),
            P(None, None, ("row", "col")),
            P(None, ("row", "col")),
            P("row", "col"),
            P(CTX, ("col", "row")),
        ),
        out_specs=(
            P(CTX, None, ("row", "col")),
            P(("row", *CTX), "col"),
            P(None, None, ("row", "col")),
            P(None, ("row", "col")),
        ),
        check_vma=False,
    )
```

```python
import math

import jax
import jax.numpy as jnp
from jax import lax
from jax.experimental import pallas as pl
from jax.experimental.pallas import tpu as pltpu
from jax.sharding import Mesh
from jax.sharding import PartitionSpec as P

TAPS = 7
HALO = 16
LEAD = 8
CHUNK = 64
LANES = 128
CTX = ("x", "zl", "core")
F32 = jnp.float32
BF16 = jnp.bfloat16
VMEM_BYTES = 24 << 20


def spread(total):
    return [(start, min(CHUNK, total - start)) for start in range(0, total, CHUNK)]


def lane_spec(*lead):
    return pl.BlockSpec((*lead, LANES), lambda i: (0,) * len(lead) + (i,))


def whole(shape):
    return pl.BlockSpec(shape, lambda *_: (0,) * len(shape))


SCALAR = pl.BlockSpec(memory_space=pltpu.SMEM)
UNREAD = pl.BlockSpec(memory_space=pl.ANY)
IN_HBM = pl.BlockSpec(memory_space=pltpu.HBM)
IN_VMEM = pl.BlockSpec(memory_space=pltpu.VMEM)


def in_hbm(value):
    return pltpu.with_memory_space_constraint(value, pltpu.HBM)


def call(kernel, name, flops, moved, **kwargs):
    return pl.pallas_call(
        kernel,
        name=name,
        compiler_params=pltpu.CompilerParams(vmem_limit_bytes=VMEM_BYTES),
        cost_estimate=pl.CostEstimate(flops=flops, bytes_accessed=moved, transcendentals=0),
        **kwargs,
    )


def load_features(before, own, feats):
    rows = own.shape[1]
    for j in range(3):
        feats[j, 0:HALO, :] = before[j].astype(F32)
        for start, count in spread(rows):
            feats[j, HALO + start : HALO + start + count, :] = own[
                j, start : start + count, :
            ].astype(F32)


def mixed_parts(feats, feat_taps, start, count):
    base = HALO - LEAD + start
    parts = []
    for j in range(3):
        total = feat_taps[j, 0:1, :] * feats[j, base : base + count, :]
        for s in range(1, TAPS):
            total = total + feat_taps[j, s : s + 1, :] * feats[j, base - s : base - s + count, :]
        parts.append(total)
    return parts


def window_rows(product, inner_taps, start, count):
    base = LEAD + start
    total = inner_taps[0:1, :] * product[base : base + count, :]
    for s in range(1, TAPS):
        total = total + inner_taps[s : s + 1, :] * product[base - s : base - s + count, :]
    return total


def forward_kernel(before, own, feat_taps, inner_taps, gated, feats, query, product):
    rows = own.shape[1]
    load_features(before, own, feats)
    for start, count in spread(rows + LEAD):
        parts = mixed_parts(feats, feat_taps, start, count)
        query[start : start + count, :] = parts[0]
        product[start : start + count, :] = parts[1] * parts[2]
    for start, count in spread(rows):
        base = LEAD + start
        gated[start : start + count, :] = (
            query[base : base + count, :] * window_rows(product, inner_taps, start, count)
        ).astype(BF16)


def forward(before, own, feat_taps, inner_taps):
    _, rows, channels = own.shape
    return call(
        forward_kernel,
        "forward",
        60 * rows * channels,
        8 * rows * channels,
        grid=(channels // LANES,),
        in_specs=[
            lane_spec(3, HALO), lane_spec(3, rows), lane_spec(3, TAPS), lane_spec(TAPS)
        ],
        out_specs=lane_spec(rows),
        out_shape=jax.ShapeDtypeStruct((rows, channels), BF16),
        scratch_shapes=[
            pltpu.VMEM((3, rows + HALO, LANES), F32),
            pltpu.VMEM((rows + LEAD, LANES), F32),
            pltpu.VMEM((rows + LEAD, LANES), F32),
        ],
    )(before, own, feat_taps, inner_taps)


def backward_kernel(
    col, near, far, before, own, feat_taps, inner_taps, _,
    grads, head, tail, tap_sums, held, sems, *scratch,
):
    copies = []
    for at in range(near.shape[1] // LANES):
        lanes = slice(at * LANES, (at + 1) * LANES)
        backward_lanes(
            col, near.at[:, lanes], far.at[:, :, lanes], before.at[:, :, lanes],
            own.at[:, :, lanes], feat_taps.at[:, :, lanes], inner_taps.at[:, lanes],
            held.at[at], head.at[:, :, lanes], tail.at[:, :, lanes], tap_sums.at[:, :, :, lanes],
            *scratch,
        )
        copies.append(
            pltpu.make_async_copy(held.at[at], grads.at[:, :, lanes], sems.at[at])
        )
        copies[-1].start()
    for copy in copies:
        copy.wait()


def backward_lanes(
    col, near, far, before, own, feat_taps, inner_taps,
    grads, head, tail, tap_sums, feats, query, key, value, product, grad_window, grad_mixed,
):
    rows = own.shape[1]
    load_features(before, own, feats)
    for start, count in spread(rows + LEAD):
        parts = mixed_parts(feats, feat_taps, start, count)
        query[start : start + count, :] = parts[0]
        key[start : start + count, :] = parts[1]
        value[start : start + count, :] = parts[2]
        product[start : start + count, :] = parts[1] * parts[2]
    zeros = jnp.zeros((HALO, LANES), F32)
    grad_window[0:HALO, :] = zeros
    grad_window[HALO + rows :, :] = zeros[:LEAD]
    for j in range(3):
        grad_mixed[j, 0:HALO, :] = zeros
        grad_mixed[j, HALO + rows :, :] = zeros[:LEAD]
    for start, count in spread(rows):
        at = HALO + start
        total = near[start : start + count, :] + far[
            1 - col[0], start : start + count, :
        ].astype(F32)
        grad_window[at : at + count, :] = total * query[LEAD + start : LEAD + start + count, :]
        grad_mixed[0, at : at + count, :] = total * window_rows(product, inner_taps, start, count)
    for start, count in spread(rows + LEAD):
        at = HALO - LEAD + start
        total = inner_taps[0:1, :] * grad_window[at : at + count, :]
        for s in range(1, TAPS):
            total = total + inner_taps[s : s + 1, :] * grad_window[at + s : at + s + count, :]
        grad_mixed[1, at : at + count, :] = total * value[start : start + count, :]
        grad_mixed[2, at : at + count, :] = total * key[start : start + count, :]

    def folded(terms):
        return jnp.sum(terms.reshape(terms.shape[0] // 8, 8, LANES), axis=0)

    tiles = [None] * 4

    def put(place, sums):
        rows = [jnp.sum(total, axis=0, keepdims=True) for total in sums]
        tiles[place] = jnp.concatenate([*rows, jnp.zeros((1, LANES), F32)], axis=0)

    def transposed(j, at, count):
        total = feat_taps[j, 0:1, :] * grad_mixed[j, at : at + count, :]
        for s in range(1, TAPS):
            total = total + feat_taps[j, s : s + 1, :] * grad_mixed[j, at + s : at + s + count, :]
        return total

    for j in range(3):
        head[j] = transposed(j, 0, HALO)
        sums = [jnp.zeros((8, LANES), F32) for _ in range(TAPS)]
        spans = [(HALO + start, count) for start, count in spread(rows)]
        for at, count in ([(HALO - LEAD, LEAD)] if j > 0 else []) + spans:
            here = grad_mixed[j, at : at + count, :]
            for s in range(TAPS):
                sums[s] = sums[s] + folded(here * feats[j, at - s : at - s + count, :])
            if at >= HALO:
                total = transposed(j, at, count)
                grads[j, at - HALO : at - HALO + count, :] = total.astype(BF16)
                if at + count == HALO + rows:
                    tail[j] = total[count - HALO :]
        put(j, sums)
    sums = [jnp.zeros((8, LANES), F32) for _ in range(TAPS)]
    for start, count in spread(rows):
        here = grad_window[HALO + start : HALO + start + count, :]
        for s in range(TAPS):
            base = LEAD + start - s
            sums[s] = sums[s] + folded(here * product[base : base + count, :])
    put(3, sums)
    for at in range(2):
        pair = jnp.concatenate([tiles[at], tiles[2 + at]], axis=0).astype(BF16)
        for copy in range(tap_sums.shape[0]):
            tap_sums[copy, at] = pair


def backward(copies, col, near, far, before, own, feat_taps, inner_taps, after):
    _, rows, channels = own.shape
    edge = jax.ShapeDtypeStruct((3, HALO, channels), F32)
    return call(
        backward_kernel,
        "backward",
        160 * rows * channels,
        20 * rows * channels,
        in_specs=[SCALAR] + [IN_VMEM] * 6 + [UNREAD],
        out_specs=[IN_HBM] + [IN_VMEM] * 3,
        out_shape=[
            pltpu.HBM((3, rows, channels), BF16),
            edge,
            edge,
            jax.ShapeDtypeStruct((copies, 2, 16, channels), BF16),
        ],
        scratch_shapes=[
            pltpu.VMEM((channels // LANES, 3, rows, LANES), BF16),
            pltpu.SemaphoreType.DMA((channels // LANES,)),
            pltpu.VMEM((3, rows + HALO, LANES), F32),
        ]
        + [pltpu.VMEM((rows + LEAD, LANES), F32)] * 4
        + [
            pltpu.VMEM((rows + HALO + LEAD, LANES), F32),
            pltpu.VMEM((3, rows + HALO + LEAD, LANES), F32),
        ],
    )(col, near, far, before, own, feat_taps, inner_taps, after)


TOKEN = jax.ShapeDtypeStruct((8, LANES), F32)


def products_kernel(
    col, core, own, other, grads, weight, far, near, out, done, held, held_weight, sems, weight_sems
):
    half = near.shape[1]
    pieces = weight_sems.shape[1]
    size = half // pieces
    fetches = [
        [
            pltpu.make_async_copy(
                weight.at[pl.ds(pl.multiple_of(which * half + piece * size, size), size), :],
                held_weight.at[at, piece * size : (piece + 1) * size],
                weight_sems.at[at, piece],
            )
            for piece in range(pieces)
        ]
        for at, which in enumerate((1 - col[0], col[0]))
    ]
    for copy in fetches[0] + fetches[1]:
        copy.start()
    done[...] = jnp.zeros_like(done)
    blocks, parts, size, _ = held.shape
    mine = [2 * b + core[0] for b in range(blocks)]
    copies = []
    gated = jnp.concatenate([own[...], other[...]], axis=1)
    for b in range(blocks):
        pair = jnp.concatenate([grads[mine[b]], grads[4 * b + 1 - mine[b]]], axis=0)
        total = jnp.dot(gated, pair, preferred_element_type=F32)
        for part in range(parts):
            held[b, part] = total[part * size : (part + 1) * size].astype(BF16)
        copies.append(pltpu.make_async_copy(held.at[b], out.at[:, b], sems.at[b]))
        copies[-1].start()
    wide = jnp.concatenate([grads[at] for at in mine], axis=1)
    for at, result in enumerate((far, near)):
        for copy in fetches[at]:
            copy.wait()
        total = lax.dot_general(
            wide, held_weight[at], (((1,), (1,)), ((), ())), preferred_element_type=F32
        )
        result[...] = total.astype(result.dtype)
    for copy in copies:
        copy.wait()


def products(parts, col, core, own, other, grads, weight):
    channels, rows = own.shape
    blocks, _, width = grads.shape
    blocks = blocks // 2
    half = weight.shape[0] // 2
    size = channels // parts
    return call(
        products_kernel,
        "products",
        4 * rows * (channels + half) * blocks * width,
        4 * blocks * width * (rows + channels) + 4 * rows * channels,
        in_specs=[SCALAR] * 2 + [IN_VMEM] * 3 + [IN_HBM],
        out_specs=[IN_VMEM, IN_VMEM, IN_HBM, IN_VMEM],
        out_shape=[
            jax.ShapeDtypeStruct((rows, half), BF16),
            jax.ShapeDtypeStruct((rows, half), F32),
            pltpu.HBM((parts, blocks, size, width), BF16),
            TOKEN,
        ],
        scratch_shapes=[
            pltpu.VMEM((blocks, parts, size, width), BF16),
            pltpu.VMEM((2, half, blocks * width), BF16),
            pltpu.SemaphoreType.DMA((blocks,)),
            pltpu.SemaphoreType.DMA((2, 4)),
        ],
    )(col, core, own, other, grads, in_hbm(weight))


def paired(sums):
    return jnp.concatenate([sums[:2], sums[2:]], axis=1).astype(BF16)


def parted(tiles):
    tiles = tiles.astype(F32)
    return jnp.concatenate([tiles[:, :8], tiles[:, 8:]], axis=0)


def middle_kernel(pair, taps, head, out, out_taps, out_head, held, sem):
    parts, _, size, _ = out.shape
    blocks = pair.shape[0]
    copy_in = pltpu.make_async_copy(pair, held, sem)
    copy_in.start()
    sums = parted(taps[0])
    for copy in range(1, taps.shape[0]):
        sums = sums + parted(taps[copy])
    out_taps[...] = sums
    out_head[...] = head[...].astype(BF16)
    both = paired(sums)
    for part in range(parts):
        out[part, blocks:] = both
    copy_in.wait()
    for part in range(parts):
        out[part, 0:blocks] = held[:, part * size : (part + 1) * size, :]


def middle(parts, pair, taps, head):
    blocks, channels, width = pair.shape
    shape = (parts, blocks + taps.shape[1], channels // parts, width)
    outs = [
        jax.ShapeDtypeStruct(shape, BF16),
        jax.ShapeDtypeStruct((2 * taps.shape[1], 8, width), F32),
        jax.ShapeDtypeStruct(head.shape, BF16),
    ]
    return call(
        middle_kernel,
        "middle",
        4 * pair.size,
        4 * pair.size,
        in_specs=[IN_HBM, IN_VMEM, IN_VMEM],
        out_specs=[IN_VMEM] * 3,
        out_shape=outs,
        scratch_shapes=[pltpu.VMEM(pair.shape, pair.dtype), pltpu.SemaphoreType.DMA],
    )(in_hbm(pair), taps, head)


def last_kernel(
    scale, z, taps, arrived, tail, head, _, out, out_feat, out_inner, out_grads
):
    parts, _, _, width = arrived.shape
    blocks = out.shape[1] // width
    out_grads[...] = (tail[...] + head[...].astype(F32)).astype(BF16)
    for b in range(blocks):
        total = arrived[0, b].astype(F32)
        for part in range(1, parts):
            total = total + arrived[part, b].astype(F32)
        out[:, b * width : (b + 1) * width] = (total * scale).astype(BF16)
    total = taps[...]
    for part in range(parts):
        total = total + jnp.where(z[0] == part, 0.0, parted(arrived[part, blocks:]))
    total = total * scale
    out_feat[...] = total[:3, :TAPS]
    out_inner[...] = total[3, :TAPS]


def last(scale, z, taps, arrived, tail, head, grads):
    parts, count, channels, width = arrived.shape
    blocks = count - taps.shape[0] // 2
    final = grads.shape[1] // HALO - 1
    args = (taps, arrived, tail, head)
    shapes = [
        jax.ShapeDtypeStruct((channels, blocks * width), BF16),
        jax.ShapeDtypeStruct((3, TAPS, width), F32),
        jax.ShapeDtypeStruct((TAPS, width), F32),
    ]
    return call(
        lambda *refs: last_kernel(scale, *refs),
        "last",
        2 * arrived.size,
        2 * arrived.size,
        grid=(1,),
        in_specs=[SCALAR] + [whole(v.shape) for v in args] + [UNREAD],
        out_specs=[whole(v.shape) for v in shapes]
        + [pl.BlockSpec(tail.shape, lambda i: (0, final, 0))],
        out_shape=shapes + [jax.ShapeDtypeStruct(grads.shape, grads.dtype)],
        input_output_aliases={5: 3},
    )(z, *args, grads)


def ctx_permute(value, target):
    nx, nz, nc = (lax.axis_size(a) for a in CTX)
    pairs = []
    for x in range(nx):
        for z in range(nz):
            for c in range(nc):
                to = target(x, z, c)
                pairs.append(((x * nz + z) * nc + c, (to[0] * nz + to[1]) * nc + to[2]))
    return lax.ppermute(value, CTX, pairs)


def ctx_shift(value, steps):
    count = math.prod(lax.axis_size(a) for a in CTX)
    return lax.ppermute(
        value, CTX, [(i, i + steps) for i in range(count) if 0 <= i + steps < count]
    )


def body(featured, feat_taps, inner_taps, out_weight, out_grad):
    rows = featured.shape[0]
    nx, nz, nc = (lax.axis_size(a) for a in CTX)
    inv_root = 1.0 / math.sqrt(rows * nx * nz * nc)
    col, core, z = (
        jnp.full((1,), lax.axis_index(a), jnp.int32) for a in ("col", "core", "zl")
    )

    grads = lax.all_gather(out_grad, ("row", "core"), axis=0)

    own = jnp.transpose(featured, (1, 0, 2))
    before = ctx_shift(own[:, rows - HALO :], 1)
    gated = forward(before, own, feat_taps, inner_taps)
    both = lax.all_gather(gated, "col", axis=1, tiled=True)
    channels = both.shape[1]
    split = both.T.reshape(nx * nz, nc, channels // (nx * nz * nc), rows)
    kept, sent = (
        lax.dynamic_index_in_dim(split, c, 1, keepdims=False).reshape(channels // nc, rows)
        for c in (core[0], 1 - core[0])
    )
    arrived = ctx_permute(sent, lambda x, z, c: (x, z, 1 - c))

    far, near, pair, done = products(nx, col, core, kept, arrived, grads, out_weight)
    summed = lax.psum_scatter(pair, "x", scatter_dimension=0)
    far = lax.all_gather(far, "col", axis=0)

    grad_own, head, tail, taps = backward(
        nx * nc, col, near, far, before, own, feat_taps, inner_taps, done
    )
    taps = lax.all_to_all(taps, ("x", "core"), split_axis=0, concat_axis=0)

    pieces, taps, head = middle(nz, summed, taps, head)
    pieces = lax.all_to_all(pieces, "zl", split_axis=0, concat_axis=0)
    head = ctx_shift(head, -1)
    grad_weight, grad_feat_taps, grad_inner_taps, grad_own = last(
        inv_root, z, taps, pieces, tail, head, grad_own
    )
    return jnp.transpose(grad_own, (1, 0, 2)), grad_weight, grad_feat_taps, grad_inner_taps


def fine_mesh(mesh):
    row, col, ctx = mesh.devices.shape
    return Mesh(mesh.devices.reshape(row, col, ctx // 8, 4, 2), ("row", "col", *CTX))


def solution(mesh):
    return jax.shard_map(
        body,
        mesh=fine_mesh(mesh),
        in_specs=(
            P(CTX, None, ("row", "col")),
            P(None, None, ("row", "col")),
            P(None, ("row", "col")),
            P("row", "col"),
            P(CTX, ("col", "row")),
        ),
        out_specs=(
            P(CTX, None, ("row", "col")),
            P(("row", *CTX), "col"),
            P(None, None, ("row", "col")),
            P(None, ("row", "col")),
        ),
        check_vma=False,
    )
```
